32 devices in a mesh: tile: 8 (over z, core), mem: 4 (over y, x).
Axes of the slice: x: 2, y: 2, z: 4, core: 2. Of those that a mesh axis runs over, the one named last changes fastest.
Arguments:
- right_side: float32 [8, 64, 16, 256], P('tile', 'mem'), may hold values from -6 to 6
- perturbations: bfloat16 [8, 64, 6, 16, 256], P('tile', 'mem'), may hold values from -0.75 to 0.75
- precision: float32 [8, 6, 16, 256], P('tile'), may hold values from 5 to 40
- covered: int32 [8, 2, 16], P('tile'), may hold values 0 or 1
Outputs:
- weights: float32 [8, 64, 16, 256], P('tile', 'mem')
- residual: float32 [8, 64, 16, 256], P('tile', 'mem')
The draws below stay inside these ranges and needn't reach their ends.
All inputs are finite; a program needn't handle non-finite values. No bound on the sum of `covered` on one device may be relied on, other than what follows from the above.
Results may differ from the reference program's by a relative error of at most 0.006.
Values sent between devices are 32-bit elements; how exact they have to be, the bound alone decides.
No kernel may reach another device: no remote copies, remote signals or barrier semaphores. Data moves between devices by JAX's collectives and lax.ppermute only.
A program may use at most 64 MiB of HBM per device.

```python
import math
import jax
import jax.numpy as jnp
from jax import lax

TY = 16
TX = 256
TCOLS = 8
VL = 6
MEMBERS = 64
TILES = 8
ITERS = 2


def set_ends(array, own_key, low, largest):
    spot = [jax.random.randint(jax.random.fold_in(own_key, axis), (), 0, length) for axis, length in enumerate(array.shape)]
    main_axis = array.shape.index(max(array.shape))
    neighbour = spot[:main_axis] + [(spot[main_axis] + 1) % array.shape[main_axis]] + spot[main_axis + 1:]
    return array.at[tuple(spot)].set(low).at[tuple(neighbour)].set(largest)


def steps_of(rng, shape, pieces, least, largest):
    def one(position, parts):
        draws = jax.random.uniform(jax.random.fold_in(jax.random.fold_in(rng, 6), position), (parts,), jnp.float32, least / len(pieces), largest / len(pieces))
        return jnp.repeat(jnp.exp(draws), shape[position] // parts).reshape((-1,) + (1,) * (len(shape) - position - 1))

    factor_of = one(*pieces[0])
    for cut in pieces[1:]:
        factor_of = factor_of * one(*cut)
    return factor_of


def scatter_about(key, dims, scale, reach, cuts=(), dtype=jnp.bfloat16):
    loudness = steps_of(key, dims, cuts, -0.22, 0.18) if cuts else 1.0
    values = jax.random.normal(key, dims, jnp.float32) * scale * loudness
    return jnp.minimum(jnp.maximum(values, -reach), reach).astype(dtype)


def setup_inputs(seed: int = 0) -> dict:
    streams_of = jax.random.split(jax.random.key(seed), 5)
    right_side = scatter_about(streams_of[0], (TILES, MEMBERS, TY, TX), 1.0, 6.0, ((0, 8), (1, 4)), jnp.float32)
    perturbations = scatter_about(streams_of[1], (TILES, MEMBERS, VL, TY, TX), MEMBERS ** -0.5, 0.75, ((0, 8), (1, 4)))
    precision = jnp.clip(jnp.exp(math.log(40.0) - 2.0794415 * jax.random.uniform(streams_of[2], (TILES, VL, TY, TX), jnp.float32) ** steps_of(streams_of[2], (TILES, VL, TY, TX), ((0, 8),), -0.2, 0.2)), 5.0, 40.0)
    covered = set_ends((jax.random.randint(streams_of[3], (TILES, TY // 8, TX // 16), 0, 4) < 3).astype(jnp.int32), jax.random.fold_in(streams_of[3], 1), 0, 1)
    return {"right_side": right_side, "perturbations": perturbations, "precision": precision, "covered": covered}


def filter_taps():
    offsets = jnp.arange(-8, 9).astype(jnp.float32)
    raw = jnp.exp(-offsets * offsets / 32.0)
    return raw / jnp.sqrt(jnp.sum(jnp.exp(-offsets * offsets / 16.0)))

def to_grid(field):
    rows = field.shape[0] // TCOLS
    return field.reshape(rows, TCOLS, TY, TX).transpose(0, 2, 1, 3).reshape(rows * TY, TCOLS * TX)

def to_tiles(grid):
    rows = grid.shape[0] // TY
    return grid.reshape(rows, TY, TCOLS, TX).transpose(0, 2, 1, 3).reshape(rows * TCOLS, TY, TX)

def smooth_grid(grid):
    taps = filter_taps()
    height, width = grid.shape
    padded = jnp.pad(grid, ((8, 8), (0, 0)))
    along = jnp.zeros_like(grid)
    for j in range(17):
        along = along + taps[j] * padded[j:j + height, :]
    tile_rows = height // TY
    strip = along.reshape(tile_rows, TY, width).transpose(1, 0, 2).reshape(TY, tile_rows * width)
    length = tile_rows * width
    padded = jnp.pad(strip, ((0, 0), (8, 8)), mode='wrap')
    result = jnp.zeros_like(strip)
    for j in range(17):
        result = result + taps[j] * padded[:, j:j + length]
    return result.reshape(TY, tile_rows, width).transpose(1, 0, 2).reshape(height, width)

def smooth_member(field):
    return to_tiles(smooth_grid(to_grid(field)))

def apply_operator(direction, perturbations, obs_weight):

    def filtered(index):
        return smooth_member(lax.dynamic_index_in_dim(direction, index, 1, keepdims=False))
    smoothed = lax.map(filtered, jnp.arange(MEMBERS))

    def accumulate(index, total):
        member = lax.dynamic_index_in_dim(perturbations, index, 1, keepdims=False).astype(jnp.float32)
        return total + member * smoothed[index][:, None, :, :]
    increment = lax.fori_loop(0, MEMBERS, accumulate, jnp.zeros(obs_weight.shape, jnp.float32))
    weighted = obs_weight * increment

    def adjoint(index):
        member = lax.dynamic_index_in_dim(perturbations, index, 1, keepdims=False).astype(jnp.float32)
        return smooth_member(lax.optimization_barrier(jnp.sum(member * weighted, axis=1)))
    back = jnp.moveaxis(lax.map(adjoint, jnp.arange(MEMBERS)), 0, 1)
    return direction + back

def reference(right_side, perturbations, precision, covered):
    mask = covered.astype(jnp.float32)
    tiles_count = precision.shape[0]
    obs_weight = (precision.reshape(tiles_count, VL, TY // 8, 8, TX // 16, 16) * mask[:, None, :, None, :, None]).reshape(tiles_count, VL, TY, TX)
    weights = jnp.zeros_like(right_side)
    residual = right_side
    direction = right_side
    norm_now = jnp.sum(residual * residual)
    for step in range(ITERS):
        image = apply_operator(direction, perturbations, obs_weight)
        length = norm_now / jnp.sum(direction * image)
        weights = weights + length * direction
        residual = residual - length * image
        if step + 1 < ITERS:
            norm_next = jnp.sum(residual * residual)
            direction = residual + norm_next / norm_now * direction
            norm_now = norm_next
    return (weights, residual)
```

```python
import functools

import jax
import jax.numpy as jnp
import ml_dtypes
import numpy as np
from jax import lax
from jax.experimental import pallas as pl
from jax.experimental.pallas import tpu as pltpu
from jax.sharding import PartitionSpec as P

ITERS = 2
TCOLS = 8
REACH = 8
LANES = 128
F32 = jnp.float32
BF16 = jnp.bfloat16


def taps_np():
    offsets = np.arange(-REACH, REACH + 1, dtype=np.float64)
    raw = np.exp(-offsets * offsets / 32.0)
    return raw / np.sqrt(np.sum(np.exp(-offsets * offsets / 16.0)))


def band(taps, source, target):
    reach = (len(taps) - 1) // 2
    gap = source[:, None] - target[None, :]
    inside = np.abs(gap) <= reach
    return np.where(inside, taps[np.clip(gap + reach, 0, 2 * reach)], 0.0)


def halves(matrix):
    whole = matrix.astype(np.float32)
    high = whole.astype(ml_dtypes.bfloat16)
    low = (whole - high.astype(np.float32)).astype(ml_dtypes.bfloat16)
    return np.stack([high, low])


def column_matrix(taps, width, edge):
    target = np.arange(width)
    slots = LANES // edge
    left = np.tile(np.arange(edge) - edge, slots)
    right = np.tile(np.arange(edge) + width, slots)
    return np.concatenate([band(taps, s, target) for s in (np.arange(width), left, right)])


def row_matrix(taps, height, members, times):
    one = band(taps, np.arange(height), np.arange(height))
    return np.kron(np.eye(members), np.linalg.matrix_power(one, times))


def split(x):
    high = x.astype(BF16)
    return high, (x - high.astype(F32)).astype(BF16)


def dot3(left, right):
    mul = functools.partial(jnp.dot, preferred_element_type=F32)
    return mul(left[0], right[0]) + (mul(left[1], right[0]) + mul(left[0], right[1]))


def both(ref):
    return ref[0], ref[1]


def lane_of(shape):
    return lax.broadcasted_iota(jnp.int32, shape, len(shape) - 1)


def pack_edges(field, edge, first):
    members, rows, width = field.shape
    slots = LANES // edge
    groups = members // slots
    lane = lane_of((rows, LANES))
    out = []
    for g in range(groups):
        total = jnp.zeros((rows, LANES), F32)
        for j in range(slots):
            member = field[j * groups + g]
            block = member[:, :LANES] if first else member[:, width - LANES :]
            start = 0 if first else LANES - edge
            shift = (j * edge - start) % LANES
            moved = pltpu.roll(block, shift, 1) if shift else block
            total = jnp.where((lane >= j * edge) & (lane < (j + 1) * edge), moved, total)
        out.append(total)
    return jnp.stack(out)


def spread_edges(packed, edge):
    groups, rows, _ = packed.shape
    slots = LANES // edge
    lane = lane_of((groups, rows, LANES))
    parts = [jnp.where((lane >= j * edge) & (lane < (j + 1) * edge), packed, 0.0) for j in range(slots)]
    return jnp.concatenate(parts, axis=0).reshape(slots * groups * rows, LANES)


def beside(field, left, right, edge):
    members, rows, width = field.shape
    return jnp.concatenate(
        [field.reshape(members * rows, width), spread_edges(left, edge), spread_edges(right, edge)], axis=1
    )


def increments(members_ref, smoothed):
    members, levels = members_ref.shape[:2]
    totals = []
    for v in range(levels):
        total = members_ref[0, v].astype(F32) * smoothed[0]
        for k in range(1, members):
            total = total + members_ref[k, v].astype(F32) * smoothed[k]
        totals.append(total)
    return jnp.stack(totals)


def adjoint(members_ref, weighted):
    members, levels = members_ref.shape[:2]
    back = []
    for k in range(members):
        total = members_ref[k, 0].astype(F32) * weighted[0]
        for v in range(1, levels):
            total = total + members_ref[k, v].astype(F32) * weighted[v]
        back.append(total)
    return jnp.stack(back)


def folded(x):
    width = x.shape[-1]
    x = x.reshape(-1, 8, width).sum(axis=0)
    return sum(x[:, i : i + LANES] for i in range(0, width, LANES))


def prepare_kernel(source, precision, covered, to_next, to_previous, obs_weight):
    levels, height, width = precision.shape
    rows, blocks = covered.shape
    to_next[...] = pack_edges(source, REACH, False)
    to_previous[...] = pack_edges(source, REACH, True)
    spread = lax.broadcasted_iota(jnp.int32, (blocks, width), 1) // (width // blocks)
    spread = (spread == lax.broadcasted_iota(jnp.int32, (blocks, width), 0)).astype(BF16)
    mask = jnp.dot(covered[...].astype(F32).astype(BF16), spread, preferred_element_type=F32)
    for v in range(levels):
        for i in range(rows):
            part = pl.ds(i * (height // rows), height // rows)
            obs_weight[v, part] = precision[v, part] * mask[i : i + 1]


def forward_kernel(source, left, right, members_ref, column, row, increment, norm):
    lhs = split(beside(source[...], left[...], right[...], REACH))
    smoothed = dot3(both(row), split(dot3(lhs, both(column))))
    increment[...] = increments(members_ref, smoothed.reshape(source.shape))
    norm[...] = folded(source[...] * source[...])


def adjoint_kernel(i0, i1, i2, i3, obs_weight, members_ref, back, to_next, to_previous, norm):
    increment = (i0[...] + i1[...]) + (i2[...] + i3[...])
    weighted = obs_weight[...] * increment
    norm[...] = folded(weighted * increment)
    back[...] = adjoint(members_ref, weighted)
    to_next[...] = pack_edges(back, 2 * REACH, False)
    to_previous[...] = pack_edges(back, 2 * REACH, True)


def middle_kernel(back, left, right, members_ref, norm_source, column, row, row_twice, first, second):
    members, height, width = back.shape
    levels = members_ref.shape[1]
    lhs = split(beside(back[...], left[...], right[...], 2 * REACH))
    both_filters = dot3(lhs, both(column))
    z = dot3(both(row), split(both_filters[:, :width]))
    smoothed = dot3(both(row_twice), split(both_filters[:, width:]))
    first[...] = z.reshape(first.shape)
    second[: levels * height] = increments(members_ref, smoothed.reshape(back.shape)).reshape(levels * height, width)
    second[levels * height :] = jnp.concatenate([norm_source[...], folded(z * z)], axis=1)


def last_kernel(i0, i1, i2, i3, obs_weight, members_ref, norm_mixed, back, to_next, to_previous, norms):
    levels, height, width = obs_weight.shape
    total = (i0[...] + i1[...]) + (i2[...] + i3[...])
    increment = total[: levels * height].reshape(levels, height, width)
    sums = total[levels * height :]
    weighted = obs_weight[...] * increment
    four = [sums[:, :LANES], norm_mixed[...], sums[:, LANES:], folded(weighted * increment)]
    row = lax.broadcasted_iota(jnp.int32, (8, LANES), 0)
    stacked = jnp.zeros((8, LANES), F32)
    for i, part in enumerate(four):
        stacked = jnp.where(row == i, jnp.sum(part, axis=0, keepdims=True), stacked)
    norms[...] = stacked
    back[...] = adjoint(members_ref, weighted)
    to_next[...] = pack_edges(back, REACH, False)
    to_previous[...] = pack_edges(back, REACH, True)


def filter_kernel(back, left, right, column, row, out):
    lhs = split(beside(back[...], left[...], right[...], REACH))
    out[...] = dot3(both(row), split(dot3(lhs, both(column)))).reshape(out.shape)


def combine_kernel(norms, source, first, second, weights, residual):
    total = jnp.sum(norms[...], axis=1, keepdims=True)
    bb, bg, gg, gh = (total[i : i + 1] for i in range(4))
    bg, gg, gh = bg / bb, gg / bb, gh / bb
    q = 1.0 / (1.0 + bg)
    p = bg * q
    ratio = (gg - bg * bg) * q * q
    d = p + ratio
    square = d * d - 2.0 * d * q * bg + q * q * gg
    image = d * d * bg - 2.0 * d * q * gg + q * q * gh
    step = ratio / (square + image)
    b, g, h = source[...], first[...], second[...]
    weights[...] = (q + step * d) * b - (step * q) * g
    residual[...] = (p - step * d) * b + (step * q - q - step * d) * g + (step * q) * h


def call(kernel, outs, *operands, cost=None):
    shapes = [jax.ShapeDtypeStruct(shape, F32) for shape in outs]
    vmem = pl.BlockSpec(memory_space=pltpu.VMEM)
    return pl.pallas_call(
        kernel,
        out_shape=shapes,
        in_specs=[vmem] * len(operands),
        out_specs=[vmem] * len(outs),
        compiler_params=pltpu.CompilerParams(vmem_limit_bytes=24 * 1024 * 1024),
        cost_estimate=cost,
    )(*operands)


def from_both_sides(to_next, to_previous, axis):
    count = lax.axis_size(axis)
    left = lax.ppermute(to_next, axis, [(i, (i + 1) % count) for i in range(count)])
    right = lax.ppermute(to_previous, axis, [((i + 1) % count, i) for i in range(count)])
    return left, right


def from_all(value, axis):
    count = lax.axis_size(axis)
    return [value] + [lax.ppermute(value, axis, [(i, i ^ k) for i in range(count)]) for k in range(1, count)]


def summed(value, axis):
    count = lax.axis_size(axis)
    step = 1
    while step < count:
        value = value + lax.ppermute(value, axis, [(i, i ^ step) for i in range(count)])
        step *= 2
    return value


def one_tile_row(right_side, perturbations, precision, covered):
    source, members_data = right_side[0], perturbations[0]
    members, levels, height, width = members_data.shape
    taps = taps_np()
    twice = np.convolve(taps, taps)
    field = (members, height, width)
    near = (members * REACH // LANES, height, LANES)
    far = (2 * members * REACH // LANES, height, LANES)
    small = (8, LANES)
    column = halves(column_matrix(taps, width, REACH))
    column_wide = halves(
        np.concatenate(
            [column_matrix(taps, width, 2 * REACH), column_matrix(twice, width, 2 * REACH)], axis=1
        )
    )
    row = halves(row_matrix(taps, height, members, 1))
    row_twice = halves(row_matrix(taps, height, members, 2))

    to_next, to_previous, obs_weight = call(
        prepare_kernel, [near, near, precision.shape[1:]], source, precision[0], covered[0]
    )
    left, right = from_both_sides(to_next, to_previous, "tile")
    increment, norm_source = call(
        forward_kernel, [(levels, height, width), small], source, left, right, members_data, column, row
    )
    parts = from_all(increment, "mem")
    back, to_next, to_previous, norm_mixed = call(
        adjoint_kernel, [field, far, far, small], *parts, obs_weight, members_data
    )
    left, right = from_both_sides(to_next, to_previous, "tile")
    first, second = call(
        middle_kernel,
        [field, (levels * height + 8, width)],
        back, left, right, members_data, norm_source, column_wide, row, row_twice,
    )
    parts = from_all(second, "mem")
    back, to_next, to_previous, norms = call(
        last_kernel, [field, near, near, small], *parts, obs_weight, members_data, norm_mixed
    )
    left, right = from_both_sides(to_next, to_previous, "tile")
    (second,) = call(filter_kernel, [field], back, left, right, column, row)
    norms = summed(norms, "tile")
    weights, residual = call(combine_kernel, [field, field], norms, source, first, second)
    return weights[None], residual[None]


def passed_along(value, axis, steps):
    count = lax.axis_size(axis)
    first, last = (max(0, -steps), min(count, count - steps))
    return lax.ppermute(value, axis, [(source, source + steps) for source in range(first, last)])


def smooth(field):
    taps = taps_np().astype(np.float32)
    height, width = field.shape[1:]
    above = passed_along(field[:, height - REACH :, :], "tile", TCOLS)
    below = passed_along(field[:, :REACH, :], "tile", -TCOLS)
    padded = jnp.concatenate([above, field, below], axis=1)
    along = sum(taps[j] * padded[:, j : j + height, :] for j in range(2 * REACH + 1))
    left, right = from_both_sides(along[:, :, width - REACH :], along[:, :, :REACH], "tile")
    sided = jnp.concatenate([left, along, right], axis=2)
    return sum(taps[j] * sided[:, :, j : j + width] for j in range(2 * REACH + 1))


def several_tile_rows(right_side, perturbations, precision, covered):
    source = right_side[0]
    members_data = perturbations[0].astype(F32)
    levels, height, width = precision.shape[1:]
    rows, blocks = covered.shape[1:]
    mask = covered[0].astype(F32)
    obs_weight = (
        precision[0].reshape(levels, rows, height // rows, blocks, width // blocks) * mask[None, :, None, :, None]
    ).reshape(levels, height, width)

    def operator(direction):
        partial_terms = jnp.einsum("kvyx,kyx->vyx", members_data, smooth(direction))
        weighted = obs_weight * lax.psum(partial_terms, "mem")
        return direction + smooth(jnp.einsum("kvyx,vyx->kyx", members_data, weighted))

    weights = jnp.zeros_like(source)
    residual = direction = source
    norm_now = lax.psum(jnp.sum(source * source), ("tile", "mem"))
    for step in range(ITERS):
        image = operator(direction)
        length = norm_now / lax.psum(jnp.sum(direction * image), ("tile", "mem"))
        weights = weights + length * direction
        residual = residual - length * image
        if step + 1 < ITERS:
            norm_next = lax.psum(jnp.sum(residual * residual), ("tile", "mem"))
            direction = residual + norm_next / norm_now * direction
            norm_now = norm_next
    return weights[None], residual[None]


def solution(mesh):
    single = mesh.shape["tile"] == TCOLS and mesh.shape["mem"] == 4
    local = one_tile_row if single else several_tile_rows
    return jax.shard_map(
        local,
        mesh=mesh,
        in_specs=(
            P("tile", "mem", None, None),
            P("tile", "mem", None, None, None),
            P("tile", None, None, None),
            P("tile", None, None),
        ),
        out_specs=(P("tile", "mem", None, None), P("tile", "mem", None, None)),
        check_vma=False,
    )
```

```python
import functools

import jax
import jax.numpy as jnp
import ml_dtypes
import numpy as np
from jax import lax
from jax.experimental import pallas as pl
from jax.experimental.pallas import tpu as pltpu
from jax.sharding import PartitionSpec as P

ITERS = 2
TCOLS = 8
REACH = 8
LANES = 128
F32 = jnp.float32
BF16 = jnp.bfloat16


def taps_np():
    offsets = np.arange(-REACH, REACH + 1, dtype=np.float64)
    raw = np.exp(-offsets * offsets / 32.0)
    return raw / np.sqrt(np.sum(np.exp(-offsets * offsets / 16.0)))


def band(taps, source, target):
    reach = (len(taps) - 1) // 2
    gap = source[:, None] - target[None, :]
    inside = np.abs(gap) <= reach
    return np.where(inside, taps[np.clip(gap + reach, 0, 2 * reach)], 0.0)


def halves(matrix):
    whole = matrix.astype(np.float32)
    high = whole.astype(ml_dtypes.bfloat16)
    low = (whole - high.astype(np.float32)).astype(ml_dtypes.bfloat16)
    return np.stack([high, low])


def column_matrix(taps, width, edge):
    target = np.arange(width)
    slots = LANES // edge
    left = np.tile(np.arange(edge) - edge, slots)
    right = np.tile(np.arange(edge) + width, slots)
    return np.concatenate([band(taps, s, target) for s in (np.arange(width), left, right)])


def row_matrix(taps, height, members, times):
    one = band(taps, np.arange(height), np.arange(height))
    return np.kron(np.eye(members), np.linalg.matrix_power(one, times))


def split(x):
    high = x.astype(BF16)
    return high, (x - high.astype(F32)).astype(BF16)


def dot3(left, right):
    mul = functools.partial(jnp.dot, preferred_element_type=F32)
    return mul(left[0], right[0]) + (mul(left[1], right[0]) + mul(left[0], right[1]))


def both(ref):
    return ref[0], ref[1]


def lane_of(shape):
    return lax.broadcasted_iota(jnp.int32, shape, len(shape) - 1)


def pack_edges(field, edge, first):
    members, rows, width = field.shape
    slots = LANES // edge
    groups = members // slots
    lane = lane_of((rows, LANES))
    out = []
    for g in range(groups):
        total = jnp.zeros((rows, LANES), F32)
        for j in range(slots):
            member = field[j * groups + g]
            block = member[:, :LANES] if first else member[:, width - LANES :]
            start = 0 if first else LANES - edge
            shift = (j * edge - start) % LANES
            moved = pltpu.roll(block, shift, 1) if shift else block
            total = jnp.where((lane >= j * edge) & (lane < (j + 1) * edge), moved, total)
        out.append(total)
    return jnp.stack(out)


def edges_for_partners(field, edge):
    odd = lax.axis_index("tile") % 2 == 1
    first, last = pack_edges(field, edge, True), pack_edges(field, edge, False)
    return jnp.where(odd, first, last), jnp.where(odd, last, first)


def sides_of(core, chip):
    odd = lax.axis_index("tile") % 2 == 1
    return jnp.where(odd, core, chip), jnp.where(odd, chip, core)


def spread_edges(packed, edge):
    groups, rows, _ = packed.shape
    slots = LANES // edge
    lane = lane_of((groups, rows, LANES))
    parts = [jnp.where((lane >= j * edge) & (lane < (j + 1) * edge), packed, 0.0) for j in range(slots)]
    return jnp.concatenate(parts, axis=0).reshape(slots * groups * rows, LANES)


def beside(field, core, chip, edge):
    members, rows, width = field.shape
    left, right = sides_of(core, chip)
    return jnp.concatenate(
        [field.reshape(members * rows, width), spread_edges(left, edge), spread_edges(right, edge)], axis=1
    )


def increments(members_ref, smoothed):
    members, levels = members_ref.shape[:2]
    totals = []
    for v in range(levels):
        total = members_ref[0, v].astype(F32) * smoothed[0]
        for k in range(1, members):
            total = total + members_ref[k, v].astype(F32) * smoothed[k]
        totals.append(total)
    return jnp.stack(totals)


def adjoint(members_ref, weighted):
    members, levels = members_ref.shape[:2]
    back = []
    for k in range(members):
        total = members_ref[k, 0].astype(F32) * weighted[0]
        for v in range(1, levels):
            total = total + members_ref[k, v].astype(F32) * weighted[v]
        back.append(total)
    return jnp.stack(back)


def folded(x):
    width = x.shape[-1]
    x = x.reshape(-1, 8, width).sum(axis=0)
    return sum(x[:, i : i + LANES] for i in range(0, width, LANES))


def edges_kernel(source, held, to_core, to_chip, sem):
    copy = pltpu.make_async_copy(source, held, sem)
    copy.start()
    copy.wait()
    to_core[...], to_chip[...] = edges_for_partners(held, REACH)


def fetch_kernel(*refs):
    count = (len(refs) - 2) // 2
    copies = [pltpu.make_async_copy(refs[1 + i], refs[1 + count + i], refs[-1].at[i]) for i in range(count)]
    for copy in copies:
        copy.start()
    for copy in copies:
        copy.wait()


def forward_kernel(source, core, chip, members_ref, column, row, increment):
    members, levels, height, width = members_ref.shape
    lhs = split(beside(source[...], core[...], chip[...], REACH))
    smoothed = dot3(both(row), split(dot3(lhs, both(column)))).reshape(source.shape)
    increment[: levels * height] = increments(members_ref, smoothed).reshape(levels * height, width)
    increment[levels * height :] = (source[...] * source[...]).reshape(-1, 8, width).sum(axis=0)


def weight_of(precision, covered):
    levels, height, width = precision.shape
    rows, blocks = covered.shape
    spread = lax.broadcasted_iota(jnp.int32, (blocks, width), 1) // (width // blocks)
    spread = (spread == lax.broadcasted_iota(jnp.int32, (blocks, width), 0)).astype(BF16)
    mask = jnp.dot(covered[...].astype(F32).astype(BF16), spread, preferred_element_type=F32)
    tall = height // rows
    mask = jnp.concatenate([jnp.broadcast_to(mask[i : i + 1], (tall, width)) for i in range(rows)], axis=0)
    return precision[...] * mask


def adjoint_kernel(
    i0, i1, i2, i3, precision, covered, members_ref, back, to_core, to_chip, obs_weight, weighted, sums
):
    levels, height, width = precision.shape
    total = (i0[...] + i1[...]) + (i2[...] + i3[...])
    increment = total[: levels * height].reshape(levels, height, width)
    obs_weight[...] = weight_of(precision, covered)
    weighted[...] = obs_weight[...] * increment
    sums[0] = folded(total[levels * height :])
    sums[1] = folded(weighted[...] * increment)
    back[...] = adjoint(members_ref, weighted)
    to_core[...], to_chip[...] = edges_for_partners(back, 2 * REACH)


def filtered(field, core, chip, edge, column, row):
    lhs = split(beside(field[...], core[...], chip[...], edge))
    return dot3(both(row), split(dot3(lhs, both(column)))).reshape(field.shape)


def middle_kernel(back, core, chip, members_ref, column_twice, row_twice, increment):
    smoothed = filtered(back, core, chip, 2 * REACH, column_twice, row_twice)
    increment[...] = increments(members_ref, smoothed)


def wide_filter_kernel(back, core, chip, column, row, out):
    out[...] = filtered(back, core, chip, 2 * REACH, column, row)


def filter_kernel(back, core, chip, column, row, out):
    rows = back.shape[1]
    out[...] = filtered(back, core[:, :rows], chip[:, :rows], REACH, column, row)


def last_kernel(i0, i1, i2, i3, obs_weight, before, sums, members_ref, back, to_core, to_chip):
    rows = back.shape[1]
    increment = (i0[...] + i1[...]) + (i2[...] + i3[...])
    weighted = obs_weight[...] * increment
    four = [sums[0], sums[1], folded(before[...] * increment), folded(weighted * increment)]
    row = lax.broadcasted_iota(jnp.int32, (8, LANES), 0)
    stacked = jnp.zeros((8, LANES), F32)
    for i, part in enumerate(four):
        stacked = jnp.where(row == i, jnp.sum(part, axis=0, keepdims=True), stacked)
    back[...] = adjoint(members_ref, weighted)
    to_core[:, :rows], to_chip[:, :rows] = edges_for_partners(back, REACH)
    to_core[0, rows:] = stacked
    to_chip[0, rows:] = stacked


def combine_kernel(own, other, source, first, second, weights, residual, held_weights, held_residual, sems):
    total = jnp.sum(own[...] + other[...], axis=1, keepdims=True)
    bb, bg, gg, gh = (total[i : i + 1] for i in range(4))
    bg, gg, gh = bg / bb, gg / bb, gh / bb
    q = 1.0 / (1.0 + bg)
    p = bg * q
    ratio = (gg - bg * bg) * q * q
    d = p + ratio
    square = d * d - 2.0 * d * q * bg + q * q * gg
    image = d * d * bg - 2.0 * d * q * gg + q * q * gh
    step = ratio / (square + image)
    members = source.shape[0]
    pieces = sems.shape[1]
    copies = []
    for i in range(pieces):
        part = pl.ds(i * (members // pieces), members // pieces)
        b, g, h = source[part], first[part], second[part]
        held_weights[part] = (q + step * d) * b - (step * q) * g
        held_residual[part] = (p - step * d) * b + (step * q - q - step * d) * g + (step * q) * h
        for k, (held, out) in enumerate(((held_weights, weights), (held_residual, residual))):
            copies.append(pltpu.make_async_copy(held.at[part], out.at[part], sems.at[k, i]))
            copies[-1].start()
    for copy in copies:
        copy.wait()


def call(kernel, outs, *operands, cost=None):
    shapes = [jax.ShapeDtypeStruct(shape, F32) for shape in outs]
    vmem = pl.BlockSpec(memory_space=pltpu.VMEM)
    return pl.pallas_call(
        kernel,
        out_shape=shapes,
        in_specs=[vmem] * len(operands),
        out_specs=[vmem] * len(outs),
        compiler_params=pltpu.CompilerParams(vmem_limit_bytes=24 * 1024 * 1024),
        cost_estimate=cost,
    )(*operands)


def in_hbm(array):
    return pltpu.with_memory_space_constraint(array, pltpu.HBM)


def held_edges(source):
    members, height, width = source.shape
    near = (members * REACH // LANES, height, LANES)
    vmem = pl.BlockSpec(memory_space=pltpu.VMEM)
    return pl.pallas_call(
        edges_kernel,
        out_shape=[pltpu.VMEM(source.shape, F32), pltpu.VMEM(near, F32), pltpu.VMEM(near, F32)],
        in_specs=[pl.BlockSpec(memory_space=pltpu.HBM)],
        out_specs=[vmem] * 3,
        scratch_shapes=[pltpu.SemaphoreType.DMA],
        compiler_params=pltpu.CompilerParams(vmem_limit_bytes=24 * 1024 * 1024),
    )(in_hbm(source))


def fetched(after, *arrays):
    vmem = pl.BlockSpec(memory_space=pltpu.VMEM)
    hbm = pl.BlockSpec(memory_space=pltpu.HBM)
    size = sum(a.size * a.dtype.itemsize for a in arrays)
    return pl.pallas_call(
        fetch_kernel,
        out_shape=[pltpu.VMEM(a.shape, a.dtype) for a in arrays],
        in_specs=[vmem] + [hbm] * len(arrays),
        out_specs=[vmem] * len(arrays),
        scratch_shapes=[pltpu.SemaphoreType.DMA((len(arrays),))],
        compiler_params=pltpu.CompilerParams(vmem_limit_bytes=24 * 1024 * 1024),
        cost_estimate=pl.CostEstimate(flops=0, bytes_accessed=2 * size, transcendentals=0),
    )(after, *map(in_hbm, arrays))


def combined(own, other, source, first, second):
    vmem = pl.BlockSpec(memory_space=pltpu.VMEM)
    hbm = pl.BlockSpec(memory_space=pltpu.HBM)
    return pl.pallas_call(
        combine_kernel,
        out_shape=[jax.ShapeDtypeStruct(source.shape, F32)] * 2,
        in_specs=[vmem] * 5,
        out_specs=[hbm] * 2,
        scratch_shapes=[pltpu.VMEM(source.shape, F32)] * 2 + [pltpu.SemaphoreType.DMA((2, 4))],
        compiler_params=pltpu.CompilerParams(vmem_limit_bytes=24 * 1024 * 1024),
    )(own, other, source, first, second)


def from_both_sides(to_next, to_previous, axis):
    count = lax.axis_size(axis)
    left = lax.ppermute(to_next, axis, [(i, (i + 1) % count) for i in range(count)])
    right = lax.ppermute(to_previous, axis, [((i + 1) % count, i) for i in range(count)])
    return left, right


def from_core(value):
    count = lax.axis_size("tile")
    return lax.ppermute(value, "tile", [(i, i ^ 1) for i in range(count)])


def from_chip(value):
    count = lax.axis_size("tile")
    return lax.ppermute(value, "tile", [(i, (i + 1) % count if i % 2 else (i - 1) % count) for i in range(count)])


def from_all(value, axis):
    count = lax.axis_size(axis)
    return [value] + [lax.ppermute(value, axis, [(i, i ^ k) for i in range(count)]) for k in range(1, count)]


def one_tile_row(right_side, perturbations, precision, covered):
    source, members_data = right_side[0], perturbations[0]
    members, levels, height, width = members_data.shape
    taps = taps_np()
    twice = np.convolve(taps, taps)
    field = (members, height, width)
    near = (members * REACH // LANES, height, LANES)
    far = (2 * members * REACH // LANES, height, LANES)
    plane = (levels, height, width)
    constants = [
        halves(column_matrix(taps, width, REACH)),
        halves(row_matrix(taps, height, members, 1)),
        halves(column_matrix(taps, width, 2 * REACH)),
        halves(column_matrix(twice, width, 2 * REACH)),
        halves(row_matrix(taps, height, members, 2)),
    ]

    source, to_core, to_chip = held_edges(source)
    core, chip = from_core(to_core), from_chip(to_chip)
    members_data, column, row = fetched(to_core, members_data, *constants[:2])
    (increment,) = call(
        forward_kernel, [(levels * height + 8, width)], source, core, chip, members_data, column, row
    )
    parts = from_all(increment, "mem")
    precision, covered, column_far, column_twice, row_twice = fetched(increment, precision[0], covered[0], *constants[2:])
    back, to_core, to_chip, obs_weight, weighted, sums = call(
        adjoint_kernel, [field, far, far, plane, plane, (2, 8, LANES)], *parts, precision, covered, members_data
    )
    core, chip = from_core(to_core), from_chip(to_chip)
    (increment,) = call(middle_kernel, [plane], back, core, chip, members_data, column_twice, row_twice)
    parts = from_all(increment, "mem")
    (first,) = call(wide_filter_kernel, [field], back, core, chip, column_far, row)
    ended = (1, height + 8, LANES)
    back, to_core, to_chip = call(
        last_kernel, [field, ended, ended], *parts, obs_weight, weighted, sums, members_data
    )
    core = from_core(to_core)
    to_chip = jnp.concatenate([to_chip[:, :height], to_chip[:, height:] + core[:, height:]], axis=1)
    chip = from_chip(to_chip)
    norms = to_chip[0, height:] + chip[0, height:]
    count = lax.axis_size("tile")
    others = lax.ppermute(norms, "tile", [(i, (i + count // 2) % count) for i in range(count)])
    (second,) = call(filter_kernel, [field], back, core, chip, column, row)
    weights, residual = combined(norms, others, source, first, second)
    return weights[None], residual[None]


def passed_along(value, axis, steps):
    count = lax.axis_size(axis)
    first, last = (max(0, -steps), min(count, count - steps))
    return lax.ppermute(value, axis, [(source, source + steps) for source in range(first, last)])


def smooth(field):
    taps = taps_np().astype(np.float32)
    height, width = field.shape[1:]
    above = passed_along(field[:, height - REACH :, :], "tile", TCOLS)
    below = passed_along(field[:, :REACH, :], "tile", -TCOLS)
    padded = jnp.concatenate([above, field, below], axis=1)
    along = sum(taps[j] * padded[:, j : j + height, :] for j in range(2 * REACH + 1))
    left, right = from_both_sides(along[:, :, width - REACH :], along[:, :, :REACH], "tile")
    sided = jnp.concatenate([left, along, right], axis=2)
    return sum(taps[j] * sided[:, :, j : j + width] for j in range(2 * REACH + 1))


def several_tile_rows(right_side, perturbations, precision, covered):
    source = right_side[0]
    members_data = perturbations[0].astype(F32)
    levels, height, width = precision.shape[1:]
    rows, blocks = covered.shape[1:]
    mask = covered[0].astype(F32)
    obs_weight = (
        precision[0].reshape(levels, rows, height // rows, blocks, width // blocks) * mask[None, :, None, :, None]
    ).reshape(levels, height, width)

    def operator(direction):
        partial_terms = jnp.einsum("kvyx,kyx->vyx", members_data, smooth(direction))
        weighted = obs_weight * lax.psum(partial_terms, "mem")
        return direction + smooth(jnp.einsum("kvyx,vyx->kyx", members_data, weighted))

    weights = jnp.zeros_like(source)
    residual = direction = source
    norm_now = lax.psum(jnp.sum(source * source), ("tile", "mem"))
    for step in range(ITERS):
        image = operator(direction)
        length = norm_now / lax.psum(jnp.sum(direction * image), ("tile", "mem"))
        weights = weights + length * direction
        residual = residual - length * image
        if step + 1 < ITERS:
            norm_next = lax.psum(jnp.sum(residual * residual), ("tile", "mem"))
            direction = residual + norm_next / norm_now * direction
            norm_now = norm_next
    return weights[None], residual[None]


def solution(mesh):
    single = mesh.shape["tile"] == TCOLS and mesh.shape["mem"] == 4
    local = one_tile_row if single else several_tile_rows
    return jax.shard_map(
        local,
        mesh=mesh,
        in_specs=(
            P("tile", "mem", None, None),
            P("tile", "mem", None, None, None),
            P("tile", None, None, None),
            P("tile", None, None),
        ),
        out_specs=(P("tile", "mem", None, None), P("tile", "mem", None, None)),
        check_vma=False,
    )
```

```python
import functools

import jax
import jax.numpy as jnp
import ml_dtypes
import numpy as np
from jax import lax
from jax.experimental import pallas as pl
from jax.experimental.pallas import tpu as pltpu
from jax.sharding import PartitionSpec as P

ITERS = 2
TCOLS = 8
REACH = 8
EDGE = 2 * REACH
LANES = 128
F32 = jnp.float32
BF16 = jnp.bfloat16


def taps_np():
    offsets = np.arange(-REACH, REACH + 1, dtype=np.float64)
    raw = np.exp(-offsets * offsets / 32.0)
    return raw / np.sqrt(np.sum(np.exp(-offsets * offsets / 16.0)))


def band(taps, source, target):
    reach = (len(taps) - 1) // 2
    gap = source[:, None] - target[None, :]
    inside = np.abs(gap) <= reach
    return np.where(inside, taps[np.clip(gap + reach, 0, 2 * reach)], 0.0)


def halves(matrix):
    whole = matrix.astype(np.float32)
    high = whole.astype(ml_dtypes.bfloat16)
    low = (whole - high.astype(np.float32)).astype(ml_dtypes.bfloat16)
    return np.stack([high, low])


def column_matrix(taps, width, edge):
    target = np.arange(width)
    slots = LANES // edge
    left = np.tile(np.arange(edge) - edge, slots)
    right = np.tile(np.arange(edge) + width, slots)
    return np.concatenate([band(taps, s, target) for s in (np.arange(width), left, right)])


def row_matrix(taps, height, members, times):
    one = band(taps, np.arange(height), np.arange(height))
    return np.kron(np.eye(members), np.linalg.matrix_power(one, times))


def edge_matrix(taps, edge):
    inner = np.arange(edge)
    sides = (band(taps, inner - edge, inner), band(taps, inner + edge, inner))
    return np.stack([halves(np.kron(np.eye(LANES // edge), side)) for side in sides])


def split(x):
    high = x.astype(BF16)
    return high, (x - high.astype(F32)).astype(BF16)


def dot3(left, right):
    mul = functools.partial(jnp.dot, preferred_element_type=F32)
    return mul(left[0], right[0]) + (mul(left[1], right[0]) + mul(left[0], right[1]))


def both(ref):
    return ref[0], ref[1]


def lane_of(shape):
    return lax.broadcasted_iota(jnp.int32, shape, len(shape) - 1)


def pack_edges(field, edge, first):
    members, rows, width = field.shape
    slots = LANES // edge
    groups = members // slots
    lane = lane_of((rows, LANES))
    out = []
    for g in range(groups):
        total = jnp.zeros((rows, LANES), F32)
        for j in range(slots):
            member = field[j * groups + g]
            block = member[:, :LANES] if first else member[:, width - LANES :]
            start = 0 if first else LANES - edge
            shift = (j * edge - start) % LANES
            moved = pltpu.roll(block, shift, 1) if shift else block
            total = jnp.where((lane >= j * edge) & (lane < (j + 1) * edge), moved, total)
        out.append(total)
    return jnp.stack(out)


def edges_for_partners(field, edge):
    odd = lax.axis_index("tile") % 2 == 1
    first, last = pack_edges(field, edge, True), pack_edges(field, edge, False)
    return jnp.where(odd, first, last), jnp.where(odd, last, first)


def sides_of(core, chip):
    odd = lax.axis_index("tile") % 2 == 1
    return jnp.where(odd, core, chip), jnp.where(odd, chip, core)


def spread_edges(packed, edge):
    groups, rows, _ = packed.shape
    slots = LANES // edge
    lane = lane_of((groups, rows, LANES))
    parts = [jnp.where((lane >= j * edge) & (lane < (j + 1) * edge), packed, 0.0) for j in range(slots)]
    return jnp.concatenate(parts, axis=0).reshape(slots * groups * rows, LANES)


def beside(field, core, chip, edge):
    members, rows, width = field.shape
    left, right = sides_of(core, chip)
    return jnp.concatenate(
        [field.reshape(members * rows, width), spread_edges(left, edge), spread_edges(right, edge)], axis=1
    )


def increments(members_ref, smoothed):
    members, levels = members_ref.shape[:2]
    totals = []
    for v in range(levels):
        total = members_ref[0, v].astype(F32) * smoothed[0]
        for k in range(1, members):
            total = total + members_ref[k, v].astype(F32) * smoothed[k]
        totals.append(total)
    return jnp.stack(totals)


def adjoint(members_ref, weighted):
    members, levels = members_ref.shape[:2]
    back = []
    for k in range(members):
        total = members_ref[k, 0].astype(F32) * weighted[0]
        for v in range(1, levels):
            total = total + members_ref[k, v].astype(F32) * weighted[v]
        back.append(total)
    return jnp.stack(back)


def folded(x):
    width = x.shape[-1]
    x = x.reshape(-1, 8, width).sum(axis=0)
    return sum(x[:, i : i + LANES] for i in range(0, width, LANES))


def edges_kernel(source, held, to_core, to_chip, sem):
    copy = pltpu.make_async_copy(source, held, sem)
    copy.start()
    copy.wait()
    to_core[...], to_chip[...] = edges_for_partners(held, EDGE)


def fetch_kernel(*refs):
    count = (len(refs) - 2) // 2
    copies = [pltpu.make_async_copy(refs[1 + i], refs[1 + count + i], refs[-1].at[i]) for i in range(count)]
    for copy in copies:
        copy.start()
    for copy in copies:
        copy.wait()


def own_columns(field, column, row):
    members, height, width = field.shape
    lhs = split(field[...].reshape(members * height, width))
    return dot3(both(row), split(dot3(lhs, both(column)))).reshape(field.shape)


def tap_at(gap, inside):
    scale = 1.0 / np.sqrt(np.sum(np.exp(-(np.arange(-REACH, REACH + 1.0) ** 2) / 16.0)))
    square = (gap * gap).astype(F32)
    return jnp.where(inside & (jnp.abs(gap) <= REACH), jnp.exp(square * (-1.0 / 32.0)) * scale, 0.0)


def gaps(rows, columns):
    shape = (rows, columns)
    down, across = (lax.broadcasted_iota(jnp.int32, shape, i) for i in range(2))
    return down, across, down - across


def kept(ref, matrix):
    ref[0], ref[1] = split(matrix)


def first_kernel(source, after, members_hbm, increment, members_ref, edge_members, edge, thin, sem):
    copy = pltpu.make_async_copy(members_hbm, members_ref, sem)
    copy.start()
    members, levels, height, width = members_ref.shape
    _, _, gap = gaps(width, width)
    column = split(tap_at(gap, True))
    down, across, gap = gaps(members * height, members * height)
    row = split(tap_at(gap, down // height == across // height))
    lhs = split(source[...].reshape(members * height, width))
    smoothed = dot3(row, split(dot3(lhs, column))).reshape(source.shape)
    increment[levels * height :] = (source[...] * source[...]).reshape(-1, 8, width).sum(axis=0)
    down, across, gap = gaps(LANES, LANES)
    same = down // EDGE == across // EDGE
    kept(edge.at[0], tap_at(gap - EDGE, same))
    kept(edge.at[1], tap_at(gap + EDGE, same))
    down, across, gap = gaps(*thin.shape[1:])
    kept(thin, tap_at(gap, down // height == across // height))
    copy.wait()
    increment[: levels * height] = increments(members_ref, smoothed).reshape(levels * height, width)
    for v in range(levels):
        level = members_ref[:, v].astype(F32)
        edge_members[0, :, v] = pack_edges(level, EDGE, True)
        edge_members[1, :, v] = pack_edges(level, EDGE, False)


def second_kernel(back, column, row, members_ref, increment):
    increment[...] = increments(members_ref, own_columns(back, column, row))


def edge_kernel(inside, core, chip, edge_members, edge, thin, out):
    groups, height, _ = core.shape
    levels = edge_members.shape[2]
    width = out.shape[-1]
    halo = jnp.concatenate([side.reshape(groups * height, LANES) for side in sides_of(core[...], chip[...])], axis=1)
    halo = dot3(both(thin), split(halo))
    lane = lane_of((levels, height, LANES))
    out[...] = inside[...]
    for side in range(2):
        part = halo[:, :LANES] if side == 0 else halo[:, LANES:]
        part = dot3(split(part), (edge[side, 0], edge[side, 1])).reshape(groups, 1, height, LANES)
        total = jnp.sum(edge_members[side] * part, axis=0).reshape(levels * height, LANES)
        step = EDGE
        while step < LANES:
            total = total + pltpu.roll(total, step, 1)
            step *= 2
        total = total.reshape(levels, height, LANES)
        if side == 0:
            span, mask = pl.ds(0, LANES), lane < EDGE
        else:
            span, mask = pl.ds(width - LANES, LANES), lane >= LANES - EDGE
        rows = pl.ds(0, levels * height)
        out[rows, span] = out[rows, span] + jnp.where(mask, total, 0.0).reshape(levels * height, LANES)


def weight_of(precision, covered):
    levels, height, width = precision.shape
    rows, blocks = covered.shape
    spread = lax.broadcasted_iota(jnp.int32, (blocks, width), 1) // (width // blocks)
    spread = (spread == lax.broadcasted_iota(jnp.int32, (blocks, width), 0)).astype(BF16)
    mask = jnp.dot(covered[...].astype(F32).astype(BF16), spread, preferred_element_type=F32)
    tall = height // rows
    mask = jnp.concatenate([jnp.broadcast_to(mask[i : i + 1], (tall, width)) for i in range(rows)], axis=0)
    return precision[...] * mask


def adjoint_kernel(
    i0, i1, i2, i3, precision, covered, members_ref, back, to_core, to_chip, obs_weight, weighted, sums
):
    levels, height, width = precision.shape
    total = (i0[...] + i1[...]) + (i2[...] + i3[...])
    increment = total[: levels * height].reshape(levels, height, width)
    obs_weight[...] = weight_of(precision, covered)
    weighted[...] = obs_weight[...] * increment
    sums[0] = folded(total[levels * height :])
    sums[1] = folded(weighted[...] * increment)
    back[...] = adjoint(members_ref, weighted)
    to_core[...], to_chip[...] = edges_for_partners(back, EDGE)


def filter_kernel(back, core, chip, column, row, out):
    groups, height = back.shape[0] * EDGE // LANES, back.shape[1]
    core, chip = (x[: groups * height].reshape(groups, height, LANES) for x in (core, chip))
    lhs = split(beside(back[...], core, chip, EDGE))
    out[...] = dot3(both(row), split(dot3(lhs, both(column)))).reshape(out.shape)


def last_kernel(i0, i1, i2, i3, obs_weight, before, sums, members_ref, back, to_core, to_chip):
    levels, height, width = obs_weight.shape
    increment = ((i0[...] + i1[...]) + (i2[...] + i3[...])).reshape(obs_weight.shape)
    weighted = obs_weight[...] * increment
    four = [sums[0], sums[1], folded(before[...] * increment), folded(weighted * increment)]
    row = lax.broadcasted_iota(jnp.int32, (8, LANES), 0)
    stacked = jnp.zeros((8, LANES), F32)
    for i, part in enumerate(four):
        stacked = jnp.where(row == i, jnp.sum(part, axis=0, keepdims=True), stacked)
    back[...] = adjoint(members_ref, weighted)
    core, chip = edges_for_partners(back, EDGE)
    rows = core.shape[0] * height
    to_core[:rows] = core.reshape(rows, LANES)
    to_core[rows:] = stacked
    to_chip[...] = chip.reshape(rows, LANES)


def combine_kernel(norms, source, first, second, weights, residual, held_weights, held_residual, sems):
    total = jnp.sum(norms[...], axis=1, keepdims=True)
    bb, bg, gg, gh = (total[i : i + 1] for i in range(4))
    bg, gg, gh = bg / bb, gg / bb, gh / bb
    q = 1.0 / (1.0 + bg)
    p = bg * q
    ratio = (gg - bg * bg) * q * q
    d = p + ratio
    square = d * d - 2.0 * d * q * bg + q * q * gg
    image = d * d * bg - 2.0 * d * q * gg + q * q * gh
    step = ratio / (square + image)
    members = source.shape[0]
    pieces = sems.shape[1]
    copies = []
    for i in range(pieces):
        part = pl.ds(i * (members // pieces), members // pieces)
        b, g, h = source[part], first[part], second[part]
        held_weights[part] = (q + step * d) * b - (step * q) * g
        held_residual[part] = (p - step * d) * b + (step * q - q - step * d) * g + (step * q) * h
        for k, (held, out) in enumerate(((held_weights, weights), (held_residual, residual))):
            copies.append(pltpu.make_async_copy(held.at[part], out.at[part], sems.at[k, i]))
            copies[-1].start()
    for copy in copies:
        copy.wait()


def call(kernel, outs, *operands, cost=None):
    shapes = [jax.ShapeDtypeStruct(shape, F32) for shape in outs]
    vmem = pl.BlockSpec(memory_space=pltpu.VMEM)
    return pl.pallas_call(
        kernel,
        out_shape=shapes,
        in_specs=[vmem] * len(operands),
        out_specs=[vmem] * len(outs),
        compiler_params=pltpu.CompilerParams(vmem_limit_bytes=24 * 1024 * 1024),
        cost_estimate=cost,
    )(*operands)


def in_hbm(array):
    return pltpu.with_memory_space_constraint(array, pltpu.HBM)


def held_edges(source):
    members, height, width = source.shape
    edges = (members * EDGE // LANES, height, LANES)
    vmem = pl.BlockSpec(memory_space=pltpu.VMEM)
    return pl.pallas_call(
        edges_kernel,
        out_shape=[pltpu.VMEM(source.shape, F32), pltpu.VMEM(edges, F32), pltpu.VMEM(edges, F32)],
        in_specs=[pl.BlockSpec(memory_space=pltpu.HBM)],
        out_specs=[vmem] * 3,
        scratch_shapes=[pltpu.SemaphoreType.DMA],
        compiler_params=pltpu.CompilerParams(vmem_limit_bytes=24 * 1024 * 1024),
    )(in_hbm(source))


def first_increment(source, after, members_data):
    members, levels, height, width = members_data.shape
    groups = members * EDGE // LANES
    vmem = pl.BlockSpec(memory_space=pltpu.VMEM)
    return pl.pallas_call(
        first_kernel,
        out_shape=[
            pltpu.VMEM((levels * height + 8, width), F32),
            pltpu.VMEM(members_data.shape, members_data.dtype),
            pltpu.VMEM((2, groups, levels, height, LANES), F32),
            pltpu.VMEM((2, 2, LANES, LANES), BF16),
            pltpu.VMEM((2, groups * height, groups * height), BF16),
        ],
        in_specs=[vmem, vmem, pl.BlockSpec(memory_space=pltpu.HBM)],
        out_specs=[vmem] * 5,
        scratch_shapes=[pltpu.SemaphoreType.DMA],
        compiler_params=pltpu.CompilerParams(vmem_limit_bytes=24 * 1024 * 1024),
        cost_estimate=pl.CostEstimate(flops=10**8, bytes_accessed=4 * 10**6, transcendentals=0),
    )(source, after, in_hbm(members_data))


def fetched(after, *arrays):
    vmem = pl.BlockSpec(memory_space=pltpu.VMEM)
    hbm = pl.BlockSpec(memory_space=pltpu.HBM)
    size = sum(a.size * a.dtype.itemsize for a in arrays)
    return pl.pallas_call(
        fetch_kernel,
        out_shape=[pltpu.VMEM(a.shape, a.dtype) for a in arrays],
        in_specs=[vmem] + [hbm] * len(arrays),
        out_specs=[vmem] * len(arrays),
        scratch_shapes=[pltpu.SemaphoreType.DMA((len(arrays),))],
        compiler_params=pltpu.CompilerParams(vmem_limit_bytes=24 * 1024 * 1024),
        cost_estimate=pl.CostEstimate(flops=0, bytes_accessed=2 * size, transcendentals=0),
    )(after, *map(in_hbm, arrays))


def combined(norms, source, first, second):
    vmem = pl.BlockSpec(memory_space=pltpu.VMEM)
    hbm = pl.BlockSpec(memory_space=pltpu.HBM)
    return pl.pallas_call(
        combine_kernel,
        out_shape=[jax.ShapeDtypeStruct(source.shape, F32)] * 2,
        in_specs=[vmem] * 4,
        out_specs=[hbm] * 2,
        scratch_shapes=[pltpu.VMEM(source.shape, F32)] * 2 + [pltpu.SemaphoreType.DMA((2, 4))],
        compiler_params=pltpu.CompilerParams(vmem_limit_bytes=24 * 1024 * 1024),
    )(norms, source, first, second)


def from_both_sides(to_next, to_previous, axis):
    count = lax.axis_size(axis)
    left = lax.ppermute(to_next, axis, [(i, (i + 1) % count) for i in range(count)])
    right = lax.ppermute(to_previous, axis, [((i + 1) % count, i) for i in range(count)])
    return left, right


def from_core(value):
    count = lax.axis_size("tile")
    return lax.ppermute(value, "tile", [(i, i ^ 1) for i in range(count)])


def from_chip(value):
    count = lax.axis_size("tile")
    return lax.ppermute(value, "tile", [(i, (i + 1) % count if i % 2 else (i - 1) % count) for i in range(count)])


def from_all(value, axis):
    count = lax.axis_size(axis)
    return [value] + [lax.ppermute(value, axis, [(i, i ^ k) for i in range(count)]) for k in range(1, count)]


def total_over_tiles(chip_sums):
    count = lax.axis_size("tile")
    step = 2
    while step < count:
        chip_sums = chip_sums + lax.ppermute(chip_sums, "tile", [(i, i ^ step) for i in range(count)])
        step *= 2
    return chip_sums


def one_tile_row(right_side, perturbations, precision, covered):
    source, members_data = right_side[0], perturbations[0]
    members, levels, height, width = members_data.shape
    groups = members * EDGE // LANES
    taps = taps_np()
    twice = np.convolve(taps, taps)
    field = (members, height, width)
    edges = (groups, height, LANES)
    plane = (levels, height, width)
    flat = (levels * height, width)
    row = halves(row_matrix(taps, height, members, 1))
    own = np.arange(width)

    source, to_core, to_chip = held_edges(source)
    core, chip = from_core(to_core), from_chip(to_chip)
    inside, members_data, edge_members, edge, thin = first_increment(source, to_core, members_data)
    (increment,) = call(edge_kernel, [inside.shape], inside, core, chip, edge_members, edge, thin)
    parts = from_all(increment, "mem")
    precision, covered, column, row, column_twice, row_twice, edge, thin = fetched(
        increment, precision[0], covered[0], halves(column_matrix(taps, width, EDGE)), row,
        halves(band(twice, own, own)), halves(row_matrix(taps, height, members, 2)),
        edge_matrix(twice, EDGE), halves(row_matrix(taps, height, groups, 2)),
    )
    back, to_core, to_chip, obs_weight, weighted, sums = call(
        adjoint_kernel, [field, edges, edges, plane, plane, (2, 8, LANES)], *parts, precision, covered, members_data
    )
    core, chip = from_core(to_core), from_chip(to_chip)
    (inside,) = call(second_kernel, [plane], back, column_twice, row_twice, members_data)
    inside = inside.reshape(flat)
    (increment,) = call(edge_kernel, [flat], inside, core, chip, edge_members, edge, thin)
    parts = from_all(increment, "mem")
    core, chip = (x.reshape(groups * height, LANES) for x in (core, chip))
    (first,) = call(filter_kernel, [field], back, core, chip, column, row)
    back, to_core, to_chip = call(
        last_kernel,
        [field, (groups * height + 8, LANES), (groups * height, LANES)],
        *parts, obs_weight, weighted, sums, members_data,
    )
    core, chip = from_core(to_core), from_chip(to_chip)
    norms = total_over_tiles(to_core[groups * height :] + core[groups * height :])
    (second,) = call(filter_kernel, [field], back, core, chip, column, row)
    weights, residual = combined(norms, source, first, second)
    return weights[None], residual[None]


def passed_along(value, axis, steps):
    count = lax.axis_size(axis)
    first, last = (max(0, -steps), min(count, count - steps))
    return lax.ppermute(value, axis, [(source, source + steps) for source in range(first, last)])


def smooth(field):
    taps = taps_np().astype(np.float32)
    height, width = field.shape[1:]
    above = passed_along(field[:, height - REACH :, :], "tile", TCOLS)
    below = passed_along(field[:, :REACH, :], "tile", -TCOLS)
    padded = jnp.concatenate([above, field, below], axis=1)
    along = sum(taps[j] * padded[:, j : j + height, :] for j in range(2 * REACH + 1))
    left, right = from_both_sides(along[:, :, width - REACH :], along[:, :, :REACH], "tile")
    sided = jnp.concatenate([left, along, right], axis=2)
    return sum(taps[j] * sided[:, :, j : j + width] for j in range(2 * REACH + 1))


def several_tile_rows(right_side, perturbations, precision, covered):
    source = right_side[0]
    members_data = perturbations[0].astype(F32)
    levels, height, width = precision.shape[1:]
    rows, blocks = covered.shape[1:]
    mask = covered[0].astype(F32)
    obs_weight = (
        precision[0].reshape(levels, rows, height // rows, blocks, width // blocks) * mask[None, :, None, :, None]
    ).reshape(levels, height, width)

    def operator(direction):
        partial_terms = jnp.einsum("kvyx,kyx->vyx", members_data, smooth(direction))
        weighted = obs_weight * lax.psum(partial_terms, "mem")
        return direction + smooth(jnp.einsum("kvyx,vyx->kyx", members_data, weighted))

    weights = jnp.zeros_like(source)
    residual = direction = source
    norm_now = lax.psum(jnp.sum(source * source), ("tile", "mem"))
    for step in range(ITERS):
        image = operator(direction)
        length = norm_now / lax.psum(jnp.sum(direction * image), ("tile", "mem"))
        weights = weights + length * direction
        residual = residual - length * image
        if step + 1 < ITERS:
            norm_next = lax.psum(jnp.sum(residual * residual), ("tile", "mem"))
            direction = residual + norm_next / norm_now * direction
            norm_now = norm_next
    return weights[None], residual[None]


def solution(mesh):
    single = mesh.shape["tile"] == TCOLS and mesh.shape["mem"] == 4
    local = one_tile_row if single else several_tile_rows
    return jax.shard_map(
        local,
        mesh=mesh,
        in_specs=(
            P("tile", "mem", None, None),
            P("tile", "mem", None, None, None),
            P("tile", None, None, None),
            P("tile", None, None),
        ),
        out_specs=(P("tile", "mem", None, None), P("tile", "mem", None, None)),
        check_vma=False,
    )
```

```python
import functools

import jax
import jax.numpy as jnp
import ml_dtypes
import numpy as np
from jax import lax
from jax.experimental import pallas as pl
from jax.experimental.pallas import tpu as pltpu
from jax.sharding import PartitionSpec as P

ITERS = 2
TCOLS = 8
REACH = 8
EDGE = 2 * REACH
LANES = 128
F32 = jnp.float32
BF16 = jnp.bfloat16
LONG = pl.CostEstimate(flops=10**9, bytes_accessed=10**6, transcendentals=0)


def taps_np():
    offsets = np.arange(-REACH, REACH + 1, dtype=np.float64)
    raw = np.exp(-offsets * offsets / 32.0)
    return raw / np.sqrt(np.sum(np.exp(-offsets * offsets / 16.0)))


def band(taps, source, target):
    reach = (len(taps) - 1) // 2
    gap = source[:, None] - target[None, :]
    inside = np.abs(gap) <= reach
    return np.where(inside, taps[np.clip(gap + reach, 0, 2 * reach)], 0.0)


def halves(matrix):
    whole = matrix.astype(np.float32)
    high = whole.astype(ml_dtypes.bfloat16)
    low = (whole - high.astype(np.float32)).astype(ml_dtypes.bfloat16)
    return np.stack([high, low])


def column_matrix(taps, width, edge):
    target = np.arange(width)
    slots = LANES // edge
    left = np.tile(np.arange(edge) - edge, slots)
    right = np.tile(np.arange(edge) + width, slots)
    return np.concatenate([band(taps, s, target) for s in (np.arange(width), left, right)])


def row_matrix(taps, height, members, times):
    one = band(taps, np.arange(height), np.arange(height))
    return np.kron(np.eye(members), np.linalg.matrix_power(one, times))


def edge_matrix(taps, edge):
    inner = np.arange(edge)
    sides = (band(taps, inner - edge, inner), band(taps, inner + edge, inner))
    return np.stack([halves(np.kron(np.eye(LANES // edge), side)) for side in sides])


def split(x):
    high = x.astype(BF16)
    return high, (x - high.astype(F32)).astype(BF16)


def dot3(left, right):
    mul = functools.partial(jnp.dot, preferred_element_type=F32)
    return mul(left[0], right[0]) + (mul(left[1], right[0]) + mul(left[0], right[1]))


def both(ref):
    return ref[0], ref[1]


def lane_of(shape):
    return lax.broadcasted_iota(jnp.int32, shape, len(shape) - 1)


def pack_edges(field, edge, first):
    members, rows, width = field.shape
    slots = LANES // edge
    groups = members // slots
    lane = lane_of((rows, LANES))
    out = []
    for g in range(groups):
        total = jnp.zeros((rows, LANES), F32)
        for j in range(slots):
            member = field[j * groups + g]
            block = member[:, :LANES] if first else member[:, width - LANES :]
            start = 0 if first else LANES - edge
            shift = (j * edge - start) % LANES
            moved = pltpu.roll(block, shift, 1) if shift else block
            total = jnp.where((lane >= j * edge) & (lane < (j + 1) * edge), moved, total)
        out.append(total)
    return jnp.stack(out)


def edges_for_partners(field, edge):
    odd = lax.axis_index("tile") % 2 == 1
    first, last = pack_edges(field, edge, True), pack_edges(field, edge, False)
    return jnp.where(odd, first, last), jnp.where(odd, last, first)


def sides_of(core, chip):
    odd = lax.axis_index("tile") % 2 == 1
    return jnp.where(odd, core, chip), jnp.where(odd, chip, core)


def spread_edges(packed, edge):
    groups, rows, _ = packed.shape
    slots = LANES // edge
    lane = lane_of((groups, rows, LANES))
    parts = [jnp.where((lane >= j * edge) & (lane < (j + 1) * edge), packed, 0.0) for j in range(slots)]
    return jnp.concatenate(parts, axis=0).reshape(slots * groups * rows, LANES)


def beside(field, core, chip, edge):
    members, rows, width = field.shape
    left, right = sides_of(core, chip)
    return jnp.concatenate(
        [field.reshape(members * rows, width), spread_edges(left, edge), spread_edges(right, edge)], axis=1
    )


def increments(members_ref, smoothed):
    members, levels = members_ref.shape[:2]
    totals = []
    for v in range(levels):
        total = members_ref[0, v].astype(F32) * smoothed[0]
        for k in range(1, members):
            total = total + members_ref[k, v].astype(F32) * smoothed[k]
        totals.append(total)
    return jnp.stack(totals)


def adjoint(members_ref, weighted):
    members, levels = members_ref.shape[:2]
    back = []
    for k in range(members):
        total = members_ref[k, 0].astype(F32) * weighted[0]
        for v in range(1, levels):
            total = total + members_ref[k, v].astype(F32) * weighted[v]
        back.append(total)
    return jnp.stack(back)


def folded(x):
    width = x.shape[-1]
    x = x.reshape(-1, 8, width).sum(axis=0)
    return sum(x[:, i : i + LANES] for i in range(0, width, LANES))


def edges_kernel(source, held, to_core, to_chip, sem):
    copy = pltpu.make_async_copy(source, held, sem)
    copy.start()
    copy.wait()
    to_core[...], to_chip[...] = edges_for_partners(held, EDGE)


def fetch_kernel(*refs):
    count = (len(refs) - 2) // 2
    copies = [pltpu.make_async_copy(refs[1 + i], refs[1 + count + i], refs[-1].at[i]) for i in range(count)]
    for copy in copies:
        copy.start()
    for copy in copies:
        copy.wait()


def own_columns(field, column, row):
    members, height, width = field.shape
    lhs = split(field[...].reshape(members * height, width))
    return dot3(both(row), split(dot3(lhs, both(column)))).reshape(field.shape)


def tap_at(gap, inside):
    scale = 1.0 / np.sqrt(np.sum(np.exp(-(np.arange(-REACH, REACH + 1.0) ** 2) / 16.0)))
    square = (gap * gap).astype(F32)
    return jnp.where(inside & (jnp.abs(gap) <= REACH), jnp.exp(square * (-1.0 / 32.0)) * scale, 0.0)


def gaps(rows, columns):
    shape = (rows, columns)
    down, across = (lax.broadcasted_iota(jnp.int32, shape, i) for i in range(2))
    return down, across, down - across


def kept(ref, matrix):
    ref[0], ref[1] = split(matrix)


def first_kernel(source, after, members_hbm, increment, members_ref, edge_members, edge, thin, sem):
    copy = pltpu.make_async_copy(members_hbm, members_ref, sem)
    copy.start()
    members, levels, height, width = members_ref.shape
    _, _, gap = gaps(width, width)
    column = split(tap_at(gap, True))
    down, across, gap = gaps(members * height, members * height)
    row = split(tap_at(gap, down // height == across // height))
    lhs = split(source[...].reshape(members * height, width))
    smoothed = dot3(row, split(dot3(lhs, column))).reshape(source.shape)
    increment[levels * height :] = (source[...] * source[...]).reshape(-1, 8, width).sum(axis=0)
    down, across, gap = gaps(LANES, LANES)
    same = down // EDGE == across // EDGE
    kept(edge.at[0], tap_at(gap - EDGE, same))
    kept(edge.at[1], tap_at(gap + EDGE, same))
    down, across, gap = gaps(*thin.shape[1:])
    kept(thin, tap_at(gap, down // height == across // height))
    copy.wait()
    increment[: levels * height] = increments(members_ref, smoothed).reshape(levels * height, width)
    for v in range(levels):
        level = members_ref[:, v].astype(F32)
        edge_members[0, :, v] = pack_edges(level, EDGE, True)
        edge_members[1, :, v] = pack_edges(level, EDGE, False)


def second_kernel(back, column, row, members_ref, increment):
    increment[...] = increments(members_ref, own_columns(back, column, row))


def edge_kernel(inside, core, chip, edge_members, edge, thin, out):
    groups, height, _ = core.shape
    levels = edge_members.shape[2]
    width = out.shape[-1]
    halo = jnp.concatenate([side.reshape(groups * height, LANES) for side in sides_of(core[...], chip[...])], axis=1)
    halo = dot3(both(thin), split(halo))
    lane = lane_of((levels, height, LANES))
    out[...] = inside[...]
    for side in range(2):
        part = halo[:, :LANES] if side == 0 else halo[:, LANES:]
        part = dot3(split(part), (edge[side, 0], edge[side, 1])).reshape(groups, 1, height, LANES)
        total = jnp.sum(edge_members[side] * part, axis=0).reshape(levels * height, LANES)
        step = EDGE
        while step < LANES:
            total = total + pltpu.roll(total, step, 1)
            step *= 2
        total = total.reshape(levels, height, LANES)
        if side == 0:
            span, mask = pl.ds(0, LANES), lane < EDGE
        else:
            span, mask = pl.ds(width - LANES, LANES), lane >= LANES - EDGE
        rows = pl.ds(0, levels * height)
        out[rows, span] = out[rows, span] + jnp.where(mask, total, 0.0).reshape(levels * height, LANES)


def weight_of(precision, covered):
    levels, height, width = precision.shape
    rows, blocks = covered.shape
    spread = lax.broadcasted_iota(jnp.int32, (blocks, width), 1) // (width // blocks)
    spread = (spread == lax.broadcasted_iota(jnp.int32, (blocks, width), 0)).astype(BF16)
    mask = jnp.dot(covered[...].astype(F32).astype(BF16), spread, preferred_element_type=F32)
    tall = height // rows
    mask = jnp.concatenate([jnp.broadcast_to(mask[i : i + 1], (tall, width)) for i in range(rows)], axis=0)
    return precision[...] * mask


def adjoint_kernel(
    i0, i1, i2, i3, precision, covered, members_ref, back, to_core, to_chip, obs_weight, weighted, sums
):
    levels, height, width = precision.shape
    total = (i0[...] + i1[...]) + (i2[...] + i3[...])
    increment = total[: levels * height].reshape(levels, height, width)
    obs_weight[...] = weight_of(precision, covered)
    weighted[...] = obs_weight[...] * increment
    sums[0] = folded(total[levels * height :])
    sums[1] = folded(weighted[...] * increment)
    back[...] = adjoint(members_ref, weighted)
    to_core[...], to_chip[...] = edges_for_partners(back, EDGE)


def filter_kernel(back, core, chip, column, row, out):
    groups, height = back.shape[0] * EDGE // LANES, back.shape[1]
    core, chip = (x[: groups * height].reshape(groups, height, LANES) for x in (core, chip))
    lhs = split(beside(back[...], core, chip, EDGE))
    out[...] = dot3(both(row), split(dot3(lhs, both(column)))).reshape(out.shape)


def last_kernel(i0, i1, i2, i3, obs_weight, before, sums, members_ref, back, to_core, to_chip):
    levels, height, width = obs_weight.shape
    increment = ((i0[...] + i1[...]) + (i2[...] + i3[...])).reshape(obs_weight.shape)
    weighted = obs_weight[...] * increment
    four = [sums[0], sums[1], folded(before[...] * increment), folded(weighted * increment)]
    row = lax.broadcasted_iota(jnp.int32, (8, LANES), 0)
    stacked = jnp.zeros((8, LANES), F32)
    for i, part in enumerate(four):
        stacked = jnp.where(row == i, jnp.sum(part, axis=0, keepdims=True), stacked)
    back[...] = adjoint(members_ref, weighted)
    odd = lax.axis_index("tile") % 2 == 1
    first, last = pack_edges(back, EDGE, True), pack_edges(back, EDGE, False)
    rows = first.shape[0] * height
    to_core[:rows] = jnp.where(odd, first, last).reshape(rows, LANES)
    to_core[rows:] = stacked
    to_chip[...] = jnp.where(odd, last, first).reshape(rows, LANES)


def copy_kernel(value, after, out):
    out[...] = value[...]


def combine_kernel(own, other, source, first, second, weights, residual, held_weights, held_residual, sems):
    total = jnp.sum(own[...] + other[...], axis=1, keepdims=True)
    bb, bg, gg, gh = (total[i : i + 1] for i in range(4))
    bg, gg, gh = bg / bb, gg / bb, gh / bb
    q = 1.0 / (1.0 + bg)
    p = bg * q
    ratio = (gg - bg * bg) * q * q
    d = p + ratio
    square = d * d - 2.0 * d * q * bg + q * q * gg
    image = d * d * bg - 2.0 * d * q * gg + q * q * gh
    step = ratio / (square + image)
    members = source.shape[0]
    pieces = sems.shape[1]
    copies = []
    for i in range(pieces):
        part = pl.ds(i * (members // pieces), members // pieces)
        b, g, h = source[part], first[part], second[part]
        held_weights[part] = (q + step * d) * b - (step * q) * g
        held_residual[part] = (p - step * d) * b + (step * q - q - step * d) * g + (step * q) * h
        for k, (held, out) in enumerate(((held_weights, weights), (held_residual, residual))):
            copies.append(pltpu.make_async_copy(held.at[part], out.at[part], sems.at[k, i]))
            copies[-1].start()
    for copy in copies:
        copy.wait()


def call(kernel, outs, *operands, cost=None):
    shapes = [jax.ShapeDtypeStruct(shape, F32) for shape in outs]
    vmem = pl.BlockSpec(memory_space=pltpu.VMEM)
    return pl.pallas_call(
        kernel,
        out_shape=shapes,
        in_specs=[vmem] * len(operands),
        out_specs=[vmem] * len(outs),
        compiler_params=pltpu.CompilerParams(vmem_limit_bytes=24 * 1024 * 1024),
        cost_estimate=cost,
    )(*operands)


def in_hbm(array):
    return pltpu.with_memory_space_constraint(array, pltpu.HBM)


def held_edges(source):
    members, height, width = source.shape
    edges = (members * EDGE // LANES, height, LANES)
    vmem = pl.BlockSpec(memory_space=pltpu.VMEM)
    return pl.pallas_call(
        edges_kernel,
        out_shape=[pltpu.VMEM(source.shape, F32), pltpu.VMEM(edges, F32), pltpu.VMEM(edges, F32)],
        in_specs=[pl.BlockSpec(memory_space=pltpu.HBM)],
        out_specs=[vmem] * 3,
        scratch_shapes=[pltpu.SemaphoreType.DMA],
        compiler_params=pltpu.CompilerParams(vmem_limit_bytes=24 * 1024 * 1024),
    )(in_hbm(source))


def first_increment(source, after, members_data):
    members, levels, height, width = members_data.shape
    groups = members * EDGE // LANES
    vmem = pl.BlockSpec(memory_space=pltpu.VMEM)
    return pl.pallas_call(
        first_kernel,
        out_shape=[
            pltpu.VMEM((levels * height + 8, width), F32),
            pltpu.VMEM(members_data.shape, members_data.dtype),
            pltpu.VMEM((2, groups, levels, height, LANES), F32),
            pltpu.VMEM((2, 2, LANES, LANES), BF16),
            pltpu.VMEM((2, groups * height, groups * height), BF16),
        ],
        in_specs=[vmem, vmem, pl.BlockSpec(memory_space=pltpu.HBM)],
        out_specs=[vmem] * 5,
        scratch_shapes=[pltpu.SemaphoreType.DMA],
        compiler_params=pltpu.CompilerParams(vmem_limit_bytes=24 * 1024 * 1024),
        cost_estimate=pl.CostEstimate(flops=10**8, bytes_accessed=4 * 10**6, transcendentals=0),
    )(source, after, in_hbm(members_data))


def fetched(after, *arrays):
    vmem = pl.BlockSpec(memory_space=pltpu.VMEM)
    hbm = pl.BlockSpec(memory_space=pltpu.HBM)
    size = sum(a.size * a.dtype.itemsize for a in arrays)
    return pl.pallas_call(
        fetch_kernel,
        out_shape=[pltpu.VMEM(a.shape, a.dtype) for a in arrays],
        in_specs=[vmem] + [hbm] * len(arrays),
        out_specs=[vmem] * len(arrays),
        scratch_shapes=[pltpu.SemaphoreType.DMA((len(arrays),))],
        compiler_params=pltpu.CompilerParams(vmem_limit_bytes=24 * 1024 * 1024),
        cost_estimate=pl.CostEstimate(flops=0, bytes_accessed=2 * size, transcendentals=0),
    )(after, *map(in_hbm, arrays))


def combined(own, other, source, first, second):
    vmem = pl.BlockSpec(memory_space=pltpu.VMEM)
    hbm = pl.BlockSpec(memory_space=pltpu.HBM)
    return pl.pallas_call(
        combine_kernel,
        out_shape=[jax.ShapeDtypeStruct(source.shape, F32)] * 2,
        in_specs=[vmem] * 5,
        out_specs=[hbm] * 2,
        scratch_shapes=[pltpu.VMEM(source.shape, F32)] * 2 + [pltpu.SemaphoreType.DMA((2, 4))],
        compiler_params=pltpu.CompilerParams(vmem_limit_bytes=24 * 1024 * 1024),
    )(own, other, source, first, second)


def from_both_sides(to_next, to_previous, axis):
    count = lax.axis_size(axis)
    left = lax.ppermute(to_next, axis, [(i, (i + 1) % count) for i in range(count)])
    right = lax.ppermute(to_previous, axis, [((i + 1) % count, i) for i in range(count)])
    return left, right


def from_tile(value, bit):
    count = lax.axis_size("tile")
    return lax.ppermute(value, "tile", [(i, i ^ bit) for i in range(count)])


def from_core(value):
    return from_tile(value, 1)


def from_chip(value):
    count = lax.axis_size("tile")
    return lax.ppermute(value, "tile", [(i, (i + 1) % count if i % 2 else (i - 1) % count) for i in range(count)])


def from_all(value, axis):
    count = lax.axis_size(axis)
    return [value] + [lax.ppermute(value, axis, [(i, i ^ k) for i in range(count)]) for k in range(1, count)]


def one_tile_row(right_side, perturbations, precision, covered):
    source, members_data = right_side[0], perturbations[0]
    members, levels, height, width = members_data.shape
    groups = members * EDGE // LANES
    taps = taps_np()
    twice = np.convolve(taps, taps)
    field = (members, height, width)
    edges = (groups, height, LANES)
    plane = (levels, height, width)
    flat = (levels * height, width)
    row = halves(row_matrix(taps, height, members, 1))
    own = np.arange(width)

    source, to_core, to_chip = held_edges(source)
    core, chip = from_core(to_core), from_chip(to_chip)
    inside, members_data, edge_members, edge, thin = first_increment(source, to_core, members_data)
    (increment,) = call(edge_kernel, [inside.shape], inside, core, chip, edge_members, edge, thin)
    parts = from_all(increment, "mem")
    precision, covered, column, row, column_twice, row_twice, edge, thin = fetched(
        increment, precision[0], covered[0], halves(column_matrix(taps, width, EDGE)), row,
        halves(band(twice, own, own)), halves(row_matrix(taps, height, members, 2)),
        edge_matrix(twice, EDGE), halves(row_matrix(taps, height, groups, 2)),
    )
    back, to_core, to_chip, obs_weight, weighted, sums = call(
        adjoint_kernel, [field, edges, edges, plane, plane, (2, 8, LANES)], *parts, precision, covered, members_data
    )
    core, chip = from_core(to_core), from_chip(to_chip)
    (inside,) = call(second_kernel, [plane], back, column_twice, row_twice, members_data)
    inside = inside.reshape(flat)
    (increment,) = call(edge_kernel, [flat], inside, core, chip, edge_members, edge, thin)
    parts = from_all(increment, "mem")
    core, chip = (x.reshape(groups * height, LANES) for x in (core, chip))
    (first,) = call(filter_kernel, [field], back, core, chip, column, row, cost=LONG)
    back, to_core, to_chip = call(
        last_kernel,
        [field, (groups * height + 8, LANES), (groups * height, LANES)],
        *parts, obs_weight, weighted, sums, members_data,
    )
    core = from_core(to_core)
    sums = to_core[groups * height :] + core[groups * height :]
    (to_chip,) = call(copy_kernel, [to_chip.shape], to_chip, sums)
    chip = from_chip(to_chip)
    sums = sums + from_tile(sums, 2)
    others = from_tile(sums, 4)
    (second,) = call(filter_kernel, [field], back, core, chip, column, row, cost=LONG)
    weights, residual = combined(sums, others, source, first, second)
    return weights[None], residual[None]


def passed_along(value, axis, steps):
    count = lax.axis_size(axis)
    first, last = (max(0, -steps), min(count, count - steps))
    return lax.ppermute(value, axis, [(source, source + steps) for source in range(first, last)])


def smooth(field):
    taps = taps_np().astype(np.float32)
    height, width = field.shape[1:]
    above = passed_along(field[:, height - REACH :, :], "tile", TCOLS)
    below = passed_along(field[:, :REACH, :], "tile", -TCOLS)
    padded = jnp.concatenate([above, field, below], axis=1)
    along = sum(taps[j] * padded[:, j : j + height, :] for j in range(2 * REACH + 1))
    left, right = from_both_sides(along[:, :, width - REACH :], along[:, :, :REACH], "tile")
    sided = jnp.concatenate([left, along, right], axis=2)
    return sum(taps[j] * sided[:, :, j : j + width] for j in range(2 * REACH + 1))


def several_tile_rows(right_side, perturbations, precision, covered):
    source = right_side[0]
    members_data = perturbations[0].astype(F32)
    levels, height, width = precision.shape[1:]
    rows, blocks = covered.shape[1:]
    mask = covered[0].astype(F32)
    obs_weight = (
        precision[0].reshape(levels, rows, height // rows, blocks, width // blocks) * mask[None, :, None, :, None]
    ).reshape(levels, height, width)

    def operator(direction):
        partial_terms = jnp.einsum("kvyx,kyx->vyx", members_data, smooth(direction))
        weighted = obs_weight * lax.psum(partial_terms, "mem")
        return direction + smooth(jnp.einsum("kvyx,vyx->kyx", members_data, weighted))

    weights = jnp.zeros_like(source)
    residual = direction = source
    norm_now = lax.psum(jnp.sum(source * source), ("tile", "mem"))
    for step in range(ITERS):
        image = operator(direction)
        length = norm_now / lax.psum(jnp.sum(direction * image), ("tile", "mem"))
        weights = weights + length * direction
        residual = residual - length * image
        if step + 1 < ITERS:
            norm_next = lax.psum(jnp.sum(residual * residual), ("tile", "mem"))
            direction = residual + norm_next / norm_now * direction
            norm_now = norm_next
    return weights[None], residual[None]


def solution(mesh):
    single = mesh.shape["tile"] == TCOLS and mesh.shape["mem"] == 4
    local = one_tile_row if single else several_tile_rows
    return jax.shard_map(
        local,
        mesh=mesh,
        in_specs=(
            P("tile", "mem", None, None),
            P("tile", "mem", None, None, None),
            P("tile", None, None, None),
            P("tile", None, None),
        ),
        out_specs=(P("tile", "mem", None, None), P("tile", "mem", None, None)),
        check_vma=False,
    )
```

```python
import functools

import jax
import jax.numpy as jnp
import ml_dtypes
import numpy as np
from jax import lax
from jax.experimental import pallas as pl
from jax.experimental.pallas import tpu as pltpu
from jax.sharding import PartitionSpec as P

ITERS = 2
TCOLS = 8
REACH = 8
EDGE = 2 * REACH
LANES = 128
F32 = jnp.float32
BF16 = jnp.bfloat16
LONG = pl.CostEstimate(flops=10**9, bytes_accessed=10**6, transcendentals=0)


def taps_np():
    offsets = np.arange(-REACH, REACH + 1, dtype=np.float64)
    raw = np.exp(-offsets * offsets / 32.0)
    return raw / np.sqrt(np.sum(np.exp(-offsets * offsets / 16.0)))


def band(taps, source, target):
    reach = (len(taps) - 1) // 2
    gap = source[:, None] - target[None, :]
    inside = np.abs(gap) <= reach
    return np.where(inside, taps[np.clip(gap + reach, 0, 2 * reach)], 0.0)


def halves(matrix):
    whole = matrix.astype(np.float32)
    high = whole.astype(ml_dtypes.bfloat16)
    low = (whole - high.astype(np.float32)).astype(ml_dtypes.bfloat16)
    return np.stack([high, low])


def column_matrix(taps, width, edge):
    target = np.arange(width)
    slots = LANES // edge
    left = np.tile(np.arange(edge) - edge, slots)
    right = np.tile(np.arange(edge) + width, slots)
    return np.concatenate([band(taps, s, target) for s in (np.arange(width), left, right)])


def row_matrix(taps, height, members, times):
    one = band(taps, np.arange(height), np.arange(height))
    return np.kron(np.eye(members), np.linalg.matrix_power(one, times))


def edge_matrix(taps, edge):
    inner = np.arange(edge)
    sides = (band(taps, inner - edge, inner), band(taps, inner + edge, inner))
    return np.stack([halves(np.kron(np.eye(LANES // edge), side)) for side in sides])


def split(x):
    high = x.astype(BF16)
    return high, (x - high.astype(F32)).astype(BF16)


def dot3(left, right):
    mul = functools.partial(jnp.dot, preferred_element_type=F32)
    return mul(left[0], right[0]) + (mul(left[1], right[0]) + mul(left[0], right[1]))


def both(ref):
    return ref[0], ref[1]


def lane_of(shape):
    return lax.broadcasted_iota(jnp.int32, shape, len(shape) - 1)


def pack_columns(field, start, edge):
    members, rows, _ = field.shape
    slots = LANES // edge
    groups = members // slots
    lane = lane_of((rows, LANES))
    origin = start // LANES * LANES
    out = []
    for g in range(groups):
        total = jnp.zeros((rows, LANES), F32)
        for j in range(slots):
            block = field[j * groups + g][:, origin : origin + LANES]
            shift = (j * edge - (start - origin)) % LANES
            moved = pltpu.roll(block, shift, 1) if shift else block
            total = jnp.where((lane >= j * edge) & (lane < (j + 1) * edge), moved, total)
        out.append(total)
    return jnp.stack(out)


def pack_edges(field, edge, first):
    return pack_columns(field, 0 if first else field.shape[-1] - edge, edge)


def repeated(x, period):
    while period < LANES:
        x = x + pltpu.roll(x, period, len(x.shape) - 1)
        period *= 2
    return x


def level_lanes(shape, level):
    lane = lane_of(shape)
    return (lane >= level * EDGE) & (lane < (level + 1) * EDGE)


def sides_of(core, chip):
    odd = lax.axis_index("tile") % 2 == 1
    return jnp.where(odd, core, chip), jnp.where(odd, chip, core)


def spread_edges(packed, edge):
    groups, rows, _ = packed.shape
    slots = LANES // edge
    lane = lane_of((groups, rows, LANES))
    parts = [jnp.where((lane >= j * edge) & (lane < (j + 1) * edge), packed, 0.0) for j in range(slots)]
    return jnp.concatenate(parts, axis=0).reshape(slots * groups * rows, LANES)


def beside(field, left, right, edge):
    members, rows, width = field.shape
    return jnp.concatenate(
        [field.reshape(members * rows, width), spread_edges(left, edge), spread_edges(right, edge)], axis=1
    )


def increments(members_ref, smoothed):
    members, levels = members_ref.shape[:2]
    totals = []
    for v in range(levels):
        total = members_ref[0, v].astype(F32) * smoothed[0]
        for k in range(1, members):
            total = total + members_ref[k, v].astype(F32) * smoothed[k]
        totals.append(total)
    return jnp.stack(totals)


def adjoint(members_ref, weighted):
    members, levels = members_ref.shape[:2]
    back = []
    for k in range(members):
        total = members_ref[k, 0].astype(F32) * weighted[0]
        for v in range(1, levels):
            total = total + members_ref[k, v].astype(F32) * weighted[v]
        back.append(total)
    return jnp.stack(back)


def folded(x):
    width = x.shape[-1]
    x = x.reshape(-1, 8, width).sum(axis=0)
    return sum(x[:, i : i + LANES] for i in range(0, width, LANES))


def edges_kernel(
    source_hbm, members_hbm, precision_hbm, covered_hbm,
    source, members_ref, obs_weight, near, edge_members, to_core, to_chip, precision, covered, sems,
):
    pairs = ((source_hbm, source), (precision_hbm, precision), (covered_hbm, covered), (members_hbm, members_ref))
    copies = [pltpu.make_async_copy(x, y, sems.at[i]) for i, (x, y) in enumerate(pairs)]
    for copy in copies:
        copy.start()
    members, levels, height, width = members_ref.shape
    groups = members * EDGE // LANES
    odd = lax.axis_index("tile") % 2 == 1
    rows = groups * height

    def send(at, first, last):
        first, last = (x.reshape(-1, LANES) for x in (first, last))
        part = pl.ds(at, first.shape[0])
        to_core[part] = jnp.where(odd, first, last)
        to_chip[part] = jnp.where(odd, last, first)

    copies[0].wait()
    near[0], near[1] = pack_columns(source, 0, EDGE), pack_columns(source, width - EDGE, EDGE)
    send(0, near[0], near[1])
    send(rows, pack_columns(source, EDGE, EDGE), pack_columns(source, width - 2 * EDGE, EDGE))
    copies[1].wait()
    copies[2].wait()
    obs_weight[...] = weight_of(precision, covered)
    sides = []
    for start in (0, width - EDGE):
        total = jnp.zeros((height, LANES), F32)
        for v in range(levels):
            origin = start // LANES * LANES
            shift = (v * EDGE - (start - origin)) % LANES
            block = obs_weight[v, :, origin : origin + LANES]
            total = jnp.where(level_lanes(total.shape, v), pltpu.roll(block, shift, 1) if shift else block, total)
        sides.append(total)
    send(rows * (2 + levels), *sides)
    copies[3].wait()
    for v in range(levels):
        level = members_ref[:, v].astype(F32)
        edge_members[0, v], edge_members[1, v] = pack_edges(level, EDGE, True), pack_edges(level, EDGE, False)
        send(rows * (2 + v), edge_members[0, v], edge_members[1, v])


def fetch_kernel(*refs):
    count = (len(refs) - 2) // 2
    copies = [pltpu.make_async_copy(refs[1 + i], refs[1 + count + i], refs[-1].at[i]) for i in range(count)]
    for copy in copies:
        copy.start()
    for copy in copies:
        copy.wait()


def own_columns(field, column, row):
    members, height, width = field.shape
    lhs = split(field[...].reshape(members * height, width))
    return dot3(both(row), split(dot3(lhs, both(column)))).reshape(field.shape)


def tap_at(gap, inside):
    scale = 1.0 / np.sqrt(np.sum(np.exp(-(np.arange(-REACH, REACH + 1.0) ** 2) / 16.0)))
    square = (gap * gap).astype(F32)
    return jnp.where(inside & (jnp.abs(gap) <= REACH), jnp.exp(square * (-1.0 / 32.0)) * scale, 0.0)


def gaps(rows, columns):
    shape = (rows, columns)
    down, across = (lax.broadcasted_iota(jnp.int32, shape, i) for i in range(2))
    return down, across, down - across


def kept(ref, matrix):
    ref[0], ref[1] = split(matrix)


def first_kernel(source, after, members_ref, increment, edge, thin):
    members, levels, height, width = members_ref.shape
    _, _, gap = gaps(width, width)
    column = split(tap_at(gap, True))
    down, across, gap = gaps(members * height, members * height)
    row = split(tap_at(gap, down // height == across // height))
    lhs = split(source[...].reshape(members * height, width))
    smoothed = dot3(row, split(dot3(lhs, column))).reshape(source.shape)
    increment[levels * height :] = (source[...] * source[...]).reshape(-1, 8, width).sum(axis=0)
    increment[: levels * height] = increments(members_ref, smoothed).reshape(levels * height, width)
    down, across, gap = gaps(LANES, LANES)
    same = down // EDGE == across // EDGE
    for i in range(3):
        kept(edge.at[i], tap_at(gap + (i - 1) * EDGE, same))
    down, across, gap = gaps(*thin.shape[1:])
    kept(thin, tap_at(gap, down // height == across // height))


def edge_sums(edge_members, smoothed):
    groups, height = edge_members.shape[1:3]
    return repeated(jnp.sum(edge_members * smoothed.reshape(1, groups, height, LANES), axis=1), EDGE)


def add_edges(out, sums, side):
    levels, height, _ = sums.shape
    width = out.shape[-1]
    lane = lane_of(sums.shape)
    if side == 0:
        span, mask = pl.ds(0, LANES), lane < EDGE
    else:
        span, mask = pl.ds(width - LANES, LANES), lane >= LANES - EDGE
    rows = pl.ds(0, levels * height)
    out[rows, span] = out[rows, span] + jnp.where(mask, sums, 0.0).reshape(levels * height, LANES)


def halo_members(block, rows, groups, levels):
    height = rows // groups
    return block[2 * rows : (2 + levels) * rows].reshape(levels, groups, height, LANES)


def edge_kernel(inside, core, chip, near, edge_members, edge, thin, out):
    levels, groups, height = edge_members.shape[1:4]
    width = out.shape[-1]
    rows = groups * height
    out[: inside.shape[0]] = inside[...]
    sides = sides_of(core[...], chip[...])
    parts = []
    for side, block in enumerate(sides):
        parts += [block[rows : 2 * rows], block[:rows], near[side].reshape(rows, LANES)]
    filtered = split(dot3(both(thin), split(jnp.concatenate(parts, axis=1))))
    outer = []
    for side, block in enumerate(sides):
        span = slice(3 * side * LANES, 3 * (side + 1) * LANES)
        order = (0, 1, 2) if side == 0 else (2, 1, 0)
        matrix = [jnp.concatenate([edge[i, k] for i in order], axis=0) for k in range(2)]
        beyond = dot3(tuple(x[:, span] for x in filtered), matrix)
        middle = slice(span.start + LANES, span.start + 2 * LANES)
        within = dot3(tuple(x[:, middle] for x in filtered), both(edge.at[order[0]]))
        add_edges(out, edge_sums(edge_members[side], within), side)
        sums = edge_sums(halo_members(block, rows, groups, levels), beyond)
        total = jnp.zeros((height, LANES), F32)
        for v in range(levels):
            total = jnp.where(level_lanes(total.shape, v), sums[v], total)
        outer.append(total)
    out[inside.shape[0] :] = jnp.concatenate(outer, axis=1)


def weight_of(precision, covered):
    levels, height, width = precision.shape
    rows, blocks = covered.shape
    spread = lax.broadcasted_iota(jnp.int32, (blocks, width), 1) // (width // blocks)
    spread = (spread == lax.broadcasted_iota(jnp.int32, (blocks, width), 0)).astype(BF16)
    mask = jnp.dot(covered[...].astype(F32).astype(BF16), spread, preferred_element_type=F32)
    tall = height // rows
    mask = jnp.concatenate([jnp.broadcast_to(mask[i : i + 1], (tall, width)) for i in range(rows)], axis=0)
    return precision[...] * mask


def middle_kernel(
    i0, i1, i2, i3, obs_weight, core, chip, members_ref, edge_members, column, row, edge, thin,
    back, halo, weighted, sums, out,
):
    levels, height, width = obs_weight.shape
    groups = edge_members.shape[2]
    rows = groups * height
    total = (i0[...] + i1[...]) + (i2[...] + i3[...])
    flat = levels * height
    increment = total[:flat].reshape(levels, height, width)
    weighted[...] = obs_weight[...] * increment
    sums[0] = folded(total[flat : flat + 8])
    sums[1] = folded(weighted[...] * increment)
    back[...] = adjoint(members_ref, weighted)
    smoothed = own_columns(back, column, row)
    for side, block in enumerate(sides_of(core[...], chip[...])):
        outer = total[flat + 8 :, side * LANES : (side + 1) * LANES] * block[(2 + levels) * rows :]
        members = halo_members(block, rows, groups, levels)
        adjoint_here = jnp.zeros((groups, height, LANES), F32)
        for v in range(levels):
            level = repeated(jnp.where(level_lanes(outer.shape, v), outer, 0.0), EDGE)
            adjoint_here = adjoint_here + members[v] * level
        halo[side] = adjoint_here
    filtered = split(dot3(both(thin), split(jnp.concatenate([halo[i].reshape(rows, LANES) for i in range(2)], axis=1))))
    out[...] = increments(members_ref, smoothed).reshape(flat, width)
    for side in range(2):
        part = dot3(tuple(x[:, side * LANES : (side + 1) * LANES] for x in filtered), both(edge.at[side]))
        add_edges(out, edge_sums(edge_members[side], part), side)


def wide_filter_kernel(back, halo, column, row, out):
    lhs = split(beside(back[...], halo[0], halo[1], EDGE))
    out[...] = dot3(both(row), split(dot3(lhs, both(column)))).reshape(out.shape)


def filter_kernel(back, core, chip, column, row, out):
    groups, height = back.shape[0] * EDGE // LANES, back.shape[1]
    left, right = sides_of(*(x[: groups * height].reshape(groups, height, LANES) for x in (core, chip)))
    lhs = split(beside(back[...], left, right, EDGE))
    out[...] = dot3(both(row), split(dot3(lhs, both(column)))).reshape(out.shape)


def last_kernel(i0, i1, i2, i3, obs_weight, before, sums, members_ref, back, to_core, to_chip):
    levels, height, width = obs_weight.shape
    increment = ((i0[...] + i1[...]) + (i2[...] + i3[...])).reshape(obs_weight.shape)
    weighted = obs_weight[...] * increment
    four = [sums[0], sums[1], folded(before[...] * increment), folded(weighted * increment)]
    row = lax.broadcasted_iota(jnp.int32, (8, LANES), 0)
    stacked = jnp.zeros((8, LANES), F32)
    for i, part in enumerate(four):
        stacked = jnp.where(row == i, jnp.sum(part, axis=0, keepdims=True), stacked)
    back[...] = adjoint(members_ref, weighted)
    odd = lax.axis_index("tile") % 2 == 1
    first, last = pack_edges(back, EDGE, True), pack_edges(back, EDGE, False)
    rows = first.shape[0] * height
    to_core[:rows] = jnp.where(odd, first, last).reshape(rows, LANES)
    to_core[rows:] = stacked
    to_chip[...] = jnp.where(odd, last, first).reshape(rows, LANES)


def copy_kernel(value, after, out):
    out[...] = value[...]


def combine_kernel(own, other, source, first, second, weights, residual, held_weights, held_residual, sems):
    total = jnp.sum(own[...] + other[...], axis=1, keepdims=True)
    bb, bg, gg, gh = (total[i : i + 1] for i in range(4))
    bg, gg, gh = bg / bb, gg / bb, gh / bb
    q = 1.0 / (1.0 + bg)
    p = bg * q
    ratio = (gg - bg * bg) * q * q
    d = p + ratio
    square = d * d - 2.0 * d * q * bg + q * q * gg
    image = d * d * bg - 2.0 * d * q * gg + q * q * gh
    step = ratio / (square + image)
    members = source.shape[0]
    pieces = sems.shape[1]
    copies = []
    for i in range(pieces):
        part = pl.ds(i * (members // pieces), members // pieces)
        b, g, h = source[part], first[part], second[part]
        held_weights[part] = (q + step * d) * b - (step * q) * g
        held_residual[part] = (p - step * d) * b + (step * q - q - step * d) * g + (step * q) * h
        for k, (held, out) in enumerate(((held_weights, weights), (held_residual, residual))):
            copies.append(pltpu.make_async_copy(held.at[part], out.at[part], sems.at[k, i]))
            copies[-1].start()
    for copy in copies:
        copy.wait()


def call(kernel, outs, *operands, cost=None):
    shapes = [jax.ShapeDtypeStruct(shape, F32) for shape in outs]
    vmem = pl.BlockSpec(memory_space=pltpu.VMEM)
    return pl.pallas_call(
        kernel,
        out_shape=shapes,
        in_specs=[vmem] * len(operands),
        out_specs=[vmem] * len(outs),
        compiler_params=pltpu.CompilerParams(vmem_limit_bytes=24 * 1024 * 1024),
        cost_estimate=cost,
    )(*operands)


def in_hbm(array):
    return pltpu.with_memory_space_constraint(array, pltpu.HBM)


def held_edges(source, members_data, precision, covered):
    members, levels, height, width = members_data.shape
    groups = members * EDGE // LANES
    payload = ((groups * (2 + levels) + 1) * height, LANES)
    vmem = pl.BlockSpec(memory_space=pltpu.VMEM)
    hbm = pl.BlockSpec(memory_space=pltpu.HBM)
    arrays = (source, members_data, precision, covered)
    return pl.pallas_call(
        edges_kernel,
        out_shape=[
            pltpu.VMEM(source.shape, F32),
            pltpu.VMEM(members_data.shape, members_data.dtype),
            pltpu.VMEM(precision.shape, F32),
            pltpu.VMEM((2, groups, height, LANES), F32),
            pltpu.VMEM((2, levels, groups, height, LANES), F32),
            pltpu.VMEM(payload, F32),
            pltpu.VMEM(payload, F32),
        ],
        in_specs=[hbm] * 4,
        out_specs=[vmem] * 7,
        scratch_shapes=[
            pltpu.VMEM(precision.shape, F32),
            pltpu.VMEM(covered.shape, covered.dtype),
            pltpu.SemaphoreType.DMA((4,)),
        ],
        compiler_params=pltpu.CompilerParams(vmem_limit_bytes=24 * 1024 * 1024),
    )(*map(in_hbm, arrays))


def first_increment(source, after, members_data):
    members, levels, height, width = members_data.shape
    groups = members * EDGE // LANES
    vmem = pl.BlockSpec(memory_space=pltpu.VMEM)
    return pl.pallas_call(
        first_kernel,
        out_shape=[
            pltpu.VMEM((levels * height + 8, width), F32),
            pltpu.VMEM((3, 2, LANES, LANES), BF16),
            pltpu.VMEM((2, groups * height, groups * height), BF16),
        ],
        in_specs=[vmem] * 3,
        out_specs=[vmem] * 3,
        compiler_params=pltpu.CompilerParams(vmem_limit_bytes=24 * 1024 * 1024),
        cost_estimate=LONG,
    )(source, after, members_data)


def fetched(after, *arrays):
    vmem = pl.BlockSpec(memory_space=pltpu.VMEM)
    hbm = pl.BlockSpec(memory_space=pltpu.HBM)
    size = sum(a.size * a.dtype.itemsize for a in arrays)
    return pl.pallas_call(
        fetch_kernel,
        out_shape=[pltpu.VMEM(a.shape, a.dtype) for a in arrays],
        in_specs=[vmem] + [hbm] * len(arrays),
        out_specs=[vmem] * len(arrays),
        scratch_shapes=[pltpu.SemaphoreType.DMA((len(arrays),))],
        compiler_params=pltpu.CompilerParams(vmem_limit_bytes=24 * 1024 * 1024),
        cost_estimate=pl.CostEstimate(flops=0, bytes_accessed=2 * size, transcendentals=0),
    )(after, *map(in_hbm, arrays))


def combined(own, other, source, first, second):
    vmem = pl.BlockSpec(memory_space=pltpu.VMEM)
    hbm = pl.BlockSpec(memory_space=pltpu.HBM)
    return pl.pallas_call(
        combine_kernel,
        out_shape=[jax.ShapeDtypeStruct(source.shape, F32)] * 2,
        in_specs=[vmem] * 5,
        out_specs=[hbm] * 2,
        scratch_shapes=[pltpu.VMEM(source.shape, F32)] * 2 + [pltpu.SemaphoreType.DMA((2, 4))],
        compiler_params=pltpu.CompilerParams(vmem_limit_bytes=24 * 1024 * 1024),
    )(own, other, source, first, second)


def from_both_sides(to_next, to_previous, axis):
    count = lax.axis_size(axis)
    left = lax.ppermute(to_next, axis, [(i, (i + 1) % count) for i in range(count)])
    right = lax.ppermute(to_previous, axis, [((i + 1) % count, i) for i in range(count)])
    return left, right


def from_tile(value, bit):
    count = lax.axis_size("tile")
    return lax.ppermute(value, "tile", [(i, i ^ bit) for i in range(count)])


def from_core(value):
    return from_tile(value, 1)


def from_chip(value):
    count = lax.axis_size("tile")
    return lax.ppermute(value, "tile", [(i, (i + 1) % count if i % 2 else (i - 1) % count) for i in range(count)])


def from_all(value, axis):
    count = lax.axis_size(axis)
    return [value] + [lax.ppermute(value, axis, [(i, i ^ k) for i in range(count)]) for k in range(1, count)]


def one_tile_row(right_side, perturbations, precision, covered):
    source, members_data = right_side[0], perturbations[0]
    members, levels, height, width = members_data.shape
    groups = members * EDGE // LANES
    taps = taps_np()
    twice = np.convolve(taps, taps)
    field = (members, height, width)
    plane = (levels, height, width)
    flat = (levels * height, width)
    row = halves(row_matrix(taps, height, members, 1))
    own = np.arange(width)

    source, members_data, obs_weight, near, edge_members, to_core, to_chip = held_edges(
        source, members_data, precision[0], covered[0]
    )
    core, chip = from_core(to_core), from_chip(to_chip)
    inside, edge, thin = first_increment(source, to_core, members_data)
    (increment,) = call(
        edge_kernel, [((levels + 1) * height + 8, width)], inside, core, chip, near, edge_members, edge, thin
    )
    parts = from_all(increment, "mem")
    column, row, column_twice, row_twice, edge, thin = fetched(
        increment, halves(column_matrix(taps, width, EDGE)), row,
        halves(band(twice, own, own)), halves(row_matrix(taps, height, members, 2)),
        edge_matrix(twice, EDGE), halves(row_matrix(taps, height, groups, 2)),
    )
    back, halo, weighted, sums, increment = call(
        middle_kernel,
        [field, (2, groups, height, LANES), plane, (2, 8, LANES), flat],
        *parts, obs_weight, core, chip, members_data, edge_members, column_twice, row_twice, edge, thin,
    )
    parts = from_all(increment, "mem")
    (first,) = call(wide_filter_kernel, [field], back, halo, column, row, cost=LONG)
    back, to_core, to_chip = call(
        last_kernel,
        [field, (groups * height + 8, LANES), (groups * height, LANES)],
        *parts, obs_weight, weighted, sums, members_data,
    )
    core = from_core(to_core)
    sums = to_core[groups * height :] + core[groups * height :]
    (to_chip,) = call(copy_kernel, [to_chip.shape], to_chip, sums)
    chip = from_chip(to_chip)
    sums = sums + from_tile(sums, 2)
    others = from_tile(sums, 4)
    (second,) = call(filter_kernel, [field], back, core, chip, column, row, cost=LONG)
    weights, residual = combined(sums, others, source, first, second)
    return weights[None], residual[None]


def passed_along(value, axis, steps):
    count = lax.axis_size(axis)
    first, last = (max(0, -steps), min(count, count - steps))
    return lax.ppermute(value, axis, [(source, source + steps) for source in range(first, last)])


def smooth(field):
    taps = taps_np().astype(np.float32)
    height, width = field.shape[1:]
    above = passed_along(field[:, height - REACH :, :], "tile", TCOLS)
    below = passed_along(field[:, :REACH, :], "tile", -TCOLS)
    padded = jnp.concatenate([above, field, below], axis=1)
    along = sum(taps[j] * padded[:, j : j + height, :] for j in range(2 * REACH + 1))
    left, right = from_both_sides(along[:, :, width - REACH :], along[:, :, :REACH], "tile")
    sided = jnp.concatenate([left, along, right], axis=2)
    return sum(taps[j] * sided[:, :, j : j + width] for j in range(2 * REACH + 1))


def several_tile_rows(right_side, perturbations, precision, covered):
    source = right_side[0]
    members_data = perturbations[0].astype(F32)
    levels, height, width = precision.shape[1:]
    rows, blocks = covered.shape[1:]
    mask = covered[0].astype(F32)
    obs_weight = (
        precision[0].reshape(levels, rows, height // rows, blocks, width // blocks) * mask[None, :, None, :, None]
    ).reshape(levels, height, width)

    def operator(direction):
        partial_terms = jnp.einsum("kvyx,kyx->vyx", members_data, smooth(direction))
        weighted = obs_weight * lax.psum(partial_terms, "mem")
        return direction + smooth(jnp.einsum("kvyx,vyx->kyx", members_data, weighted))

    weights = jnp.zeros_like(source)
    residual = direction = source
    norm_now = lax.psum(jnp.sum(source * source), ("tile", "mem"))
    for step in range(ITERS):
        image = operator(direction)
        length = norm_now / lax.psum(jnp.sum(direction * image), ("tile", "mem"))
        weights = weights + length * direction
        residual = residual - length * image
        if step + 1 < ITERS:
            norm_next = lax.psum(jnp.sum(residual * residual), ("tile", "mem"))
            direction = residual + norm_next / norm_now * direction
            norm_now = norm_next
    return weights[None], residual[None]


def solution(mesh):
    single = mesh.shape["tile"] == TCOLS and mesh.shape["mem"] == 4
    local = one_tile_row if single else several_tile_rows
    return jax.shard_map(
        local,
        mesh=mesh,
        in_specs=(
            P("tile", "mem", None, None),
            P("tile", "mem", None, None, None),
            P("tile", None, None, None),
            P("tile", None, None),
        ),
        out_specs=(P("tile", "mem", None, None), P("tile", "mem", None, None)),
        check_vma=False,
    )
```

```python
import functools

import jax
import jax.numpy as jnp
import ml_dtypes
import numpy as np
from jax import lax
from jax.experimental import pallas as pl
from jax.experimental.pallas import tpu as pltpu
from jax.sharding import PartitionSpec as P

ITERS = 2
TCOLS = 8
REACH = 8
EDGE = 2 * REACH
SPARE = 32
LANES = 128
F32 = jnp.float32
BF16 = jnp.bfloat16
LONG = pl.CostEstimate(flops=10**9, bytes_accessed=10**6, transcendentals=0)


def taps_np():
    offsets = np.arange(-REACH, REACH + 1, dtype=np.float64)
    raw = np.exp(-offsets * offsets / 32.0)
    return raw / np.sqrt(np.sum(np.exp(-offsets * offsets / 16.0)))


def band(taps, source, target):
    reach = (len(taps) - 1) // 2
    gap = source[:, None] - target[None, :]
    inside = np.abs(gap) <= reach
    return np.where(inside, taps[np.clip(gap + reach, 0, 2 * reach)], 0.0)


def halves(matrix):
    whole = matrix.astype(np.float32)
    high = whole.astype(ml_dtypes.bfloat16)
    low = (whole - high.astype(np.float32)).astype(ml_dtypes.bfloat16)
    return np.stack([high, low])


def column_matrix(taps, width, edge):
    target = np.arange(width)
    slots = LANES // edge
    left = np.tile(np.arange(edge) - edge, slots)
    right = np.tile(np.arange(edge) + width, slots)
    return np.concatenate([band(taps, s, target) for s in (np.arange(width), left, right)])


def row_matrix(taps, height, members, times):
    one = band(taps, np.arange(height), np.arange(height))
    return np.kron(np.eye(members), np.linalg.matrix_power(one, times))


def edge_matrix(taps, edge):
    inner = np.arange(edge)
    sides = (band(taps, inner - edge, inner), band(taps, inner + edge, inner))
    return np.stack([halves(np.kron(np.eye(LANES // edge), side)) for side in sides])


def split(x):
    high = x.astype(BF16)
    return high, (x - high.astype(F32)).astype(BF16)


def dot3(left, right):
    mul = functools.partial(jnp.dot, preferred_element_type=F32)
    return mul(left[0], right[0]) + (mul(left[1], right[0]) + mul(left[0], right[1]))


def both(ref):
    return ref[0], ref[1]


def lane_of(shape):
    return lax.broadcasted_iota(jnp.int32, shape, len(shape) - 1)


def pack_columns(field, start, edge):
    members, rows, _ = field.shape
    slots = LANES // edge
    groups = members // slots
    lane = lane_of((rows, LANES))
    origin = start // LANES * LANES
    out = []
    for g in range(groups):
        total = jnp.zeros((rows, LANES), F32)
        for j in range(slots):
            block = field[j * groups + g][:, origin : origin + LANES]
            shift = (j * edge - (start - origin)) % LANES
            moved = pltpu.roll(block, shift, 1) if shift else block
            total = jnp.where((lane >= j * edge) & (lane < (j + 1) * edge), moved, total)
        out.append(total)
    return jnp.stack(out)


def pack_edges(field, edge, first):
    return pack_columns(field, 0 if first else field.shape[-1] - edge, edge)


def repeated(x, period):
    while period < LANES:
        x = x + pltpu.roll(x, period, len(x.shape) - 1)
        period *= 2
    return x


def level_lanes(shape, level):
    lane = lane_of(shape)
    return (lane >= level * EDGE) & (lane < (level + 1) * EDGE)


def sides_of(core, chip):
    odd = lax.axis_index("tile") % 2 == 1
    return jnp.where(odd, core, chip), jnp.where(odd, chip, core)


def spread_edges(packed, edge):
    groups, rows, _ = packed.shape
    slots = LANES // edge
    lane = lane_of((groups, rows, LANES))
    parts = [jnp.where((lane >= j * edge) & (lane < (j + 1) * edge), packed, 0.0) for j in range(slots)]
    return jnp.concatenate(parts, axis=0).reshape(slots * groups * rows, LANES)


def beside(field, left, right, edge):
    members, rows, width = field.shape
    return jnp.concatenate(
        [field.reshape(members * rows, width), spread_edges(left, edge), spread_edges(right, edge)], axis=1
    )


def increments(members_ref, smoothed):
    members, levels = members_ref.shape[:2]
    totals = []
    for v in range(levels):
        total = members_ref[0, v].astype(F32) * smoothed[0]
        for k in range(1, members):
            total = total + members_ref[k, v].astype(F32) * smoothed[k]
        totals.append(total)
    return jnp.stack(totals)


def adjoint(members_ref, weighted):
    members, levels = members_ref.shape[:2]
    back = []
    for k in range(members):
        total = members_ref[k, 0].astype(F32) * weighted[0]
        for v in range(1, levels):
            total = total + members_ref[k, v].astype(F32) * weighted[v]
        back.append(total)
    return jnp.stack(back)


def folded(x):
    width = x.shape[-1]
    x = x.reshape(-1, 8, width).sum(axis=0)
    return sum(x[:, i : i + LANES] for i in range(0, width, LANES))


def edges_kernel(
    source_hbm, members_hbm, precision_hbm, covered_hbm,
    source, members_ref, obs_weight, near, edge_members, to_core, to_chip, precision, covered, sems,
):
    pairs = ((source_hbm, source), (precision_hbm, precision), (covered_hbm, covered), (members_hbm, members_ref))
    copies = [pltpu.make_async_copy(x, y, sems.at[i]) for i, (x, y) in enumerate(pairs)]
    for copy in copies:
        copy.start()
    members, levels, height, width = members_ref.shape
    groups = members * EDGE // LANES
    odd = lax.axis_index("tile") % 2 == 1
    rows = groups * height

    def send(at, first, last):
        first, last = (x.reshape(-1, LANES) for x in (first, last))
        part = pl.ds(at, first.shape[0])
        to_core[part] = jnp.where(odd, first, last)
        to_chip[part] = jnp.where(odd, last, first)

    copies[0].wait()
    near[0], near[1] = pack_columns(source, 0, EDGE), pack_columns(source, width - EDGE, EDGE)
    send(0, near[0], near[1])
    send(rows, pack_columns(source, EDGE, EDGE), pack_columns(source, width - 2 * EDGE, EDGE))
    copies[1].wait()
    copies[2].wait()
    obs_weight[...] = weight_of(precision, covered)
    sides = []
    for start in (0, width - EDGE):
        total = jnp.zeros((height, LANES), F32)
        for v in range(levels):
            origin = start // LANES * LANES
            shift = (v * EDGE - (start - origin)) % LANES
            block = obs_weight[v, :, origin : origin + LANES]
            total = jnp.where(level_lanes(total.shape, v), pltpu.roll(block, shift, 1) if shift else block, total)
        sides.append(total)
    send(rows * (2 + levels), *sides)
    copies[3].wait()
    for v in range(levels):
        level = members_ref[:, v].astype(F32)
        edge_members[0, v], edge_members[1, v] = pack_edges(level, EDGE, True), pack_edges(level, EDGE, False)
        send(rows * (2 + v), edge_members[0, v], edge_members[1, v])


def fetch_kernel(*refs):
    count = (len(refs) - 2) // 2
    copies = [pltpu.make_async_copy(refs[1 + i], refs[1 + count + i], refs[-1].at[i]) for i in range(count)]
    for copy in copies:
        copy.start()
    for copy in copies:
        copy.wait()


def own_columns(field, column, row):
    members, height, width = field.shape
    lhs = split(field[...].reshape(members * height, width))
    return dot3(both(row), split(dot3(lhs, both(column)))).reshape(field.shape)


def tap_at(gap, inside):
    scale = 1.0 / np.sqrt(np.sum(np.exp(-(np.arange(-REACH, REACH + 1.0) ** 2) / 16.0)))
    square = (gap * gap).astype(F32)
    return jnp.where(inside & (jnp.abs(gap) <= REACH), jnp.exp(square * (-1.0 / 32.0)) * scale, 0.0)


def gaps(rows, columns):
    shape = (rows, columns)
    down, across = (lax.broadcasted_iota(jnp.int32, shape, i) for i in range(2))
    return down, across, down - across


def kept(ref, matrix):
    ref[0], ref[1] = split(matrix)


def first_kernel(source, after, members_ref, increment, norm, edge, thin):
    members, levels, height, width = members_ref.shape
    _, _, gap = gaps(width, width)
    column = split(tap_at(gap, True))
    down, across, gap = gaps(members * height, members * height)
    row = split(tap_at(gap, down // height == across // height))
    lhs = split(source[...].reshape(members * height, width))
    smoothed = dot3(row, split(dot3(lhs, column))).reshape(source.shape)
    increment[...] = increments(members_ref, smoothed).reshape(levels * height, width)
    norm[...] = repeated(folded(source[...] * source[...]), SPARE)
    down, across, gap = gaps(LANES, LANES)
    same = down // EDGE == across // EDGE
    for i in range(3):
        kept(edge.at[i], tap_at(gap + (i - 1) * EDGE, same))
    down, across, gap = gaps(*thin.shape[1:])
    kept(thin, tap_at(gap, down // height == across // height))


def edge_sums(edge_members, smoothed):
    groups, height = edge_members.shape[1:3]
    return repeated(jnp.sum(edge_members * smoothed.reshape(1, groups, height, LANES), axis=1), EDGE)


def add_edges(out, sums, side):
    levels, height, _ = sums.shape
    width = out.shape[-1]
    lane = lane_of(sums.shape)
    if side == 0:
        span, mask = pl.ds(0, LANES), lane < EDGE
    else:
        span, mask = pl.ds(width - LANES, LANES), lane >= LANES - EDGE
    rows = pl.ds(0, levels * height)
    out[rows, span] = out[rows, span] + jnp.where(mask, sums, 0.0).reshape(levels * height, LANES)


def halo_members(block, rows, groups, levels):
    height = rows // groups
    return block[2 * rows : (2 + levels) * rows].reshape(levels, groups, height, LANES)


def edge_kernel(inside, norm, core, chip, near, edge_members, edge, thin, out):
    levels, groups, height = edge_members.shape[1:4]
    width = out.shape[-1]
    rows = groups * height
    out[: inside.shape[0]] = inside[...]
    sides = sides_of(core[...], chip[...])
    parts = []
    for side, block in enumerate(sides):
        parts += [block[rows : 2 * rows], block[:rows], near[side].reshape(rows, LANES)]
    filtered = split(dot3(both(thin), split(jnp.concatenate(parts, axis=1))))
    outer = []
    for side, block in enumerate(sides):
        span = slice(3 * side * LANES, 3 * (side + 1) * LANES)
        order = (0, 1, 2) if side == 0 else (2, 1, 0)
        matrix = [jnp.concatenate([edge[i, k] for i in order], axis=0) for k in range(2)]
        beyond = dot3(tuple(x[:, span] for x in filtered), matrix)
        middle = slice(span.start + LANES, span.start + 2 * LANES)
        within = dot3(tuple(x[:, middle] for x in filtered), both(edge.at[order[0]]))
        add_edges(out, edge_sums(edge_members[side], within), side)
        sums = edge_sums(halo_members(block, rows, groups, levels), beyond)
        total = jnp.zeros((height, LANES), F32)
        for v in range(levels):
            total = jnp.where(level_lanes(total.shape, v), sums[v], total)
        outer.append(total)
    lane = lane_of(norm.shape)
    out[inside.shape[0] :] = jnp.concatenate(outer, axis=1)
    top = pl.ds(inside.shape[0], norm.shape[0])
    out[top, :LANES] = jnp.where(lane >= LANES - SPARE, norm[...], out[top, :LANES])


def weight_of(precision, covered):
    levels, height, width = precision.shape
    rows, blocks = covered.shape
    spread = lax.broadcasted_iota(jnp.int32, (blocks, width), 1) // (width // blocks)
    spread = (spread == lax.broadcasted_iota(jnp.int32, (blocks, width), 0)).astype(BF16)
    mask = jnp.dot(covered[...].astype(F32).astype(BF16), spread, preferred_element_type=F32)
    tall = height // rows
    mask = jnp.concatenate([jnp.broadcast_to(mask[i : i + 1], (tall, width)) for i in range(rows)], axis=0)
    return precision[...] * mask


def middle_kernel(
    i0, i1, i2, i3, obs_weight, core, chip, members_ref, edge_members, column, row, edge, thin,
    back, halo, weighted, sums, out,
):
    levels, height, width = obs_weight.shape
    groups = edge_members.shape[2]
    rows = groups * height
    total = (i0[...] + i1[...]) + (i2[...] + i3[...])
    flat = levels * height
    increment = total[:flat].reshape(levels, height, width)
    weighted[...] = obs_weight[...] * increment
    top = total[flat : flat + 8, :LANES]
    sums[0] = jnp.where(lane_of(top.shape) >= LANES - SPARE, top, 0.0)
    sums[1] = folded(weighted[...] * increment)
    back[...] = adjoint(members_ref, weighted)
    smoothed = own_columns(back, column, row)
    for side, block in enumerate(sides_of(core[...], chip[...])):
        outer = total[flat:, side * LANES : (side + 1) * LANES] * block[(2 + levels) * rows :]
        members = halo_members(block, rows, groups, levels)
        adjoint_here = jnp.zeros((groups, height, LANES), F32)
        for v in range(levels):
            level = repeated(jnp.where(level_lanes(outer.shape, v), outer, 0.0), EDGE)
            adjoint_here = adjoint_here + members[v] * level
        halo[side] = adjoint_here
    filtered = split(dot3(both(thin), split(jnp.concatenate([halo[i].reshape(rows, LANES) for i in range(2)], axis=1))))
    out[...] = increments(members_ref, smoothed).reshape(flat, width)
    for side in range(2):
        part = dot3(tuple(x[:, side * LANES : (side + 1) * LANES] for x in filtered), both(edge.at[side]))
        add_edges(out, edge_sums(edge_members[side], part), side)


def wide_filter_kernel(back, halo, column, row, out):
    lhs = split(beside(back[...], halo[0], halo[1], EDGE))
    out[...] = dot3(both(row), split(dot3(lhs, both(column)))).reshape(out.shape)


def filter_kernel(back, core, chip, column, row, out):
    groups, height = back.shape[0] * EDGE // LANES, back.shape[1]
    left, right = sides_of(*(x[: groups * height].reshape(groups, height, LANES) for x in (core, chip)))
    lhs = split(beside(back[...], left, right, EDGE))
    out[...] = dot3(both(row), split(dot3(lhs, both(column)))).reshape(out.shape)


def last_kernel(i0, i1, i2, i3, obs_weight, before, sums, members_ref, back, to_core, to_chip):
    levels, height, width = obs_weight.shape
    increment = ((i0[...] + i1[...]) + (i2[...] + i3[...])).reshape(obs_weight.shape)
    weighted = obs_weight[...] * increment
    four = [sums[0], sums[1], folded(before[...] * increment), folded(weighted * increment)]
    row = lax.broadcasted_iota(jnp.int32, (8, LANES), 0)
    stacked = jnp.zeros((8, LANES), F32)
    for i, part in enumerate(four):
        stacked = jnp.where(row == i, jnp.sum(part, axis=0, keepdims=True), stacked)
    back[...] = adjoint(members_ref, weighted)
    odd = lax.axis_index("tile") % 2 == 1
    first, last = pack_edges(back, EDGE, True), pack_edges(back, EDGE, False)
    rows = first.shape[0] * height
    to_core[:rows] = jnp.where(odd, first, last).reshape(rows, LANES)
    to_core[rows:] = stacked
    to_chip[...] = jnp.where(odd, last, first).reshape(rows, LANES)


def copy_kernel(value, after, out):
    out[...] = value[...]


def pass_kernel(value, after, out):
    pass


def combine_kernel(own, other, source, first, second, weights, residual, held_weights, held_residual, sems):
    total = jnp.sum(own[...] + other[...], axis=1, keepdims=True)
    bb, bg, gg, gh = (total[i : i + 1] for i in range(4))
    bg, gg, gh = bg / bb, gg / bb, gh / bb
    q = 1.0 / (1.0 + bg)
    p = bg * q
    ratio = (gg - bg * bg) * q * q
    d = p + ratio
    square = d * d - 2.0 * d * q * bg + q * q * gg
    image = d * d * bg - 2.0 * d * q * gg + q * q * gh
    step = ratio / (square + image)
    members = source.shape[0]
    pieces = sems.shape[1]
    copies = []
    for i in range(pieces):
        part = pl.ds(i * (members // pieces), members // pieces)
        b, g, h = source[part], first[part], second[part]
        held_weights[part] = (q + step * d) * b - (step * q) * g
        held_residual[part] = (p - step * d) * b + (step * q - q - step * d) * g + (step * q) * h
        for k, (held, out) in enumerate(((held_weights, weights), (held_residual, residual))):
            copies.append(pltpu.make_async_copy(held.at[part], out.at[part], sems.at[k, i]))
            copies[-1].start()
    for copy in copies:
        copy.wait()


def call(kernel, outs, *operands, cost=None):
    shapes = [jax.ShapeDtypeStruct(shape, F32) for shape in outs]
    vmem = pl.BlockSpec(memory_space=pltpu.VMEM)
    return pl.pallas_call(
        kernel,
        out_shape=shapes,
        in_specs=[vmem] * len(operands),
        out_specs=[vmem] * len(outs),
        compiler_params=pltpu.CompilerParams(vmem_limit_bytes=24 * 1024 * 1024),
        cost_estimate=cost,
    )(*operands)


def passed(value, after):
    vmem = pl.BlockSpec(memory_space=pltpu.VMEM)
    return pl.pallas_call(
        pass_kernel,
        out_shape=pltpu.VMEM(value.shape, value.dtype),
        in_specs=[vmem] * 2,
        out_specs=vmem,
        input_output_aliases={0: 0},
        compiler_params=pltpu.CompilerParams(vmem_limit_bytes=24 * 1024 * 1024),
        cost_estimate=LONG,
    )(value, after)


def in_hbm(array):
    return pltpu.with_memory_space_constraint(array, pltpu.HBM)


def held_edges(source, members_data, precision, covered):
    members, levels, height, width = members_data.shape
    groups = members * EDGE // LANES
    payload = ((groups * (2 + levels) + 1) * height, LANES)
    vmem = pl.BlockSpec(memory_space=pltpu.VMEM)
    hbm = pl.BlockSpec(memory_space=pltpu.HBM)
    arrays = (source, members_data, precision, covered)
    return pl.pallas_call(
        edges_kernel,
        out_shape=[
            pltpu.VMEM(source.shape, F32),
            pltpu.VMEM(members_data.shape, members_data.dtype),
            pltpu.VMEM(precision.shape, F32),
            pltpu.VMEM((2, groups, height, LANES), F32),
            pltpu.VMEM((2, levels, groups, height, LANES), F32),
            pltpu.VMEM(payload, F32),
            pltpu.VMEM(payload, F32),
        ],
        in_specs=[hbm] * 4,
        out_specs=[vmem] * 7,
        scratch_shapes=[
            pltpu.VMEM(precision.shape, F32),
            pltpu.VMEM(covered.shape, covered.dtype),
            pltpu.SemaphoreType.DMA((4,)),
        ],
        compiler_params=pltpu.CompilerParams(vmem_limit_bytes=24 * 1024 * 1024),
    )(*map(in_hbm, arrays))


def first_increment(source, after, members_data):
    members, levels, height, width = members_data.shape
    groups = members * EDGE // LANES
    vmem = pl.BlockSpec(memory_space=pltpu.VMEM)
    return pl.pallas_call(
        first_kernel,
        out_shape=[
            pltpu.VMEM((levels * height, width), F32),
            pltpu.VMEM((8, LANES), F32),
            pltpu.VMEM((3, 2, LANES, LANES), BF16),
            pltpu.VMEM((2, groups * height, groups * height), BF16),
        ],
        in_specs=[vmem] * 3,
        out_specs=[vmem] * 4,
        compiler_params=pltpu.CompilerParams(vmem_limit_bytes=24 * 1024 * 1024),
        cost_estimate=LONG,
    )(source, after, members_data)


def fetched(after, *arrays):
    vmem = pl.BlockSpec(memory_space=pltpu.VMEM)
    hbm = pl.BlockSpec(memory_space=pltpu.HBM)
    size = sum(a.size * a.dtype.itemsize for a in arrays)
    return pl.pallas_call(
        fetch_kernel,
        out_shape=[pltpu.VMEM(a.shape, a.dtype) for a in arrays],
        in_specs=[vmem] + [hbm] * len(arrays),
        out_specs=[vmem] * len(arrays),
        scratch_shapes=[pltpu.SemaphoreType.DMA((len(arrays),))],
        compiler_params=pltpu.CompilerParams(vmem_limit_bytes=24 * 1024 * 1024),
        cost_estimate=pl.CostEstimate(flops=0, bytes_accessed=2 * size, transcendentals=0),
    )(after, *map(in_hbm, arrays))


def combined(own, other, source, first, second):
    vmem = pl.BlockSpec(memory_space=pltpu.VMEM)
    hbm = pl.BlockSpec(memory_space=pltpu.HBM)
    return pl.pallas_call(
        combine_kernel,
        out_shape=[jax.ShapeDtypeStruct(source.shape, F32)] * 2,
        in_specs=[vmem] * 5,
        out_specs=[hbm] * 2,
        scratch_shapes=[pltpu.VMEM(source.shape, F32)] * 2 + [pltpu.SemaphoreType.DMA((2, 4))],
        compiler_params=pltpu.CompilerParams(vmem_limit_bytes=24 * 1024 * 1024),
    )(own, other, source, first, second)


def from_both_sides(to_next, to_previous, axis):
    count = lax.axis_size(axis)
    left = lax.ppermute(to_next, axis, [(i, (i + 1) % count) for i in range(count)])
    right = lax.ppermute(to_previous, axis, [((i + 1) % count, i) for i in range(count)])
    return left, right


def from_tile(value, bit):
    count = lax.axis_size("tile")
    return lax.ppermute(value, "tile", [(i, i ^ bit) for i in range(count)])


def from_core(value):
    return from_tile(value, 1)


def from_chip(value):
    count = lax.axis_size("tile")
    return lax.ppermute(value, "tile", [(i, (i + 1) % count if i % 2 else (i - 1) % count) for i in range(count)])


def from_all(value, axis):
    count = lax.axis_size(axis)
    return [value] + [lax.ppermute(value, axis, [(i, i ^ k) for i in range(count)]) for k in range(1, count)]


def one_tile_row(right_side, perturbations, precision, covered):
    source, members_data = right_side[0], perturbations[0]
    members, levels, height, width = members_data.shape
    groups = members * EDGE // LANES
    taps = taps_np()
    twice = np.convolve(taps, taps)
    field = (members, height, width)
    plane = (levels, height, width)
    flat = (levels * height, width)
    row = halves(row_matrix(taps, height, members, 1))
    own = np.arange(width)

    source, members_data, obs_weight, near, edge_members, to_core, to_chip = held_edges(
        source, members_data, precision[0], covered[0]
    )
    core, chip = from_core(to_core), from_chip(to_chip)
    inside, norm, edge, thin = first_increment(source, to_core, members_data)
    (increment,) = call(
        edge_kernel, [((levels + 1) * height, width)], inside, norm, core, chip, near, edge_members, edge, thin
    )
    parts = from_all(increment, "mem")
    column, row, column_twice, row_twice, edge, thin = fetched(
        increment, halves(column_matrix(taps, width, EDGE)), row,
        halves(band(twice, own, own)), halves(row_matrix(taps, height, members, 2)),
        edge_matrix(twice, EDGE), halves(row_matrix(taps, height, groups, 2)),
    )
    back, halo, weighted, sums, increment = call(
        middle_kernel,
        [field, (2, groups, height, LANES), plane, (2, 8, LANES), flat],
        *parts, obs_weight, core, chip, members_data, edge_members, column_twice, row_twice, edge, thin,
    )
    parts = from_all(increment, "mem")
    (first,) = call(wide_filter_kernel, [field], back, halo, column, row, cost=LONG)
    first, weighted = lax.optimization_barrier((first, weighted))
    back, to_core, to_chip = call(
        last_kernel,
        [field, (groups * height + 8, LANES), (groups * height, LANES)],
        *parts, obs_weight, weighted, sums, members_data,
    )
    core = from_core(to_core)
    sums = to_core[groups * height :] + core[groups * height :]
    (to_chip,) = call(copy_kernel, [to_chip.shape], to_chip, sums)
    chip = from_chip(to_chip)
    first = passed(first, sums)
    sums = sums + from_tile(sums, 2)
    others = from_tile(sums, 4)
    (second,) = call(filter_kernel, [field], back, core, chip, column, row, cost=LONG)
    weights, residual = combined(sums, others, source, first, second)
    return weights[None], residual[None]


def passed_along(value, axis, steps):
    count = lax.axis_size(axis)
    first, last = (max(0, -steps), min(count, count - steps))
    return lax.ppermute(value, axis, [(source, source + steps) for source in range(first, last)])


def smooth(field):
    taps = taps_np().astype(np.float32)
    height, width = field.shape[1:]
    above = passed_along(field[:, height - REACH :, :], "tile", TCOLS)
    below = passed_along(field[:, :REACH, :], "tile", -TCOLS)
    padded = jnp.concatenate([above, field, below], axis=1)
    along = sum(taps[j] * padded[:, j : j + height, :] for j in range(2 * REACH + 1))
    left, right = from_both_sides(along[:, :, width - REACH :], along[:, :, :REACH], "tile")
    sided = jnp.concatenate([left, along, right], axis=2)
    return sum(taps[j] * sided[:, :, j : j + width] for j in range(2 * REACH + 1))


def several_tile_rows(right_side, perturbations, precision, covered):
    source = right_side[0]
    members_data = perturbations[0].astype(F32)
    levels, height, width = precision.shape[1:]
    rows, blocks = covered.shape[1:]
    mask = covered[0].astype(F32)
    obs_weight = (
        precision[0].reshape(levels, rows, height // rows, blocks, width // blocks) * mask[None, :, None, :, None]
    ).reshape(levels, height, width)

    def operator(direction):
        partial_terms = jnp.einsum("kvyx,kyx->vyx", members_data, smooth(direction))
        weighted = obs_weight * lax.psum(partial_terms, "mem")
        return direction + smooth(jnp.einsum("kvyx,vyx->kyx", members_data, weighted))

    weights = jnp.zeros_like(source)
    residual = direction = source
    norm_now = lax.psum(jnp.sum(source * source), ("tile", "mem"))
    for step in range(ITERS):
        image = operator(direction)
        length = norm_now / lax.psum(jnp.sum(direction * image), ("tile", "mem"))
        weights = weights + length * direction
        residual = residual - length * image
        if step + 1 < ITERS:
            norm_next = lax.psum(jnp.sum(residual * residual), ("tile", "mem"))
            direction = residual + norm_next / norm_now * direction
            norm_now = norm_next
    return weights[None], residual[None]


def solution(mesh):
    single = mesh.shape["tile"] == TCOLS and mesh.shape["mem"] == 4
    local = one_tile_row if single else several_tile_rows
    return jax.shard_map(
        local,
        mesh=mesh,
        in_specs=(
            P("tile", "mem", None, None),
            P("tile", "mem", None, None, None),
            P("tile", None, None, None),
            P("tile", None, None),
        ),
        out_specs=(P("tile", "mem", None, None), P("tile", "mem", None, None)),
        check_vma=False,
    )
```

```python
import functools

import jax
import jax.numpy as jnp
import ml_dtypes
import numpy as np
from jax import lax
from jax.experimental import pallas as pl
from jax.experimental.pallas import tpu as pltpu
from jax.sharding import PartitionSpec as P

ITERS = 2
TCOLS = 8
REACH = 8
EDGE = 2 * REACH
SPARE = 32
LANES = 128
F32 = jnp.float32
BF16 = jnp.bfloat16
LONG = pl.CostEstimate(flops=10**9, bytes_accessed=10**6, transcendentals=0)


def taps_np():
    offsets = np.arange(-REACH, REACH + 1, dtype=np.float64)
    raw = np.exp(-offsets * offsets / 32.0)
    return raw / np.sqrt(np.sum(np.exp(-offsets * offsets / 16.0)))


def band(taps, source, target):
    reach = (len(taps) - 1) // 2
    gap = source[:, None] - target[None, :]
    inside = np.abs(gap) <= reach
    return np.where(inside, taps[np.clip(gap + reach, 0, 2 * reach)], 0.0)


def halves(matrix):
    whole = matrix.astype(np.float32)
    high = whole.astype(ml_dtypes.bfloat16)
    low = (whole - high.astype(np.float32)).astype(ml_dtypes.bfloat16)
    return np.stack([high, low])


def column_matrix(taps, width, edge):
    target = np.arange(width)
    slots = LANES // edge
    left = np.tile(np.arange(edge) - edge, slots)
    right = np.tile(np.arange(edge) + width, slots)
    return np.concatenate([band(taps, s, target) for s in (np.arange(width), left, right)])


def row_matrix(taps, height, members, times):
    one = band(taps, np.arange(height), np.arange(height))
    return np.kron(np.eye(members), np.linalg.matrix_power(one, times))


def edge_matrix(taps, edge):
    inner = np.arange(edge)
    sides = (band(taps, inner - edge, inner), band(taps, inner + edge, inner))
    return np.stack([halves(np.kron(np.eye(LANES // edge), side)) for side in sides])


def split(x):
    high = x.astype(BF16)
    return high, (x - high.astype(F32)).astype(BF16)


def dot3(left, right):
    mul = functools.partial(jnp.dot, preferred_element_type=F32)
    return mul(left[0], right[0]) + (mul(left[1], right[0]) + mul(left[0], right[1]))


def both(ref):
    return ref[0], ref[1]


def lane_of(shape):
    return lax.broadcasted_iota(jnp.int32, shape, len(shape) - 1)


def pack_columns(field, start, edge):
    members, rows, _ = field.shape
    slots = LANES // edge
    groups = members // slots
    lane = lane_of((rows, LANES))
    origin = start // LANES * LANES
    out = []
    for g in range(groups):
        total = jnp.zeros((rows, LANES), F32)
        for j in range(slots):
            block = field[j * groups + g][:, origin : origin + LANES]
            shift = (j * edge - (start - origin)) % LANES
            moved = pltpu.roll(block, shift, 1) if shift else block
            total = jnp.where((lane >= j * edge) & (lane < (j + 1) * edge), moved, total)
        out.append(total)
    return jnp.stack(out)


def pack_edges(field, edge, first):
    return pack_columns(field, 0 if first else field.shape[-1] - edge, edge)


def repeated(x, period):
    while period < LANES:
        x = x + pltpu.roll(x, period, len(x.shape) - 1)
        period *= 2
    return x


def level_lanes(shape, level):
    lane = lane_of(shape)
    return (lane >= level * EDGE) & (lane < (level + 1) * EDGE)


def sides_of(core, chip):
    odd = lax.axis_index("tile") % 2 == 1
    return jnp.where(odd, core, chip), jnp.where(odd, chip, core)


def spread_edges(packed, edge):
    groups, rows, _ = packed.shape
    slots = LANES // edge
    lane = lane_of((groups, rows, LANES))
    parts = [jnp.where((lane >= j * edge) & (lane < (j + 1) * edge), packed, 0.0) for j in range(slots)]
    return jnp.concatenate(parts, axis=0).reshape(slots * groups * rows, LANES)


def beside(field, left, right, edge):
    members, rows, width = field.shape
    return jnp.concatenate(
        [field.reshape(members * rows, width), spread_edges(left, edge), spread_edges(right, edge)], axis=1
    )


def increments(members_ref, smoothed):
    members, levels = members_ref.shape[:2]
    totals = []
    for v in range(levels):
        total = members_ref[0, v].astype(F32) * smoothed[0]
        for k in range(1, members):
            total = total + members_ref[k, v].astype(F32) * smoothed[k]
        totals.append(total)
    return jnp.stack(totals)


def adjoint(members_ref, weighted):
    members, levels = members_ref.shape[:2]
    back = []
    for k in range(members):
        total = members_ref[k, 0].astype(F32) * weighted[0]
        for v in range(1, levels):
            total = total + members_ref[k, v].astype(F32) * weighted[v]
        back.append(total)
    return jnp.stack(back)


def folded(x):
    width = x.shape[-1]
    x = x.reshape(-1, 8, width).sum(axis=0)
    return sum(x[:, i : i + LANES] for i in range(0, width, LANES))


def edges_kernel(
    source_hbm, members_hbm, precision_hbm, covered_hbm,
    source, members_ref, obs_weight, near, edge_members, to_core, to_chip, precision, covered, sems,
):
    pairs = ((source_hbm, source), (precision_hbm, precision), (covered_hbm, covered), (members_hbm, members_ref))
    copies = [pltpu.make_async_copy(x, y, sems.at[i]) for i, (x, y) in enumerate(pairs)]
    for copy in copies:
        copy.start()
    members, levels, height, width = members_ref.shape
    groups = members * EDGE // LANES
    odd = lax.axis_index("tile") % 2 == 1
    rows = groups * height

    def send(at, first, last):
        first, last = (x.reshape(-1, LANES) for x in (first, last))
        part = pl.ds(at, first.shape[0])
        to_core[part] = jnp.where(odd, first, last)
        to_chip[part] = jnp.where(odd, last, first)

    copies[0].wait()
    near[0], near[1] = pack_columns(source, 0, EDGE), pack_columns(source, width - EDGE, EDGE)
    send(0, near[0], near[1])
    send(rows, pack_columns(source, EDGE, EDGE), pack_columns(source, width - 2 * EDGE, EDGE))
    copies[1].wait()
    copies[2].wait()
    obs_weight[...] = weight_of(precision, covered)
    sides = []
    for start in (0, width - EDGE):
        total = jnp.zeros((height, LANES), F32)
        for v in range(levels):
            origin = start // LANES * LANES
            shift = (v * EDGE - (start - origin)) % LANES
            block = obs_weight[v, :, origin : origin + LANES]
            total = jnp.where(level_lanes(total.shape, v), pltpu.roll(block, shift, 1) if shift else block, total)
        sides.append(total)
    send(rows * (2 + levels), *sides)
    copies[3].wait()
    for v in range(levels):
        level = members_ref[:, v].astype(F32)
        edge_members[0, v], edge_members[1, v] = pack_edges(level, EDGE, True), pack_edges(level, EDGE, False)
        send(rows * (2 + v), edge_members[0, v], edge_members[1, v])


def fetch_kernel(*refs):
    count = (len(refs) - 2) // 2
    copies = [pltpu.make_async_copy(refs[1 + i], refs[1 + count + i], refs[-1].at[i]) for i in range(count)]
    for copy in copies:
        copy.start()
    for copy in copies:
        copy.wait()


def own_columns(field, column, row):
    members, height, width = field.shape
    lhs = split(field[...].reshape(members * height, width))
    return dot3(both(row), split(dot3(lhs, both(column)))).reshape(field.shape)


def tap_at(gap, inside):
    scale = 1.0 / np.sqrt(np.sum(np.exp(-(np.arange(-REACH, REACH + 1.0) ** 2) / 16.0)))
    square = (gap * gap).astype(F32)
    return jnp.where(inside & (jnp.abs(gap) <= REACH), jnp.exp(square * (-1.0 / 32.0)) * scale, 0.0)


def gaps(rows, columns):
    shape = (rows, columns)
    down, across = (lax.broadcasted_iota(jnp.int32, shape, i) for i in range(2))
    return down, across, down - across


def kept(ref, matrix):
    ref[0], ref[1] = split(matrix)


def first_kernel(source, after, members_ref, increment, norm, edge, thin):
    members, levels, height, width = members_ref.shape
    _, _, gap = gaps(width, width)
    column = split(tap_at(gap, True))
    down, across, gap = gaps(members * height, members * height)
    row = split(tap_at(gap, down // height == across // height))
    lhs = split(source[...].reshape(members * height, width))
    smoothed = dot3(row, split(dot3(lhs, column))).reshape(source.shape)
    increment[...] = increments(members_ref, smoothed).reshape(levels * height, width)
    norm[...] = repeated(folded(source[...] * source[...]), SPARE)
    down, across, gap = gaps(LANES, LANES)
    same = down // EDGE == across // EDGE
    for i in range(3):
        kept(edge.at[i], tap_at(gap + (i - 1) * EDGE, same))
    down, across, gap = gaps(*thin.shape[1:])
    kept(thin, tap_at(gap, down // height == across // height))


def edge_sums(edge_members, smoothed):
    groups, height = edge_members.shape[1:3]
    return repeated(jnp.sum(edge_members * smoothed.reshape(1, groups, height, LANES), axis=1), EDGE)


def add_edges(out, sums, side):
    levels, height, _ = sums.shape
    width = out.shape[-1]
    lane = lane_of(sums.shape)
    if side == 0:
        span, mask = pl.ds(0, LANES), lane < EDGE
    else:
        span, mask = pl.ds(width - LANES, LANES), lane >= LANES - EDGE
    rows = pl.ds(0, levels * height)
    out[rows, span] = out[rows, span] + jnp.where(mask, sums, 0.0).reshape(levels * height, LANES)


def beside_levels(sums):
    total = jnp.zeros(sums.shape[1:], F32)
    for v in range(sums.shape[0]):
        total = jnp.where(level_lanes(total.shape, v), sums[v], total)
    return total


def apart_levels(packed, levels):
    return [repeated(jnp.where(level_lanes(packed.shape, v), packed, 0.0), EDGE) for v in range(levels)]


def halo_members(block, rows, groups, levels):
    height = rows // groups
    return block[2 * rows : (2 + levels) * rows].reshape(levels, groups, height, LANES)


def edge_kernel(norm, core, chip, near, edge_members, edge, thin, out):
    levels, groups, height = edge_members.shape[1:4]
    rows = groups * height
    sides = sides_of(core[...], chip[...])
    parts = []
    for side, block in enumerate(sides):
        parts += [block[rows : 2 * rows], block[:rows], near[side].reshape(rows, LANES)]
    filtered = split(dot3(both(thin), split(jnp.concatenate(parts, axis=1))))
    for side, block in enumerate(sides):
        span = slice(3 * side * LANES, 3 * (side + 1) * LANES)
        order = (0, 1, 2) if side == 0 else (2, 1, 0)
        matrix = [jnp.concatenate([edge[i, k] for i in order], axis=0) for k in range(2)]
        beyond = dot3(tuple(x[:, span] for x in filtered), matrix)
        middle = slice(span.start + LANES, span.start + 2 * LANES)
        within = dot3(tuple(x[:, middle] for x in filtered), both(edge.at[order[0]]))
        lanes = pl.ds(side * LANES, LANES)
        out[:height, lanes] = beside_levels(edge_sums(edge_members[side], within))
        out[height:, lanes] = beside_levels(edge_sums(halo_members(block, rows, groups, levels), beyond))
    lane = lane_of(norm.shape)
    top = pl.ds(0, norm.shape[0])
    out[top, :LANES] = jnp.where(lane >= LANES - SPARE, norm[...], out[top, :LANES])


def weight_of(precision, covered):
    levels, height, width = precision.shape
    rows, blocks = covered.shape
    spread = lax.broadcasted_iota(jnp.int32, (blocks, width), 1) // (width // blocks)
    spread = (spread == lax.broadcasted_iota(jnp.int32, (blocks, width), 0)).astype(BF16)
    mask = jnp.dot(covered[...].astype(F32).astype(BF16), spread, preferred_element_type=F32)
    tall = height // rows
    mask = jnp.concatenate([jnp.broadcast_to(mask[i : i + 1], (tall, width)) for i in range(rows)], axis=0)
    return precision[...] * mask


def middle_kernel(
    i0, i1, i2, i3, e0, e1, e2, e3, obs_weight, core, chip, members_ref, edge_members, column, row, edge, thin,
    back, halo, weighted, sums, out,
):
    levels, height, width = obs_weight.shape
    groups = edge_members.shape[2]
    rows = groups * height
    flat = levels * height
    outer = (e0[...] + e1[...]) + (e2[...] + e3[...])
    out[...] = (i0[...] + i1[...]) + (i2[...] + i3[...])
    for side in range(2):
        add_edges(out, jnp.stack(apart_levels(outer[:height, side * LANES : (side + 1) * LANES], levels)), side)
    increment = out[...].reshape(levels, height, width)
    weighted[...] = obs_weight[...] * increment
    top = outer[: sums.shape[1], :LANES]
    sums[0] = jnp.where(lane_of(top.shape) >= LANES - SPARE, top, 0.0)
    sums[1] = folded(weighted[...] * increment)
    back[...] = adjoint(members_ref, weighted)
    smoothed = own_columns(back, column, row)
    for side, block in enumerate(sides_of(core[...], chip[...])):
        here = outer[height:, side * LANES : (side + 1) * LANES] * block[(2 + levels) * rows :]
        members = halo_members(block, rows, groups, levels)
        adjoint_here = jnp.zeros((groups, height, LANES), F32)
        for v, level in enumerate(apart_levels(here, levels)):
            adjoint_here = adjoint_here + members[v] * level
        halo[side] = adjoint_here
    filtered = split(dot3(both(thin), split(jnp.concatenate([halo[i].reshape(rows, LANES) for i in range(2)], axis=1))))
    out[...] = increments(members_ref, smoothed).reshape(flat, width)
    for side in range(2):
        part = dot3(tuple(x[:, side * LANES : (side + 1) * LANES] for x in filtered), both(edge.at[side]))
        add_edges(out, edge_sums(edge_members[side], part), side)


def wide_filter_kernel(back, halo, column, row, out):
    lhs = split(beside(back[...], halo[0], halo[1], EDGE))
    out[...] = dot3(both(row), split(dot3(lhs, both(column)))).reshape(out.shape)


def filter_kernel(back, core, chip, column, row, out):
    groups, height = back.shape[0] * EDGE // LANES, back.shape[1]
    left, right = sides_of(*(x[: groups * height].reshape(groups, height, LANES) for x in (core, chip)))
    lhs = split(beside(back[...], left, right, EDGE))
    out[...] = dot3(both(row), split(dot3(lhs, both(column)))).reshape(out.shape)


def last_kernel(i0, i1, i2, i3, obs_weight, before, sums, members_ref, back, to_core, to_chip):
    levels, height, width = obs_weight.shape
    increment = ((i0[...] + i1[...]) + (i2[...] + i3[...])).reshape(obs_weight.shape)
    weighted = obs_weight[...] * increment
    four = [sums[0], sums[1], folded(before[...] * increment), folded(weighted * increment)]
    row = lax.broadcasted_iota(jnp.int32, (8, LANES), 0)
    stacked = jnp.zeros((8, LANES), F32)
    for i, part in enumerate(four):
        stacked = jnp.where(row == i, jnp.sum(part, axis=0, keepdims=True), stacked)
    back[...] = adjoint(members_ref, weighted)
    odd = lax.axis_index("tile") % 2 == 1
    first, last = pack_edges(back, EDGE, True), pack_edges(back, EDGE, False)
    rows = first.shape[0] * height
    to_core[:rows] = jnp.where(odd, first, last).reshape(rows, LANES)
    to_core[rows:] = stacked
    to_chip[...] = jnp.where(odd, last, first).reshape(rows, LANES)


def copy_kernel(value, after, out):
    out[...] = value[...]


def pass_kernel(value, after, out):
    pass


def combine_kernel(own, other, source, first, second, weights, residual, held_weights, held_residual, sems):
    total = jnp.sum(own[...] + other[...], axis=1, keepdims=True)
    bb, bg, gg, gh = (total[i : i + 1] for i in range(4))
    bg, gg, gh = bg / bb, gg / bb, gh / bb
    q = 1.0 / (1.0 + bg)
    p = bg * q
    ratio = (gg - bg * bg) * q * q
    d = p + ratio
    square = d * d - 2.0 * d * q * bg + q * q * gg
    image = d * d * bg - 2.0 * d * q * gg + q * q * gh
    step = ratio / (square + image)
    members = source.shape[0]
    pieces = sems.shape[1]
    copies = []
    for i in range(pieces):
        part = pl.ds(i * (members // pieces), members // pieces)
        b, g, h = source[part], first[part], second[part]
        held_weights[part] = (q + step * d) * b - (step * q) * g
        held_residual[part] = (p - step * d) * b + (step * q - q - step * d) * g + (step * q) * h
        for k, (held, out) in enumerate(((held_weights, weights), (held_residual, residual))):
            copies.append(pltpu.make_async_copy(held.at[part], out.at[part], sems.at[k, i]))
            copies[-1].start()
    for copy in copies:
        copy.wait()


def call(kernel, outs, *operands, cost=None):
    shapes = [jax.ShapeDtypeStruct(shape, F32) for shape in outs]
    vmem = pl.BlockSpec(memory_space=pltpu.VMEM)
    return pl.pallas_call(
        kernel,
        out_shape=shapes,
        in_specs=[vmem] * len(operands),
        out_specs=[vmem] * len(outs),
        compiler_params=pltpu.CompilerParams(vmem_limit_bytes=24 * 1024 * 1024),
        cost_estimate=cost,
    )(*operands)


def passed(value, after):
    vmem = pl.BlockSpec(memory_space=pltpu.VMEM)
    return pl.pallas_call(
        pass_kernel,
        out_shape=pltpu.VMEM(value.shape, value.dtype),
        in_specs=[vmem] * 2,
        out_specs=vmem,
        input_output_aliases={0: 0},
        compiler_params=pltpu.CompilerParams(vmem_limit_bytes=24 * 1024 * 1024),
        cost_estimate=LONG,
    )(value, after)


def in_hbm(array):
    return pltpu.with_memory_space_constraint(array, pltpu.HBM)


def held_edges(source, members_data, precision, covered):
    members, levels, height, width = members_data.shape
    groups = members * EDGE // LANES
    payload = ((groups * (2 + levels) + 1) * height, LANES)
    vmem = pl.BlockSpec(memory_space=pltpu.VMEM)
    hbm = pl.BlockSpec(memory_space=pltpu.HBM)
    arrays = (source, members_data, precision, covered)
    return pl.pallas_call(
        edges_kernel,
        out_shape=[
            pltpu.VMEM(source.shape, F32),
            pltpu.VMEM(members_data.shape, members_data.dtype),
            pltpu.VMEM(precision.shape, F32),
            pltpu.VMEM((2, groups, height, LANES), F32),
            pltpu.VMEM((2, levels, groups, height, LANES), F32),
            pltpu.VMEM(payload, F32),
            pltpu.VMEM(payload, F32),
        ],
        in_specs=[hbm] * 4,
        out_specs=[vmem] * 7,
        scratch_shapes=[
            pltpu.VMEM(precision.shape, F32),
            pltpu.VMEM(covered.shape, covered.dtype),
            pltpu.SemaphoreType.DMA((4,)),
        ],
        compiler_params=pltpu.CompilerParams(vmem_limit_bytes=24 * 1024 * 1024),
    )(*map(in_hbm, arrays))


def first_increment(source, after, members_data):
    members, levels, height, width = members_data.shape
    groups = members * EDGE // LANES
    vmem = pl.BlockSpec(memory_space=pltpu.VMEM)
    return pl.pallas_call(
        first_kernel,
        out_shape=[
            pltpu.VMEM((levels * height, width), F32),
            pltpu.VMEM((8, LANES), F32),
            pltpu.VMEM((3, 2, LANES, LANES), BF16),
            pltpu.VMEM((2, groups * height, groups * height), BF16),
        ],
        in_specs=[vmem] * 3,
        out_specs=[vmem] * 4,
        compiler_params=pltpu.CompilerParams(vmem_limit_bytes=24 * 1024 * 1024),
        cost_estimate=LONG,
    )(source, after, members_data)


def fetched(after, *arrays):
    vmem = pl.BlockSpec(memory_space=pltpu.VMEM)
    hbm = pl.BlockSpec(memory_space=pltpu.HBM)
    size = sum(a.size * a.dtype.itemsize for a in arrays)
    return pl.pallas_call(
        fetch_kernel,
        out_shape=[pltpu.VMEM(a.shape, a.dtype) for a in arrays],
        in_specs=[vmem] + [hbm] * len(arrays),
        out_specs=[vmem] * len(arrays),
        scratch_shapes=[pltpu.SemaphoreType.DMA((len(arrays),))],
        compiler_params=pltpu.CompilerParams(vmem_limit_bytes=24 * 1024 * 1024),
        cost_estimate=pl.CostEstimate(flops=0, bytes_accessed=2 * size, transcendentals=0),
    )(after, *map(in_hbm, arrays))


def combined(own, other, source, first, second):
    vmem = pl.BlockSpec(memory_space=pltpu.VMEM)
    hbm = pl.BlockSpec(memory_space=pltpu.HBM)
    return pl.pallas_call(
        combine_kernel,
        out_shape=[jax.ShapeDtypeStruct(source.shape, F32)] * 2,
        in_specs=[vmem] * 5,
        out_specs=[hbm] * 2,
        scratch_shapes=[pltpu.VMEM(source.shape, F32)] * 2 + [pltpu.SemaphoreType.DMA((2, 4))],
        compiler_params=pltpu.CompilerParams(vmem_limit_bytes=24 * 1024 * 1024),
    )(own, other, source, first, second)


def from_both_sides(to_next, to_previous, axis):
    count = lax.axis_size(axis)
    left = lax.ppermute(to_next, axis, [(i, (i + 1) % count) for i in range(count)])
    right = lax.ppermute(to_previous, axis, [((i + 1) % count, i) for i in range(count)])
    return left, right


def from_tile(value, bit):
    count = lax.axis_size("tile")
    return lax.ppermute(value, "tile", [(i, i ^ bit) for i in range(count)])


def from_core(value):
    return from_tile(value, 1)


def from_chip(value):
    count = lax.axis_size("tile")
    return lax.ppermute(value, "tile", [(i, (i + 1) % count if i % 2 else (i - 1) % count) for i in range(count)])


def from_all(value, axis):
    count = lax.axis_size(axis)
    return [value] + [lax.ppermute(value, axis, [(i, i ^ k) for i in range(count)]) for k in range(1, count)]


def one_tile_row(right_side, perturbations, precision, covered):
    source, members_data = right_side[0], perturbations[0]
    members, levels, height, width = members_data.shape
    groups = members * EDGE // LANES
    taps = taps_np()
    twice = np.convolve(taps, taps)
    field = (members, height, width)
    plane = (levels, height, width)
    flat = (levels * height, width)
    row = halves(row_matrix(taps, height, members, 1))
    own = np.arange(width)

    source, members_data, obs_weight, near, edge_members, to_core, to_chip = held_edges(
        source, members_data, precision[0], covered[0]
    )
    core, chip = from_core(to_core), from_chip(to_chip)
    inside, norm, edge, thin = first_increment(source, to_core, members_data)
    parts = from_all(inside, "mem")
    (outer,) = call(edge_kernel, [(2 * height, 2 * LANES)], norm, core, chip, near, edge_members, edge, thin)
    parts += from_all(outer, "mem")
    column, row, column_twice, row_twice, edge, thin = fetched(
        outer, halves(column_matrix(taps, width, EDGE)), row,
        halves(band(twice, own, own)), halves(row_matrix(taps, height, members, 2)),
        edge_matrix(twice, EDGE), halves(row_matrix(taps, height, groups, 2)),
    )
    back, halo, weighted, sums, increment = call(
        middle_kernel,
        [field, (2, groups, height, LANES), plane, (2, 8, LANES), flat],
        *parts, obs_weight, core, chip, members_data, edge_members, column_twice, row_twice, edge, thin,
    )
    parts = from_all(increment, "mem")
    (first,) = call(wide_filter_kernel, [field], back, halo, column, row, cost=LONG)
    first, weighted = lax.optimization_barrier((first, weighted))
    back, to_core, to_chip = call(
        last_kernel,
        [field, (groups * height + 8, LANES), (groups * height, LANES)],
        *parts, obs_weight, weighted, sums, members_data,
    )
    core = from_core(to_core)
    sums = to_core[groups * height :] + core[groups * height :]
    (to_chip,) = call(copy_kernel, [to_chip.shape], to_chip, sums)
    chip = from_chip(to_chip)
    first = passed(first, sums)
    sums = sums + from_tile(sums, 2)
    others = from_tile(sums, 4)
    (second,) = call(filter_kernel, [field], back, core, chip, column, row, cost=LONG)
    weights, residual = combined(sums, others, source, first, second)
    return weights[None], residual[None]


def passed_along(value, axis, steps):
    count = lax.axis_size(axis)
    first, last = (max(0, -steps), min(count, count - steps))
    return lax.ppermute(value, axis, [(source, source + steps) for source in range(first, last)])


def smooth(field):
    taps = taps_np().astype(np.float32)
    height, width = field.shape[1:]
    above = passed_along(field[:, height - REACH :, :], "tile", TCOLS)
    below = passed_along(field[:, :REACH, :], "tile", -TCOLS)
    padded = jnp.concatenate([above, field, below], axis=1)
    along = sum(taps[j] * padded[:, j : j + height, :] for j in range(2 * REACH + 1))
    left, right = from_both_sides(along[:, :, width - REACH :], along[:, :, :REACH], "tile")
    sided = jnp.concatenate([left, along, right], axis=2)
    return sum(taps[j] * sided[:, :, j : j + width] for j in range(2 * REACH + 1))


def several_tile_rows(right_side, perturbations, precision, covered):
    source = right_side[0]
    members_data = perturbations[0].astype(F32)
    levels, height, width = precision.shape[1:]
    rows, blocks = covered.shape[1:]
    mask = covered[0].astype(F32)
    obs_weight = (
        precision[0].reshape(levels, rows, height // rows, blocks, width // blocks) * mask[None, :, None, :, None]
    ).reshape(levels, height, width)

    def operator(direction):
        partial_terms = jnp.einsum("kvyx,kyx->vyx", members_data, smooth(direction))
        weighted = obs_weight * lax.psum(partial_terms, "mem")
        return direction + smooth(jnp.einsum("kvyx,vyx->kyx", members_data, weighted))

    weights = jnp.zeros_like(source)
    residual = direction = source
    norm_now = lax.psum(jnp.sum(source * source), ("tile", "mem"))
    for step in range(ITERS):
        image = operator(direction)
        length = norm_now / lax.psum(jnp.sum(direction * image), ("tile", "mem"))
        weights = weights + length * direction
        residual = residual - length * image
        if step + 1 < ITERS:
            norm_next = lax.psum(jnp.sum(residual * residual), ("tile", "mem"))
            direction = residual + norm_next / norm_now * direction
            norm_now = norm_next
    return weights[None], residual[None]


def solution(mesh):
    single = mesh.shape["tile"] == TCOLS and mesh.shape["mem"] == 4
    local = one_tile_row if single else several_tile_rows
    return jax.shard_map(
        local,
        mesh=mesh,
        in_specs=(
            P("tile", "mem", None, None),
            P("tile", "mem", None, None, None),
            P("tile", None, None, None),
            P("tile", None, None),
        ),
        out_specs=(P("tile", "mem", None, None), P("tile", "mem", None, None)),
        check_vma=False,
    )
```

```python
import functools

import jax
import jax.numpy as jnp
import ml_dtypes
import numpy as np
from jax import lax
from jax.experimental import pallas as pl
from jax.experimental.pallas import tpu as pltpu
from jax.sharding import PartitionSpec as P

ITERS = 2
TCOLS = 8
REACH = 8
EDGE = 2 * REACH
SPARE = 32
LANES = 128
F32 = jnp.float32
BF16 = jnp.bfloat16
LONG = pl.CostEstimate(flops=10**9, bytes_accessed=10**6, transcendentals=0)


def taps_np():
    offsets = np.arange(-REACH, REACH + 1, dtype=np.float64)
    raw = np.exp(-offsets * offsets / 32.0)
    return raw / np.sqrt(np.sum(np.exp(-offsets * offsets / 16.0)))


def band(taps, source, target):
    reach = (len(taps) - 1) // 2
    gap = source[:, None] - target[None, :]
    inside = np.abs(gap) <= reach
    return np.where(inside, taps[np.clip(gap + reach, 0, 2 * reach)], 0.0)


def halves(matrix):
    whole = matrix.astype(np.float32)
    high = whole.astype(ml_dtypes.bfloat16)
    low = (whole - high.astype(np.float32)).astype(ml_dtypes.bfloat16)
    return np.stack([high, low])


def column_matrix(taps, width, edge):
    target = np.arange(width)
    slots = LANES // edge
    left = np.tile(np.arange(edge) - edge, slots)
    right = np.tile(np.arange(edge) + width, slots)
    return np.concatenate([band(taps, s, target) for s in (np.arange(width), left, right)])


def row_matrix(taps, height, members, times):
    one = band(taps, np.arange(height), np.arange(height))
    return np.kron(np.eye(members), np.linalg.matrix_power(one, times))


def edge_matrix(taps, edge):
    inner = np.arange(edge)
    return np.stack(
        [halves(np.kron(np.eye(LANES // edge), band(taps, inner + shift * edge, inner))) for shift in (-1, 0, 1)]
    )


def split(x):
    high = x.astype(BF16)
    return high, (x - high.astype(F32)).astype(BF16)


def dot3(left, right):
    mul = functools.partial(jnp.dot, preferred_element_type=F32)
    return mul(left[0], right[0]) + (mul(left[1], right[0]) + mul(left[0], right[1]))


def both(ref):
    return ref[0], ref[1]


def lane_of(shape):
    return lax.broadcasted_iota(jnp.int32, shape, len(shape) - 1)


def pack_columns(field, start, edge):
    members, rows, _ = field.shape
    slots = LANES // edge
    groups = members // slots
    lane = lane_of((rows, LANES))
    origin = start // LANES * LANES
    out = []
    for g in range(groups):
        total = jnp.zeros((rows, LANES), F32)
        for j in range(slots):
            block = field[j * groups + g][:, origin : origin + LANES]
            shift = (j * edge - (start - origin)) % LANES
            moved = pltpu.roll(block, shift, 1) if shift else block
            total = jnp.where((lane >= j * edge) & (lane < (j + 1) * edge), moved, total)
        out.append(total)
    return jnp.stack(out)


def pack_edges(field, edge, first):
    return pack_columns(field, 0 if first else field.shape[-1] - edge, edge)


def repeated(x, period):
    while period < LANES:
        x = x + pltpu.roll(x, period, len(x.shape) - 1)
        period *= 2
    return x


def level_lanes(shape, level):
    lane = lane_of(shape)
    return (lane >= level * EDGE) & (lane < (level + 1) * EDGE)


def sides_of(core, chip):
    odd = lax.axis_index("tile") % 2 == 1
    return jnp.where(odd, core, chip), jnp.where(odd, chip, core)


def spread_edges(packed, edge):
    groups, rows, _ = packed.shape
    slots = LANES // edge
    lane = lane_of((groups, rows, LANES))
    parts = [jnp.where((lane >= j * edge) & (lane < (j + 1) * edge), packed, 0.0) for j in range(slots)]
    return jnp.concatenate(parts, axis=0).reshape(slots * groups * rows, LANES)


def beside(field, left, right, edge):
    members, rows, width = field.shape
    return jnp.concatenate(
        [field.reshape(members * rows, width), spread_edges(left, edge), spread_edges(right, edge)], axis=1
    )


def increments(members_ref, smoothed):
    members, levels = members_ref.shape[:2]
    totals = []
    for v in range(levels):
        total = members_ref[0, v].astype(F32) * smoothed[0]
        for k in range(1, members):
            total = total + members_ref[k, v].astype(F32) * smoothed[k]
        totals.append(total)
    return jnp.stack(totals)


def adjoint(members_ref, weighted):
    members, levels = members_ref.shape[:2]
    back = []
    for k in range(members):
        total = members_ref[k, 0].astype(F32) * weighted[0]
        for v in range(1, levels):
            total = total + members_ref[k, v].astype(F32) * weighted[v]
        back.append(total)
    return jnp.stack(back)


def folded(x):
    width = x.shape[-1]
    x = x.reshape(-1, 8, width).sum(axis=0)
    return sum(x[:, i : i + LANES] for i in range(0, width, LANES))


def edges_kernel(
    source_hbm, members_hbm, precision_hbm, covered_hbm,
    source, members_ref, obs_weight, near, near_weight, edge_members, to_core, to_chip, precision, covered, sems,
):
    members, levels, height, width = members_ref.shape
    pairs = ((source_hbm, source), (precision_hbm, precision), (covered_hbm, covered), (members_hbm, members_ref))
    copies = [pltpu.make_async_copy(x, y, sems.at[i]) for i, (x, y) in enumerate(pairs)]
    for copy in copies:
        copy.start()
    groups = members * EDGE // LANES
    odd = lax.axis_index("tile") % 2 == 1
    rows = groups * height

    def send(at, first, last):
        first, last = (x.reshape(-1, LANES) for x in (first, last))
        part = pl.ds(at, first.shape[0])
        to_core[part] = jnp.where(odd, first, last)
        to_chip[part] = jnp.where(odd, last, first)

    copies[0].wait()
    near[0], near[1] = pack_columns(source, 0, EDGE), pack_columns(source, width - EDGE, EDGE)
    send(0, near[0], near[1])
    send(rows, pack_columns(source, EDGE, EDGE), pack_columns(source, width - 2 * EDGE, EDGE))
    copies[1].wait()
    copies[2].wait()
    obs_weight[...] = weight_of(precision, covered)
    for side, start in enumerate((0, width - EDGE)):
        total = jnp.zeros((height, LANES), F32)
        for v in range(levels):
            origin = start // LANES * LANES
            shift = (v * EDGE - (start - origin)) % LANES
            block = obs_weight[v, :, origin : origin + LANES]
            total = jnp.where(level_lanes(total.shape, v), pltpu.roll(block, shift, 1) if shift else block, total)
        near_weight[side] = total
    send(rows * (2 + levels), near_weight[0], near_weight[1])
    copies[3].wait()
    for v in range(levels):
        level = members_ref[:, v].astype(F32)
        edge_members[0, v], edge_members[1, v] = pack_edges(level, EDGE, True), pack_edges(level, EDGE, False)
        send(rows * (2 + v), edge_members[0, v], edge_members[1, v])


def own_columns(field, column, row):
    members, height, width = field.shape
    lhs = split(field[...].reshape(members * height, width))
    return dot3(both(row), split(dot3(lhs, both(column)))).reshape(field.shape)


def tap_at(gap, inside):
    scale = 1.0 / np.sqrt(np.sum(np.exp(-(np.arange(-REACH, REACH + 1.0) ** 2) / 16.0)))
    square = (gap * gap).astype(F32)
    return jnp.where(inside & (jnp.abs(gap) <= REACH), jnp.exp(square * (-1.0 / 32.0)) * scale, 0.0)


def gaps(rows, columns):
    shape = (rows, columns)
    down, across = (lax.broadcasted_iota(jnp.int32, shape, i) for i in range(2))
    return down, across, down - across


def kept(ref, matrix):
    ref[0], ref[1] = split(matrix)


def first_kernel(source, after, members_ref, increment, norm, edge, thin):
    members, levels, height, width = members_ref.shape
    _, _, gap = gaps(width, width)
    column = split(tap_at(gap, True))
    down, across, gap = gaps(members * height, members * height)
    row = split(tap_at(gap, down // height == across // height))
    lhs = split(source[...].reshape(members * height, width))
    smoothed = dot3(row, split(dot3(lhs, column))).reshape(source.shape)
    increment[...] = increments(members_ref, smoothed).reshape(levels * height, width)
    norm[...] = repeated(folded(source[...] * source[...]), SPARE)
    down, across, gap = gaps(LANES, LANES)
    same = down // EDGE == across // EDGE
    for i in range(3):
        kept(edge.at[i], tap_at(gap + (i - 1) * EDGE, same))
    down, across, gap = gaps(*thin.shape[1:])
    kept(thin, tap_at(gap, down // height == across // height))


def edge_sums(edge_members, smoothed):
    groups, height = edge_members.shape[1:3]
    return repeated(jnp.sum(edge_members * smoothed.reshape(1, groups, height, LANES), axis=1), EDGE)


def add_columns(out, start, blocks):
    levels, height, _ = blocks[0].shape
    origin = start // LANES * LANES
    lane = lane_of(blocks[0].shape)
    total = jnp.zeros(lane.shape, F32)
    for i, block in enumerate(blocks):
        first = start - origin + i * EDGE
        total = jnp.where((lane >= first) & (lane < first + EDGE), block, total)
    rows, span = pl.ds(0, levels * height), pl.ds(origin, LANES)
    out[rows, span] = out[rows, span] + total.reshape(levels * height, LANES)


def beside_levels(sums):
    total = jnp.zeros(sums.shape[1:], F32)
    for v in range(sums.shape[0]):
        total = jnp.where(level_lanes(total.shape, v), sums[v], total)
    return total


def apart_levels(packed, levels):
    return [repeated(jnp.where(level_lanes(packed.shape, v), packed, 0.0), EDGE) for v in range(levels)]


def halo_members(block, rows, groups, levels):
    height = rows // groups
    return block[2 * rows : (2 + levels) * rows].reshape(levels, groups, height, LANES)


def edge_kernel(norm, chip, core, near, edge_members, edge, thin, out):
    levels, groups, height = edge_members.shape[1:4]
    rows = groups * height
    sides = sides_of(core[...], chip[...])
    parts = []
    for side, block in enumerate(sides):
        here = [block[rows : 2 * rows], block[:rows], near[side].reshape(rows, LANES)]
        parts += here if side == 0 else here[::-1]
    filtered = dot3(both(thin), split(jnp.concatenate(parts, axis=1)))
    filtered = split(jnp.concatenate([filtered[:, : 3 * LANES], filtered[:, 3 * LANES :]], axis=0))
    beyond = dot3(filtered, [jnp.concatenate([edge[i, k] for i in range(3)], axis=0) for k in range(2)])
    middle = tuple(x[:, LANES : 2 * LANES] for x in filtered)
    for side, block in enumerate(sides):
        own = slice(side * rows, (side + 1) * rows)
        within = dot3(tuple(x[own] for x in middle), both(edge.at[2 * side]))
        lanes = pl.ds(side * LANES, LANES)
        out[:height, lanes] = beside_levels(edge_sums(edge_members[side], within))
        out[height:, lanes] = beside_levels(edge_sums(halo_members(block, rows, groups, levels), beyond[own]))
    lane = lane_of(norm.shape)
    top = pl.ds(0, norm.shape[0])
    out[top, :LANES] = jnp.where(lane >= LANES - SPARE, norm[...], out[top, :LANES])


def weight_of(precision, covered):
    levels, height, width = precision.shape
    rows, blocks = covered.shape
    spread = lax.broadcasted_iota(jnp.int32, (blocks, width), 1) // (width // blocks)
    spread = (spread == lax.broadcasted_iota(jnp.int32, (blocks, width), 0)).astype(BF16)
    mask = jnp.dot(covered[...].astype(F32).astype(BF16), spread, preferred_element_type=F32)
    tall = height // rows
    mask = jnp.concatenate([jnp.broadcast_to(mask[i : i + 1], (tall, width)) for i in range(rows)], axis=0)
    return precision[...] * mask


def packed_adjoint(members, weighted):
    total = jnp.zeros(members.shape[1:], F32)
    for v, level in enumerate(apart_levels(weighted, members.shape[0])):
        total = total + members[v] * level
    return total


def prepare_kernel(
    after, members_ref, column_hbm, row_hbm, edge_hbm, thin_hbm, next_members, column, row, edge, thin, sems
):
    pairs = ((column_hbm, column), (row_hbm, row), (edge_hbm, edge), (thin_hbm, thin))
    copies = [pltpu.make_async_copy(x, y, sems.at[i]) for i, (x, y) in enumerate(pairs)]
    for copy in copies:
        copy.start()
    levels, width = members_ref.shape[1], members_ref.shape[-1]
    for v in range(levels):
        level = members_ref[:, v].astype(F32)
        next_members[0, v] = pack_columns(level, EDGE, EDGE)
        next_members[1, v] = pack_columns(level, width - 2 * EDGE, EDGE)
    for copy in copies:
        copy.wait()


def main_kernel(i0, i1, i2, i3, obs_weight, members_ref, column, row, first, back, second):
    first[...] = (i0[...] + i1[...]) + (i2[...] + i3[...])
    back[...] = adjoint(members_ref, obs_weight[...] * first[...].reshape(obs_weight.shape))
    second[...] = increments(members_ref, own_columns(back, column, row)).reshape(second.shape)


def correction_kernel(
    e0, e1, e2, e3, main, near_weight, chip, core, edge_members, next_members, edge, thin, outer, own, halo, out
):
    levels, groups, height = edge_members.shape[1:4]
    width = out.shape[-1]
    rows = groups * height
    outer[...] = (e0[...] + e1[...]) + (e2[...] + e3[...])
    out[...] = main[...]
    for side, block in enumerate(sides_of(core[...], chip[...])):
        lanes = pl.ds(side * LANES, LANES)
        own[side] = packed_adjoint(edge_members[side], outer[:height, lanes] * near_weight[side])
        halo[side] = packed_adjoint(
            halo_members(block, rows, groups, levels), outer[height:, lanes] * block[(2 + levels) * rows :]
        )
    parts = [x[side].reshape(rows, LANES) for side in range(2) for x in (halo, own)]
    filtered = split(dot3(both(thin), split(jnp.concatenate(parts, axis=1))))
    for side in range(2):
        span = slice(2 * side * LANES, 2 * (side + 1) * LANES)
        matrix = [jnp.concatenate([edge[2 * side, k], edge[1, k]], axis=0) for k in range(2)]
        outermost = dot3(tuple(x[:, span] for x in filtered), matrix)
        inner = dot3(tuple(x[:, span.start + LANES : span.stop] for x in filtered), both(edge.at[2 * side]))
        blocks = [edge_sums(edge_members[side], outermost), edge_sums(next_members[side], inner)]
        if side == 0:
            add_columns(out, 0, blocks)
        else:
            add_columns(out, width - 2 * EDGE, blocks[::-1])


def wide_filter_kernel(
    main, own, halo, first, outer, obs_weight, column_hbm, row_hbm, weighted, sums, out, column, row, sems
):
    copies = [pltpu.make_async_copy(x, y, sems.at[i]) for i, (x, y) in enumerate(((column_hbm, column), (row_hbm, row)))]
    for copy in copies:
        copy.start()
    levels, height, width = obs_weight.shape
    weighted[...] = first[...].reshape(obs_weight.shape)
    for side, start in enumerate((0, width - EDGE)):
        origin = start // LANES * LANES
        lane = lane_of((height, LANES))
        mask = (lane >= start - origin) & (lane < start - origin + EDGE)
        for v, level in enumerate(apart_levels(outer[:height, pl.ds(side * LANES, LANES)], levels)):
            span = pl.ds(origin, LANES)
            weighted[v, :, span] = weighted[v, :, span] + jnp.where(mask, level, 0.0)
    increment = weighted[...]
    weighted[...] = obs_weight[...] * increment
    top = outer[: sums.shape[1], :LANES]
    sums[0] = jnp.where(lane_of(top.shape) >= LANES - SPARE, top, 0.0)
    sums[1] = folded(weighted[...] * increment)
    groups = own.shape[1]
    fields = []
    for k in range(main.shape[0]):
        field = main[k]
        slot, group = k // groups, k % groups
        ends = []
        for side, at in enumerate((0, LANES - EDGE)):
            moved = pltpu.roll(own[side, group], (at - slot * EDGE) % LANES, 1)
            lane = lane_of(moved.shape)
            ends.append(jnp.where((lane >= at) & (lane < at + EDGE), moved, 0.0))
        middle = [jnp.zeros((height, width - 2 * LANES), F32)] if width > 2 * LANES else []
        fields.append(field + jnp.concatenate([ends[0]] + middle + [ends[1]], axis=1))
    for copy in copies:
        copy.wait()
    lhs = split(beside(jnp.stack(fields), halo[0], halo[1], EDGE))
    out[...] = dot3(both(row), split(dot3(lhs, both(column)))).reshape(out.shape)


def filter_kernel(back, core, chip, column, row, out):
    groups, height = back.shape[0] * EDGE // LANES, back.shape[1]
    left, right = sides_of(*(x[: groups * height].reshape(groups, height, LANES) for x in (core, chip)))
    lhs = split(beside(back[...], left, right, EDGE))
    out[...] = dot3(both(row), split(dot3(lhs, both(column)))).reshape(out.shape)


def last_kernel(i0, i1, i2, i3, obs_weight, before, sums, members_ref, back, to_core, to_chip):
    levels, height, width = obs_weight.shape
    increment = ((i0[...] + i1[...]) + (i2[...] + i3[...])).reshape(obs_weight.shape)
    weighted = obs_weight[...] * increment
    four = [sums[0], sums[1], folded(before[...] * increment), folded(weighted * increment)]
    row = lax.broadcasted_iota(jnp.int32, (8, LANES), 0)
    stacked = jnp.zeros((8, LANES), F32)
    for i, part in enumerate(four):
        stacked = jnp.where(row == i, jnp.sum(part, axis=0, keepdims=True), stacked)
    back[...] = adjoint(members_ref, weighted)
    odd = lax.axis_index("tile") % 2 == 1
    first, last = pack_edges(back, EDGE, True), pack_edges(back, EDGE, False)
    rows = first.shape[0] * height
    to_core[:rows] = jnp.where(odd, first, last).reshape(rows, LANES)
    to_core[rows:] = stacked
    to_chip[...] = jnp.where(odd, last, first).reshape(rows, LANES)


def copy_kernel(value, after, out):
    out[...] = value[...]


def pass_kernel(value, after, out):
    pass


def combine_kernel(own, other, source, first, second, weights, residual, held_weights, held_residual, sems):
    total = jnp.sum(own[...] + other[...], axis=1, keepdims=True)
    bb, bg, gg, gh = (total[i : i + 1] for i in range(4))
    bg, gg, gh = bg / bb, gg / bb, gh / bb
    q = 1.0 / (1.0 + bg)
    p = bg * q
    ratio = (gg - bg * bg) * q * q
    d = p + ratio
    square = d * d - 2.0 * d * q * bg + q * q * gg
    image = d * d * bg - 2.0 * d * q * gg + q * q * gh
    step = ratio / (square + image)
    members = source.shape[0]
    pieces = sems.shape[1]
    copies = []
    for i in range(pieces):
        part = pl.ds(i * (members // pieces), members // pieces)
        b, g, h = source[part], first[part], second[part]
        held_weights[part] = (q + step * d) * b - (step * q) * g
        held_residual[part] = (p - step * d) * b + (step * q - q - step * d) * g + (step * q) * h
        for k, (held, out) in enumerate(((held_weights, weights), (held_residual, residual))):
            copies.append(pltpu.make_async_copy(held.at[part], out.at[part], sems.at[k, i]))
            copies[-1].start()
    for copy in copies:
        copy.wait()


def call(kernel, outs, *operands, cost=None):
    shapes = [jax.ShapeDtypeStruct(shape, F32) for shape in outs]
    vmem = pl.BlockSpec(memory_space=pltpu.VMEM)
    return pl.pallas_call(
        kernel,
        out_shape=shapes,
        in_specs=[vmem] * len(operands),
        out_specs=[vmem] * len(outs),
        compiler_params=pltpu.CompilerParams(vmem_limit_bytes=24 * 1024 * 1024),
        cost_estimate=cost,
    )(*operands)


def passed(value, after):
    vmem = pl.BlockSpec(memory_space=pltpu.VMEM)
    return pl.pallas_call(
        pass_kernel,
        out_shape=pltpu.VMEM(value.shape, value.dtype),
        in_specs=[vmem] * 2,
        out_specs=vmem,
        input_output_aliases={0: 0},
        compiler_params=pltpu.CompilerParams(vmem_limit_bytes=24 * 1024 * 1024),
        cost_estimate=LONG,
    )(value, after)


def in_hbm(array):
    return pltpu.with_memory_space_constraint(array, pltpu.HBM)


def held_edges(source, members_data, precision, covered):
    members, levels, height, width = members_data.shape
    groups = members * EDGE // LANES
    payload = ((groups * (2 + levels) + 1) * height, LANES)
    vmem = pl.BlockSpec(memory_space=pltpu.VMEM)
    hbm = pl.BlockSpec(memory_space=pltpu.HBM)
    arrays = (source, members_data, precision, covered)
    return pl.pallas_call(
        edges_kernel,
        out_shape=[
            pltpu.VMEM(source.shape, F32),
            pltpu.VMEM(members_data.shape, members_data.dtype),
            pltpu.VMEM(precision.shape, F32),
            pltpu.VMEM((2, groups, height, LANES), F32),
            pltpu.VMEM((2, height, LANES), F32),
            pltpu.VMEM((2, levels, groups, height, LANES), F32),
            pltpu.VMEM(payload, F32),
            pltpu.VMEM(payload, F32),
        ],
        in_specs=[hbm] * 4,
        out_specs=[vmem] * 8,
        scratch_shapes=[
            pltpu.VMEM(precision.shape, F32),
            pltpu.VMEM(covered.shape, covered.dtype),
            pltpu.SemaphoreType.DMA((4,)),
        ],
        compiler_params=pltpu.CompilerParams(vmem_limit_bytes=24 * 1024 * 1024),
    )(*map(in_hbm, arrays))


def first_increment(source, after, members_data):
    members, levels, height, width = members_data.shape
    groups = members * EDGE // LANES
    vmem = pl.BlockSpec(memory_space=pltpu.VMEM)
    return pl.pallas_call(
        first_kernel,
        out_shape=[
            pltpu.VMEM((levels * height, width), F32),
            pltpu.VMEM((8, LANES), F32),
            pltpu.VMEM((3, 2, LANES, LANES), BF16),
            pltpu.VMEM((2, groups * height, groups * height), BF16),
        ],
        in_specs=[vmem] * 3,
        out_specs=[vmem] * 4,
        compiler_params=pltpu.CompilerParams(vmem_limit_bytes=24 * 1024 * 1024),
        cost_estimate=LONG,
    )(source, after, members_data)


def call_with_constants(kernel, outs, kept, scratch, operands, constants):
    vmem = pl.BlockSpec(memory_space=pltpu.VMEM)
    hbm = pl.BlockSpec(memory_space=pltpu.HBM)
    held = [pltpu.VMEM(x.shape, x.dtype) for x in kept]
    return pl.pallas_call(
        kernel,
        out_shape=[pltpu.VMEM(shape, F32) for shape in outs] + held,
        in_specs=[vmem] * len(operands) + [hbm] * len(constants),
        out_specs=[vmem] * (len(outs) + len(kept)),
        scratch_shapes=[pltpu.VMEM(x.shape, x.dtype) for x in scratch] + [pltpu.SemaphoreType.DMA((len(constants),))],
        compiler_params=pltpu.CompilerParams(vmem_limit_bytes=24 * 1024 * 1024),
        cost_estimate=LONG,
    )(*operands, *map(in_hbm, constants))


def combined(own, other, source, first, second):
    vmem = pl.BlockSpec(memory_space=pltpu.VMEM)
    hbm = pl.BlockSpec(memory_space=pltpu.HBM)
    return pl.pallas_call(
        combine_kernel,
        out_shape=[jax.ShapeDtypeStruct(source.shape, F32)] * 2,
        in_specs=[vmem] * 5,
        out_specs=[hbm] * 2,
        scratch_shapes=[pltpu.VMEM(source.shape, F32)] * 2 + [pltpu.SemaphoreType.DMA((2, 4))],
        compiler_params=pltpu.CompilerParams(vmem_limit_bytes=24 * 1024 * 1024),
    )(own, other, source, first, second)


def from_both_sides(to_next, to_previous, axis):
    count = lax.axis_size(axis)
    left = lax.ppermute(to_next, axis, [(i, (i + 1) % count) for i in range(count)])
    right = lax.ppermute(to_previous, axis, [((i + 1) % count, i) for i in range(count)])
    return left, right


def from_tile(value, bit):
    count = lax.axis_size("tile")
    return lax.ppermute(value, "tile", [(i, i ^ bit) for i in range(count)])


def from_core(value):
    return from_tile(value, 1)


def from_chip(value):
    count = lax.axis_size("tile")
    return lax.ppermute(value, "tile", [(i, (i + 1) % count if i % 2 else (i - 1) % count) for i in range(count)])


def from_all(value, axis, order):
    count = lax.axis_size(axis)
    return [value] + [lax.ppermute(value, axis, [(i, i ^ k) for i in range(count)]) for k in order]


def one_tile_row(right_side, perturbations, precision, covered):
    source, members_data = right_side[0], perturbations[0]
    members, levels, height, width = members_data.shape
    groups = members * EDGE // LANES
    taps = taps_np()
    twice = np.convolve(taps, taps)
    field = (members, height, width)
    plane = (levels, height, width)
    flat = (levels * height, width)
    own = np.arange(width)

    source, members_data, obs_weight, near, near_weight, edge_members, to_core, to_chip = held_edges(
        source, members_data, precision[0], covered[0]
    )
    core, chip = from_core(to_core), from_chip(to_chip)
    inside, norm, edge, thin = first_increment(source, to_chip, members_data)
    inside = from_all(inside, "mem", (3, 2, 1))
    (outer,) = call(edge_kernel, [(2 * height, 2 * LANES)], norm, chip, core, near, edge_members, edge, thin)
    column_twice, row_twice = halves(band(twice, own, own)), halves(row_matrix(taps, height, members, 2))
    edge, thin = edge_matrix(twice, EDGE), halves(row_matrix(taps, height, groups, 2))
    constants = [column_twice, row_twice, edge, thin]
    next_members, column, row, edge, thin = call_with_constants(
        prepare_kernel, [edge_members.shape], constants, [], [outer, members_data], constants
    )
    increment, main, inside = call(
        main_kernel, [flat, field, flat], *inside, obs_weight, members_data, column, row
    )
    ends = (2, groups, height, LANES)
    outer, corrected, halo, second = call(
        correction_kernel, [outer.shape, ends, ends, flat],
        *from_all(outer, "mem", (3, 2, 1)), inside, near_weight, chip, core, edge_members, next_members, edge, thin,
    )
    parts = from_all(second, "mem", (2, 1, 3))
    column, row = halves(column_matrix(taps, width, EDGE)), halves(row_matrix(taps, height, members, 1))
    weighted, sums, first, column, row = call_with_constants(
        wide_filter_kernel, [plane, (2, 8, LANES), field], [column, row], [],
        [main, corrected, halo, increment, outer, obs_weight], [column, row],
    )
    back, to_core, to_chip = call(
        last_kernel,
        [field, (groups * height + 8, LANES), (groups * height, LANES)],
        *parts, obs_weight, weighted, sums, members_data,
    )
    core = from_core(to_core)
    sums = to_core[groups * height :] + core[groups * height :]
    (to_chip,) = call(copy_kernel, [to_chip.shape], to_chip, sums)
    chip = from_chip(to_chip)
    first = passed(first, sums)
    sums = sums + from_tile(sums, 2)
    others = from_tile(sums, 4)
    (second,) = call(filter_kernel, [field], back, core, chip, column, row, cost=LONG)
    weights, residual = combined(sums, others, source, first, second)
    return weights[None], residual[None]


def passed_along(value, axis, steps):
    count = lax.axis_size(axis)
    first, last = (max(0, -steps), min(count, count - steps))
    return lax.ppermute(value, axis, [(source, source + steps) for source in range(first, last)])


def smooth(field):
    taps = taps_np().astype(np.float32)
    height, width = field.shape[1:]
    above = passed_along(field[:, height - REACH :, :], "tile", TCOLS)
    below = passed_along(field[:, :REACH, :], "tile", -TCOLS)
    padded = jnp.concatenate([above, field, below], axis=1)
    along = sum(taps[j] * padded[:, j : j + height, :] for j in range(2 * REACH + 1))
    left, right = from_both_sides(along[:, :, width - REACH :], along[:, :, :REACH], "tile")
    sided = jnp.concatenate([left, along, right], axis=2)
    return sum(taps[j] * sided[:, :, j : j + width] for j in range(2 * REACH + 1))


def several_tile_rows(right_side, perturbations, precision, covered):
    source = right_side[0]
    members_data = perturbations[0].astype(F32)
    levels, height, width = precision.shape[1:]
    rows, blocks = covered.shape[1:]
    mask = covered[0].astype(F32)
    obs_weight = (
        precision[0].reshape(levels, rows, height // rows, blocks, width // blocks) * mask[None, :, None, :, None]
    ).reshape(levels, height, width)

    def operator(direction):
        partial_terms = jnp.einsum("kvyx,kyx->vyx", members_data, smooth(direction))
        weighted = obs_weight * lax.psum(partial_terms, "mem")
        return direction + smooth(jnp.einsum("kvyx,vyx->kyx", members_data, weighted))

    weights = jnp.zeros_like(source)
    residual = direction = source
    norm_now = lax.psum(jnp.sum(source * source), ("tile", "mem"))
    for step in range(ITERS):
        image = operator(direction)
        length = norm_now / lax.psum(jnp.sum(direction * image), ("tile", "mem"))
        weights = weights + length * direction
        residual = residual - length * image
        if step + 1 < ITERS:
            norm_next = lax.psum(jnp.sum(residual * residual), ("tile", "mem"))
            direction = residual + norm_next / norm_now * direction
            norm_now = norm_next
    return weights[None], residual[None]


def solution(mesh):
    single = mesh.shape["tile"] == TCOLS and mesh.shape["mem"] == 4
    local = one_tile_row if single else several_tile_rows
    return jax.shard_map(
        local,
        mesh=mesh,
        in_specs=(
            P("tile", "mem", None, None),
            P("tile", "mem", None, None, None),
            P("tile", None, None, None),
            P("tile", None, None),
        ),
        out_specs=(P("tile", "mem", None, None), P("tile", "mem", None, None)),
        check_vma=False,
    )
```

```python
import functools

import jax
import jax.numpy as jnp
import ml_dtypes
import numpy as np
from jax import lax
from jax.experimental import pallas as pl
from jax.experimental.pallas import tpu as pltpu
from jax.sharding import PartitionSpec as P

ITERS = 2
TCOLS = 8
REACH = 8
EDGE = 2 * REACH
SPARE = 32
LANES = 128
F32 = jnp.float32
BF16 = jnp.bfloat16
LONG = pl.CostEstimate(flops=10**9, bytes_accessed=10**6, transcendentals=0)


def taps_np():
    offsets = np.arange(-REACH, REACH + 1, dtype=np.float64)
    raw = np.exp(-offsets * offsets / 32.0)
    return raw / np.sqrt(np.sum(np.exp(-offsets * offsets / 16.0)))


def band(taps, source, target):
    reach = (len(taps) - 1) // 2
    gap = source[:, None] - target[None, :]
    inside = np.abs(gap) <= reach
    return np.where(inside, taps[np.clip(gap + reach, 0, 2 * reach)], 0.0)


def halves(matrix):
    whole = matrix.astype(np.float32)
    high = whole.astype(ml_dtypes.bfloat16)
    low = (whole - high.astype(np.float32)).astype(ml_dtypes.bfloat16)
    return np.stack([high, low])


def column_matrix(taps, width, edge):
    target = np.arange(width)
    slots = LANES // edge
    left = np.tile(np.arange(edge) - edge, slots)
    right = np.tile(np.arange(edge) + width, slots)
    return np.concatenate([band(taps, s, target) for s in (np.arange(width), left, right)])


def row_matrix(taps, height, members, times):
    one = band(taps, np.arange(height), np.arange(height))
    return np.kron(np.eye(members), np.linalg.matrix_power(one, times))


def edge_matrix(taps, edge):
    inner = np.arange(edge)
    return np.stack(
        [halves(np.kron(np.eye(LANES // edge), band(taps, inner + shift * edge, inner))) for shift in (-1, 0, 1)]
    )


def split(x):
    high = x.astype(BF16)
    return high, (x - high.astype(F32)).astype(BF16)


def dot3(left, right):
    mul = functools.partial(jnp.dot, preferred_element_type=F32)
    return mul(left[0], right[0]) + (mul(left[1], right[0]) + mul(left[0], right[1]))


def both(ref):
    return ref[0], ref[1]


def lane_of(shape):
    return lax.broadcasted_iota(jnp.int32, shape, len(shape) - 1)


def pack_columns(field, start, edge):
    members, rows, _ = field.shape
    slots = LANES // edge
    groups = members // slots
    lane = lane_of((rows, LANES))
    origin = start // LANES * LANES
    out = []
    for g in range(groups):
        total = jnp.zeros((rows, LANES), F32)
        for j in range(slots):
            block = field[j * groups + g][:, origin : origin + LANES]
            shift = (j * edge - (start - origin)) % LANES
            moved = pltpu.roll(block, shift, 1) if shift else block
            total = jnp.where((lane >= j * edge) & (lane < (j + 1) * edge), moved, total)
        out.append(total)
    return jnp.stack(out)


def pack_edges(field, edge, first):
    return pack_columns(field, 0 if first else field.shape[-1] - edge, edge)


def repeated(x, period):
    while period < LANES:
        x = x + pltpu.roll(x, period, len(x.shape) - 1)
        period *= 2
    return x


def level_lanes(shape, level):
    lane = lane_of(shape)
    return (lane >= level * EDGE) & (lane < (level + 1) * EDGE)


def sides_of(core, chip):
    odd = lax.axis_index("tile") % 2 == 1
    return jnp.where(odd, core, chip), jnp.where(odd, chip, core)


def spread_edges(packed, edge):
    groups, rows, _ = packed.shape
    slots = LANES // edge
    lane = lane_of((groups, rows, LANES))
    parts = [jnp.where((lane >= j * edge) & (lane < (j + 1) * edge), packed, 0.0) for j in range(slots)]
    return jnp.concatenate(parts, axis=0).reshape(slots * groups * rows, LANES)


def beside(field, left, right, edge):
    members, rows, width = field.shape
    return jnp.concatenate(
        [field.reshape(members * rows, width), spread_edges(left, edge), spread_edges(right, edge)], axis=1
    )


def increments(members_ref, smoothed):
    members, levels = members_ref.shape[:2]
    totals = []
    for v in range(levels):
        total = members_ref[0, v].astype(F32) * smoothed[0]
        for k in range(1, members):
            total = total + members_ref[k, v].astype(F32) * smoothed[k]
        totals.append(total)
    return jnp.stack(totals)


def adjoint(members_ref, weighted):
    members, levels = members_ref.shape[:2]
    back = []
    for k in range(members):
        total = members_ref[k, 0].astype(F32) * weighted[0]
        for v in range(1, levels):
            total = total + members_ref[k, v].astype(F32) * weighted[v]
        back.append(total)
    return jnp.stack(back)


def folded(x):
    width = x.shape[-1]
    x = x.reshape(-1, 8, width).sum(axis=0)
    return sum(x[:, i : i + LANES] for i in range(0, width, LANES))


def edges_kernel(
    source_hbm, members_hbm, precision_hbm, covered_hbm,
    source, members_ref, obs_weight, near, near_weight, edge_members, to_core, to_chip, precision, covered, sems,
):
    members, levels, height, width = members_ref.shape
    pairs = ((source_hbm, source), (precision_hbm, precision), (covered_hbm, covered), (members_hbm, members_ref))
    copies = [pltpu.make_async_copy(x, y, sems.at[i]) for i, (x, y) in enumerate(pairs)]
    for copy in copies:
        copy.start()
    groups = members * EDGE // LANES
    odd = lax.axis_index("tile") % 2 == 1
    rows = groups * height

    def send(at, first, last):
        first, last = (x.reshape(-1, LANES) for x in (first, last))
        part = pl.ds(at, first.shape[0])
        to_core[part] = jnp.where(odd, first, last)
        to_chip[part] = jnp.where(odd, last, first)

    copies[0].wait()
    near[0], near[1] = pack_columns(source, 0, EDGE), pack_columns(source, width - EDGE, EDGE)
    send(0, near[0], near[1])
    send(rows, pack_columns(source, EDGE, EDGE), pack_columns(source, width - 2 * EDGE, EDGE))
    copies[1].wait()
    copies[2].wait()
    obs_weight[...] = weight_of(precision, covered)
    for side, start in enumerate((0, width - EDGE)):
        total = jnp.zeros((height, LANES), F32)
        for v in range(levels):
            origin = start // LANES * LANES
            shift = (v * EDGE - (start - origin)) % LANES
            block = obs_weight[v, :, origin : origin + LANES]
            total = jnp.where(level_lanes(total.shape, v), pltpu.roll(block, shift, 1) if shift else block, total)
        near_weight[side] = total
    send(rows * (2 + levels), near_weight[0], near_weight[1])
    copies[3].wait()
    for v in range(levels):
        level = members_ref[:, v].astype(F32)
        edge_members[0, v], edge_members[1, v] = pack_edges(level, EDGE, True), pack_edges(level, EDGE, False)
        send(rows * (2 + v), edge_members[0, v], edge_members[1, v])


def own_columns(field, column, row):
    members, height, width = field.shape
    lhs = split(field[...].reshape(members * height, width))
    return dot3(both(row), split(dot3(lhs, both(column)))).reshape(field.shape)


def tap_at(gap, inside):
    scale = 1.0 / np.sqrt(np.sum(np.exp(-(np.arange(-REACH, REACH + 1.0) ** 2) / 16.0)))
    square = (gap * gap).astype(F32)
    return jnp.where(inside & (jnp.abs(gap) <= REACH), jnp.exp(square * (-1.0 / 32.0)) * scale, 0.0)


def gaps(rows, columns):
    shape = (rows, columns)
    down, across = (lax.broadcasted_iota(jnp.int32, shape, i) for i in range(2))
    return down, across, down - across


def kept(ref, matrix):
    ref[0], ref[1] = split(matrix)


def first_kernel(source, after, members_ref, increment, norm, edge, thin):
    members, levels, height, width = members_ref.shape
    _, _, gap = gaps(width, width)
    column = split(tap_at(gap, True))
    down, across, gap = gaps(members * height, members * height)
    row = split(tap_at(gap, down // height == across // height))
    lhs = split(source[...].reshape(members * height, width))
    smoothed = dot3(row, split(dot3(lhs, column))).reshape(source.shape)
    increment[...] = increments(members_ref, smoothed).reshape(levels * height, width)
    norm[...] = repeated(folded(source[...] * source[...]), SPARE)
    down, across, gap = gaps(LANES, LANES)
    same = down // EDGE == across // EDGE
    for i in range(3):
        kept(edge.at[i], tap_at(gap + (i - 1) * EDGE, same))
    down, across, gap = gaps(*thin.shape[1:])
    kept(thin, tap_at(gap, down // height == across // height))


def edge_sums(edge_members, smoothed):
    groups, height = edge_members.shape[1:3]
    return repeated(jnp.sum(edge_members * smoothed.reshape(1, groups, height, LANES), axis=1), EDGE)


def add_columns(out, start, blocks):
    levels, height, _ = blocks[0].shape
    origin = start // LANES * LANES
    lane = lane_of(blocks[0].shape)
    total = jnp.zeros(lane.shape, F32)
    for i, block in enumerate(blocks):
        first = start - origin + i * EDGE
        total = jnp.where((lane >= first) & (lane < first + EDGE), block, total)
    rows, span = pl.ds(0, levels * height), pl.ds(origin, LANES)
    out[rows, span] = out[rows, span] + total.reshape(levels * height, LANES)


def beside_levels(sums):
    total = jnp.zeros(sums.shape[1:], F32)
    for v in range(sums.shape[0]):
        total = jnp.where(level_lanes(total.shape, v), sums[v], total)
    return total


def apart_levels(packed, levels):
    return [repeated(jnp.where(level_lanes(packed.shape, v), packed, 0.0), EDGE) for v in range(levels)]


def halo_members(block, rows, groups, levels):
    height = rows // groups
    return block[2 * rows : (2 + levels) * rows].reshape(levels, groups, height, LANES)


def edge_kernel(norm, chip, core, near, edge_members, edge, thin, out):
    levels, groups, height = edge_members.shape[1:4]
    rows = groups * height
    sides = sides_of(core[...], chip[...])
    parts = []
    for side, block in enumerate(sides):
        here = [block[rows : 2 * rows], block[:rows], near[side].reshape(rows, LANES)]
        parts += here if side == 0 else here[::-1]
    filtered = dot3(both(thin), split(jnp.concatenate(parts, axis=1)))
    filtered = split(jnp.concatenate([filtered[:, : 3 * LANES], filtered[:, 3 * LANES :]], axis=0))
    beyond = dot3(filtered, [jnp.concatenate([edge[i, k] for i in range(3)], axis=0) for k in range(2)])
    middle = tuple(x[:, LANES : 2 * LANES] for x in filtered)
    for side, block in enumerate(sides):
        own = slice(side * rows, (side + 1) * rows)
        within = dot3(tuple(x[own] for x in middle), both(edge.at[2 * side]))
        lanes = pl.ds(side * LANES, LANES)
        out[:height, lanes] = beside_levels(edge_sums(edge_members[side], within))
        out[height:, lanes] = beside_levels(edge_sums(halo_members(block, rows, groups, levels), beyond[own]))
    lane = lane_of(norm.shape)
    top = pl.ds(0, norm.shape[0])
    out[top, :LANES] = jnp.where(lane >= LANES - SPARE, norm[...], out[top, :LANES])


def weight_of(precision, covered):
    levels, height, width = precision.shape
    rows, blocks = covered.shape
    spread = lax.broadcasted_iota(jnp.int32, (blocks, width), 1) // (width // blocks)
    spread = (spread == lax.broadcasted_iota(jnp.int32, (blocks, width), 0)).astype(BF16)
    mask = jnp.dot(covered[...].astype(F32).astype(BF16), spread, preferred_element_type=F32)
    tall = height // rows
    mask = jnp.concatenate([jnp.broadcast_to(mask[i : i + 1], (tall, width)) for i in range(rows)], axis=0)
    return precision[...] * mask


def packed_adjoint(members, weighted):
    total = jnp.zeros(members.shape[1:], F32)
    for v, level in enumerate(apart_levels(weighted, members.shape[0])):
        total = total + members[v] * level
    return total


def prepare_kernel(
    after, members_ref, column_hbm, row_hbm, edge_hbm, thin_hbm, next_members, column, row, edge, thin, sems
):
    pairs = ((column_hbm, column), (row_hbm, row), (edge_hbm, edge), (thin_hbm, thin))
    copies = [pltpu.make_async_copy(x, y, sems.at[i]) for i, (x, y) in enumerate(pairs)]
    for copy in copies:
        copy.start()
    levels, width = members_ref.shape[1], members_ref.shape[-1]
    for v in range(levels):
        level = members_ref[:, v].astype(F32)
        next_members[0, v] = pack_columns(level, EDGE, EDGE)
        next_members[1, v] = pack_columns(level, width - 2 * EDGE, EDGE)
    for copy in copies:
        copy.wait()


def main_kernel(i0, i1, i2, i3, obs_weight, members_ref, column, row, first, back, second):
    first[...] = (i0[...] + i1[...]) + (i2[...] + i3[...])
    back[...] = adjoint(members_ref, obs_weight[...] * first[...].reshape(obs_weight.shape))
    second[...] = increments(members_ref, own_columns(back, column, row)).reshape(second.shape)


def correction_kernel(
    e0, e1, e2, e3, main, near_weight, chip, core, edge_members, next_members, edge, thin, outer, own, halo, out
):
    levels, groups, height = edge_members.shape[1:4]
    width = out.shape[-1]
    rows = groups * height
    outer[...] = (e0[...] + e1[...]) + (e2[...] + e3[...])
    out[...] = main[...]
    for side, block in enumerate(sides_of(core[...], chip[...])):
        lanes = pl.ds(side * LANES, LANES)
        own[side] = packed_adjoint(edge_members[side], outer[:height, lanes] * near_weight[side])
        halo[side] = packed_adjoint(
            halo_members(block, rows, groups, levels), outer[height:, lanes] * block[(2 + levels) * rows :]
        )
    parts = [x[side].reshape(rows, LANES) for side in range(2) for x in (halo, own)]
    filtered = split(dot3(both(thin), split(jnp.concatenate(parts, axis=1))))
    for side in range(2):
        span = slice(2 * side * LANES, 2 * (side + 1) * LANES)
        matrix = [jnp.concatenate([edge[2 * side, k], edge[1, k]], axis=0) for k in range(2)]
        outermost = dot3(tuple(x[:, span] for x in filtered), matrix)
        inner = dot3(tuple(x[:, span.start + LANES : span.stop] for x in filtered), both(edge.at[2 * side]))
        blocks = [edge_sums(edge_members[side], outermost), edge_sums(next_members[side], inner)]
        if side == 0:
            add_columns(out, 0, blocks)
        else:
            add_columns(out, width - 2 * EDGE, blocks[::-1])


def wide_filter_kernel(
    main, own, halo, first, outer, obs_weight, column_hbm, row_hbm, weighted, sums, out, column, row, sems
):
    copies = [pltpu.make_async_copy(x, y, sems.at[i]) for i, (x, y) in enumerate(((column_hbm, column), (row_hbm, row)))]
    for copy in copies:
        copy.start()
    levels, height, width = obs_weight.shape
    weighted[...] = first[...].reshape(obs_weight.shape)
    for side, start in enumerate((0, width - EDGE)):
        origin = start // LANES * LANES
        lane = lane_of((height, LANES))
        mask = (lane >= start - origin) & (lane < start - origin + EDGE)
        for v, level in enumerate(apart_levels(outer[:height, pl.ds(side * LANES, LANES)], levels)):
            span = pl.ds(origin, LANES)
            weighted[v, :, span] = weighted[v, :, span] + jnp.where(mask, level, 0.0)
    increment = weighted[...]
    weighted[...] = obs_weight[...] * increment
    top = outer[: sums.shape[1], :LANES]
    sums[0] = jnp.where(lane_of(top.shape) >= LANES - SPARE, top, 0.0)
    sums[1] = folded(weighted[...] * increment)
    groups = own.shape[1]
    fields = []
    for k in range(main.shape[0]):
        field = main[k]
        slot, group = k // groups, k % groups
        ends = []
        for side, at in enumerate((0, LANES - EDGE)):
            moved = pltpu.roll(own[side, group], (at - slot * EDGE) % LANES, 1)
            lane = lane_of(moved.shape)
            ends.append(jnp.where((lane >= at) & (lane < at + EDGE), moved, 0.0))
        middle = [jnp.zeros((height, width - 2 * LANES), F32)] if width > 2 * LANES else []
        fields.append(field + jnp.concatenate([ends[0]] + middle + [ends[1]], axis=1))
    for copy in copies:
        copy.wait()
    lhs = split(beside(jnp.stack(fields), halo[0], halo[1], EDGE))
    out[...] = dot3(both(row), split(dot3(lhs, both(column)))).reshape(out.shape)


def filter_kernel(back, core, chip, column, row, out):
    groups, height = back.shape[0] * EDGE // LANES, back.shape[1]
    left, right = sides_of(*(x[: groups * height].reshape(groups, height, LANES) for x in (core, chip)))
    lhs = split(beside(back[...], left, right, EDGE))
    out[...] = dot3(both(row), split(dot3(lhs, both(column)))).reshape(out.shape)


def last_kernel(i0, i1, i2, i3, obs_weight, before, sums, members_ref, back, to_core, to_chip):
    levels, height, width = obs_weight.shape
    increment = ((i0[...] + i1[...]) + (i2[...] + i3[...])).reshape(obs_weight.shape)
    weighted = obs_weight[...] * increment
    four = [sums[0], sums[1], folded(before[...] * increment), folded(weighted * increment)]
    row = lax.broadcasted_iota(jnp.int32, (8, LANES), 0)
    stacked = jnp.zeros((8, LANES), F32)
    for i, part in enumerate(four):
        stacked = jnp.where(row == i, jnp.sum(part, axis=0, keepdims=True), stacked)
    back[...] = adjoint(members_ref, weighted)
    odd = lax.axis_index("tile") % 2 == 1
    first, last = pack_edges(back, EDGE, True), pack_edges(back, EDGE, False)
    rows = first.shape[0] * height
    to_core[:rows] = jnp.where(odd, first, last).reshape(rows, LANES)
    to_core[rows:] = stacked
    to_chip[...] = jnp.where(odd, last, first).reshape(rows, LANES)


def copy_kernel(value, after, out):
    out[...] = value[...]


def pass_kernel(value, after, out):
    pass


def combine_kernel(own, other, source, first, second, weights, residual, held_weights, held_residual, sems):
    total = jnp.sum(own[...] + other[...], axis=1, keepdims=True)
    bb, bg, gg, gh = (total[i : i + 1] for i in range(4))
    bg, gg, gh = bg / bb, gg / bb, gh / bb
    q = 1.0 / (1.0 + bg)
    p = bg * q
    ratio = (gg - bg * bg) * q * q
    d = p + ratio
    square = d * d - 2.0 * d * q * bg + q * q * gg
    image = d * d * bg - 2.0 * d * q * gg + q * q * gh
    step = ratio / (square + image)
    members = source.shape[0]
    pieces = sems.shape[1]
    copies = []
    for i in range(pieces):
        part = pl.ds(i * (members // pieces), members // pieces)
        b, g, h = source[part], first[part], second[part]
        held_weights[part] = (q + step * d) * b - (step * q) * g
        held_residual[part] = (p - step * d) * b + (step * q - q - step * d) * g + (step * q) * h
        for k, (held, out) in enumerate(((held_weights, weights), (held_residual, residual))):
            copies.append(pltpu.make_async_copy(held.at[part], out.at[part], sems.at[k, i]))
            copies[-1].start()
    for copy in copies:
        copy.wait()


def call(kernel, outs, *operands, cost=None):
    shapes = [jax.ShapeDtypeStruct(shape, F32) for shape in outs]
    vmem = pl.BlockSpec(memory_space=pltpu.VMEM)
    return pl.pallas_call(
        kernel,
        out_shape=shapes,
        in_specs=[vmem] * len(operands),
        out_specs=[vmem] * len(outs),
        compiler_params=pltpu.CompilerParams(vmem_limit_bytes=24 * 1024 * 1024),
        cost_estimate=cost,
    )(*operands)


def passed(value, after):
    vmem = pl.BlockSpec(memory_space=pltpu.VMEM)
    return pl.pallas_call(
        pass_kernel,
        out_shape=pltpu.VMEM(value.shape, value.dtype),
        in_specs=[vmem] * 2,
        out_specs=vmem,
        input_output_aliases={0: 0},
        compiler_params=pltpu.CompilerParams(vmem_limit_bytes=24 * 1024 * 1024),
        cost_estimate=LONG,
    )(value, after)


def in_hbm(array):
    return pltpu.with_memory_space_constraint(array, pltpu.HBM)


def held_edges(source, members_data, precision, covered):
    members, levels, height, width = members_data.shape
    groups = members * EDGE // LANES
    payload = ((groups * (2 + levels) + 1) * height, LANES)
    vmem = pl.BlockSpec(memory_space=pltpu.VMEM)
    hbm = pl.BlockSpec(memory_space=pltpu.HBM)
    arrays = (source, members_data, precision, covered)
    return pl.pallas_call(
        edges_kernel,
        out_shape=[
            pltpu.VMEM(source.shape, F32),
            pltpu.VMEM(members_data.shape, members_data.dtype),
            pltpu.VMEM(precision.shape, F32),
            pltpu.VMEM((2, groups, height, LANES), F32),
            pltpu.VMEM((2, height, LANES), F32),
            pltpu.VMEM((2, levels, groups, height, LANES), F32),
            pltpu.VMEM(payload, F32),
            pltpu.VMEM(payload, F32),
        ],
        in_specs=[hbm] * 4,
        out_specs=[vmem] * 8,
        scratch_shapes=[
            pltpu.VMEM(precision.shape, F32),
            pltpu.VMEM(covered.shape, covered.dtype),
            pltpu.SemaphoreType.DMA((4,)),
        ],
        compiler_params=pltpu.CompilerParams(vmem_limit_bytes=24 * 1024 * 1024),
    )(*map(in_hbm, arrays))


def first_increment(source, after, members_data):
    members, levels, height, width = members_data.shape
    groups = members * EDGE // LANES
    vmem = pl.BlockSpec(memory_space=pltpu.VMEM)
    return pl.pallas_call(
        first_kernel,
        out_shape=[
            pltpu.VMEM((levels * height, width), F32),
            pltpu.VMEM((8, LANES), F32),
            pltpu.VMEM((3, 2, LANES, LANES), BF16),
            pltpu.VMEM((2, groups * height, groups * height), BF16),
        ],
        in_specs=[vmem] * 3,
        out_specs=[vmem] * 4,
        compiler_params=pltpu.CompilerParams(vmem_limit_bytes=24 * 1024 * 1024),
        cost_estimate=LONG,
    )(source, after, members_data)


def call_with_constants(kernel, outs, kept, scratch, operands, constants):
    vmem = pl.BlockSpec(memory_space=pltpu.VMEM)
    hbm = pl.BlockSpec(memory_space=pltpu.HBM)
    held = [pltpu.VMEM(x.shape, x.dtype) for x in kept]
    return pl.pallas_call(
        kernel,
        out_shape=[pltpu.VMEM(shape, F32) for shape in outs] + held,
        in_specs=[vmem] * len(operands) + [hbm] * len(constants),
        out_specs=[vmem] * (len(outs) + len(kept)),
        scratch_shapes=[pltpu.VMEM(x.shape, x.dtype) for x in scratch] + [pltpu.SemaphoreType.DMA((len(constants),))],
        compiler_params=pltpu.CompilerParams(vmem_limit_bytes=24 * 1024 * 1024),
        cost_estimate=LONG,
    )(*operands, *map(in_hbm, constants))


def combined(own, other, source, first, second):
    vmem = pl.BlockSpec(memory_space=pltpu.VMEM)
    hbm = pl.BlockSpec(memory_space=pltpu.HBM)
    return pl.pallas_call(
        combine_kernel,
        out_shape=[jax.ShapeDtypeStruct(source.shape, F32)] * 2,
        in_specs=[vmem] * 5,
        out_specs=[hbm] * 2,
        scratch_shapes=[pltpu.VMEM(source.shape, F32)] * 2 + [pltpu.SemaphoreType.DMA((2, 4))],
        compiler_params=pltpu.CompilerParams(vmem_limit_bytes=24 * 1024 * 1024),
    )(own, other, source, first, second)


def from_both_sides(to_next, to_previous, axis):
    count = lax.axis_size(axis)
    left = lax.ppermute(to_next, axis, [(i, (i + 1) % count) for i in range(count)])
    right = lax.ppermute(to_previous, axis, [((i + 1) % count, i) for i in range(count)])
    return left, right


def from_tile(value, bit):
    count = lax.axis_size("tile")
    return lax.ppermute(value, "tile", [(i, i ^ bit) for i in range(count)])


def from_core(value):
    return from_tile(value, 1)


def from_chip(value):
    count = lax.axis_size("tile")
    return lax.ppermute(value, "tile", [(i, (i + 1) % count if i % 2 else (i - 1) % count) for i in range(count)])


def from_all(value, axis, order):
    count = lax.axis_size(axis)
    return [value] + [lax.ppermute(value, axis, [(i, i ^ k) for i in range(count)]) for k in order]


def one_tile_row(right_side, perturbations, precision, covered):
    source, members_data = right_side[0], perturbations[0]
    members, levels, height, width = members_data.shape
    groups = members * EDGE // LANES
    taps = taps_np()
    twice = np.convolve(taps, taps)
    field = (members, height, width)
    plane = (levels, height, width)
    flat = (levels * height, width)
    own = np.arange(width)

    source, members_data, obs_weight, near, near_weight, edge_members, to_core, to_chip = held_edges(
        source, members_data, precision[0], covered[0]
    )
    core, chip = from_core(to_core), from_chip(to_chip)
    inside, norm, edge, thin = first_increment(source, to_chip, members_data)
    inside = from_all(inside, "mem", (3, 2, 1))
    (outer,) = call(edge_kernel, [(2 * height, 2 * LANES)], norm, chip, core, near, edge_members, edge, thin)
    column_twice, row_twice = halves(band(twice, own, own)), halves(row_matrix(taps, height, members, 2))
    edge, thin = edge_matrix(twice, EDGE), halves(row_matrix(taps, height, groups, 2))
    constants = [column_twice, row_twice, edge, thin]
    next_members, column, row, edge, thin = call_with_constants(
        prepare_kernel, [edge_members.shape], constants, [], [outer, members_data], constants
    )
    increment, main, inside = call(
        main_kernel, [flat, field, flat], *inside, obs_weight, members_data, column, row
    )
    ends = (2, groups, height, LANES)
    outer, corrected, halo, second = call(
        correction_kernel, [outer.shape, ends, ends, flat],
        *from_all(outer, "mem", (3, 2, 1)), inside, near_weight, chip, core, edge_members, next_members, edge, thin,
    )
    parts = from_all(second, "mem", (2, 1, 3))
    column, row = halves(column_matrix(taps, width, EDGE)), halves(row_matrix(taps, height, members, 1))
    weighted, sums, first, column, row = call_with_constants(
        wide_filter_kernel, [plane, (2, 8, LANES), field], [column, row], [],
        [main, corrected, halo, increment, outer, obs_weight], [column, row],
    )
    back, to_core, to_chip = call(
        last_kernel,
        [field, (groups * height + 8, LANES), (groups * height, LANES)],
        *parts, obs_weight, weighted, sums, members_data,
    )
    core = from_core(to_core)
    sums = to_core[groups * height :] + core[groups * height :]
    (to_chip,) = call(copy_kernel, [to_chip.shape], to_chip, sums)
    chip = from_chip(to_chip)
    first = passed(first, sums)
    sums = sums + from_tile(sums, 3)
    others = from_tile(sums, 5)
    (second,) = call(filter_kernel, [field], back, core, chip, column, row, cost=LONG)
    weights, residual = combined(sums, others, source, first, second)
    return weights[None], residual[None]


def passed_along(value, axis, steps):
    count = lax.axis_size(axis)
    first, last = (max(0, -steps), min(count, count - steps))
    return lax.ppermute(value, axis, [(source, source + steps) for source in range(first, last)])


def smooth(field):
    taps = taps_np().astype(np.float32)
    height, width = field.shape[1:]
    above = passed_along(field[:, height - REACH :, :], "tile", TCOLS)
    below = passed_along(field[:, :REACH, :], "tile", -TCOLS)
    padded = jnp.concatenate([above, field, below], axis=1)
    along = sum(taps[j] * padded[:, j : j + height, :] for j in range(2 * REACH + 1))
    left, right = from_both_sides(along[:, :, width - REACH :], along[:, :, :REACH], "tile")
    sided = jnp.concatenate([left, along, right], axis=2)
    return sum(taps[j] * sided[:, :, j : j + width] for j in range(2 * REACH + 1))


def several_tile_rows(right_side, perturbations, precision, covered):
    source = right_side[0]
    members_data = perturbations[0].astype(F32)
    levels, height, width = precision.shape[1:]
    rows, blocks = covered.shape[1:]
    mask = covered[0].astype(F32)
    obs_weight = (
        precision[0].reshape(levels, rows, height // rows, blocks, width // blocks) * mask[None, :, None, :, None]
    ).reshape(levels, height, width)

    def operator(direction):
        partial_terms = jnp.einsum("kvyx,kyx->vyx", members_data, smooth(direction))
        weighted = obs_weight * lax.psum(partial_terms, "mem")
        return direction + smooth(jnp.einsum("kvyx,vyx->kyx", members_data, weighted))

    weights = jnp.zeros_like(source)
    residual = direction = source
    norm_now = lax.psum(jnp.sum(source * source), ("tile", "mem"))
    for step in range(ITERS):
        image = operator(direction)
        length = norm_now / lax.psum(jnp.sum(direction * image), ("tile", "mem"))
        weights = weights + length * direction
        residual = residual - length * image
        if step + 1 < ITERS:
            norm_next = lax.psum(jnp.sum(residual * residual), ("tile", "mem"))
            direction = residual + norm_next / norm_now * direction
            norm_now = norm_next
    return weights[None], residual[None]


def solution(mesh):
    single = mesh.shape["tile"] == TCOLS and mesh.shape["mem"] == 4
    local = one_tile_row if single else several_tile_rows
    return jax.shard_map(
        local,
        mesh=mesh,
        in_specs=(
            P("tile", "mem", None, None),
            P("tile", "mem", None, None, None),
            P("tile", None, None, None),
            P("tile", None, None),
        ),
        out_specs=(P("tile", "mem", None, None), P("tile", "mem", None, None)),
        check_vma=False,
    )
```

```python
import functools

import jax
import jax.numpy as jnp
import ml_dtypes
import numpy as np
from jax import lax
from jax.experimental import pallas as pl
from jax.experimental.pallas import tpu as pltpu
from jax.sharding import PartitionSpec as P

ITERS = 2
TCOLS = 8
REACH = 8
EDGE = 2 * REACH
SPARE = 32
LANES = 128
F32 = jnp.float32
BF16 = jnp.bfloat16
LONG = pl.CostEstimate(flops=10**9, bytes_accessed=10**6, transcendentals=0)


def taps_np():
    offsets = np.arange(-REACH, REACH + 1, dtype=np.float64)
    raw = np.exp(-offsets * offsets / 32.0)
    return raw / np.sqrt(np.sum(np.exp(-offsets * offsets / 16.0)))


def band(taps, source, target):
    reach = (len(taps) - 1) // 2
    gap = source[:, None] - target[None, :]
    inside = np.abs(gap) <= reach
    return np.where(inside, taps[np.clip(gap + reach, 0, 2 * reach)], 0.0)


def halves(matrix):
    whole = matrix.astype(np.float32)
    high = whole.astype(ml_dtypes.bfloat16)
    low = (whole - high.astype(np.float32)).astype(ml_dtypes.bfloat16)
    return np.stack([high, low])


def column_matrix(taps, width, edge):
    target = np.arange(width)
    slots = LANES // edge
    left = np.tile(np.arange(edge) - edge, slots)
    right = np.tile(np.arange(edge) + width, slots)
    return np.concatenate([band(taps, s, target) for s in (np.arange(width), left, right)])


def row_matrix(taps, height, members, times):
    one = band(taps, np.arange(height), np.arange(height))
    return np.kron(np.eye(members), np.linalg.matrix_power(one, times))


def edge_matrix(taps, edge):
    inner = np.arange(edge)
    return np.stack(
        [halves(np.kron(np.eye(LANES // edge), band(taps, inner + shift * edge, inner))) for shift in (-1, 0, 1)]
    )


def split(x):
    high = x.astype(BF16)
    return high, (x - high.astype(F32)).astype(BF16)


def dot3(left, right):
    mul = functools.partial(jnp.dot, preferred_element_type=F32)
    return mul(left[0], right[0]) + (mul(left[1], right[0]) + mul(left[0], right[1]))


def both(ref):
    return ref[0], ref[1]


def lane_of(shape):
    return lax.broadcasted_iota(jnp.int32, shape, len(shape) - 1)


def pack_columns(field, start, edge):
    members, rows, _ = field.shape
    slots = LANES // edge
    groups = members // slots
    lane = lane_of((rows, LANES))
    origin = start // LANES * LANES
    out = []
    for g in range(groups):
        total = jnp.zeros((rows, LANES), F32)
        for j in range(slots):
            block = field[j * groups + g][:, origin : origin + LANES]
            shift = (j * edge - (start - origin)) % LANES
            moved = pltpu.roll(block, shift, 1) if shift else block
            total = jnp.where((lane >= j * edge) & (lane < (j + 1) * edge), moved, total)
        out.append(total)
    return jnp.stack(out)


def pack_edges(field, edge, first):
    return pack_columns(field, 0 if first else field.shape[-1] - edge, edge)


def repeated(x, period):
    while period < LANES:
        x = x + pltpu.roll(x, period, len(x.shape) - 1)
        period *= 2
    return x


def level_lanes(shape, level):
    lane = lane_of(shape)
    return (lane >= level * EDGE) & (lane < (level + 1) * EDGE)


def sides_of(core, chip):
    odd = lax.axis_index("tile") % 2 == 1
    return jnp.where(odd, core, chip), jnp.where(odd, chip, core)


def spread_edges(packed, edge):
    groups, rows, _ = packed.shape
    slots = LANES // edge
    lane = lane_of((groups, rows, LANES))
    parts = [jnp.where((lane >= j * edge) & (lane < (j + 1) * edge), packed, 0.0) for j in range(slots)]
    return jnp.concatenate(parts, axis=0).reshape(slots * groups * rows, LANES)


def beside(field, left, right, edge):
    members, rows, width = field.shape
    return jnp.concatenate(
        [field.reshape(members * rows, width), spread_edges(left, edge), spread_edges(right, edge)], axis=1
    )


def increments(members_ref, smoothed):
    members, levels = members_ref.shape[:2]
    totals = []
    for v in range(levels):
        total = members_ref[0, v].astype(F32) * smoothed[0]
        for k in range(1, members):
            total = total + members_ref[k, v].astype(F32) * smoothed[k]
        totals.append(total)
    return jnp.stack(totals)


def adjoint(members_ref, weighted):
    members, levels = members_ref.shape[:2]
    back = []
    for k in range(members):
        total = members_ref[k, 0].astype(F32) * weighted[0]
        for v in range(1, levels):
            total = total + members_ref[k, v].astype(F32) * weighted[v]
        back.append(total)
    return jnp.stack(back)


def folded(x):
    width = x.shape[-1]
    x = x.reshape(-1, 8, width).sum(axis=0)
    return sum(x[:, i : i + LANES] for i in range(0, width, LANES))


def edges_kernel(
    source_hbm, members_hbm, precision_hbm, covered_hbm,
    source, members_ref, obs_weight, near, near_weight, edge_members, to_core, to_chip, precision, covered, sems,
):
    members, levels, height, width = members_ref.shape
    pairs = ((source_hbm, source), (precision_hbm, precision), (covered_hbm, covered), (members_hbm, members_ref))
    copies = [pltpu.make_async_copy(x, y, sems.at[i]) for i, (x, y) in enumerate(pairs)]
    for copy in copies:
        copy.start()
    groups = members * EDGE // LANES
    odd = lax.axis_index("tile") % 2 == 1
    rows = groups * height

    def send(at, first, last):
        first, last = (x.reshape(-1, LANES) for x in (first, last))
        part = pl.ds(at, first.shape[0])
        to_core[part] = jnp.where(odd, first, last)
        to_chip[part] = jnp.where(odd, last, first)

    copies[0].wait()
    near[0], near[1] = pack_columns(source, 0, EDGE), pack_columns(source, width - EDGE, EDGE)
    send(0, near[0], near[1])
    send(rows, pack_columns(source, EDGE, EDGE), pack_columns(source, width - 2 * EDGE, EDGE))
    copies[1].wait()
    copies[2].wait()
    obs_weight[...] = weight_of(precision, covered)
    for side, start in enumerate((0, width - EDGE)):
        total = jnp.zeros((height, LANES), F32)
        for v in range(levels):
            origin = start // LANES * LANES
            shift = (v * EDGE - (start - origin)) % LANES
            block = obs_weight[v, :, origin : origin + LANES]
            total = jnp.where(level_lanes(total.shape, v), pltpu.roll(block, shift, 1) if shift else block, total)
        near_weight[side] = total
    send(rows * (2 + levels), near_weight[0], near_weight[1])
    copies[3].wait()
    for v in range(levels):
        level = members_ref[:, v].astype(F32)
        edge_members[0, v], edge_members[1, v] = pack_edges(level, EDGE, True), pack_edges(level, EDGE, False)
        send(rows * (2 + v), edge_members[0, v], edge_members[1, v])


def own_columns(field, column, row):
    members, height, width = field.shape
    lhs = split(field[...].reshape(members * height, width))
    return dot3(both(row), split(dot3(lhs, both(column)))).reshape(field.shape)


def tap_at(gap, inside):
    scale = 1.0 / np.sqrt(np.sum(np.exp(-(np.arange(-REACH, REACH + 1.0) ** 2) / 16.0)))
    square = (gap * gap).astype(F32)
    return jnp.where(inside & (jnp.abs(gap) <= REACH), jnp.exp(square * (-1.0 / 32.0)) * scale, 0.0)


def gaps(rows, columns):
    shape = (rows, columns)
    down, across = (lax.broadcasted_iota(jnp.int32, shape, i) for i in range(2))
    return down, across, down - across


def kept(ref, matrix):
    ref[0], ref[1] = split(matrix)


def first_kernel(source, after, members_ref, increment, norm, edge, thin):
    members, levels, height, width = members_ref.shape
    _, _, gap = gaps(width, width)
    column = split(tap_at(gap, True))
    down, across, gap = gaps(members * height, members * height)
    row = split(tap_at(gap, down // height == across // height))
    lhs = split(source[...].reshape(members * height, width))
    smoothed = dot3(row, split(dot3(lhs, column))).reshape(source.shape)
    increment[...] = increments(members_ref, smoothed).reshape(levels * height, width)
    norm[...] = repeated(folded(source[...] * source[...]), SPARE)
    down, across, gap = gaps(LANES, LANES)
    same = down // EDGE == across // EDGE
    for i in range(3):
        kept(edge.at[i], tap_at(gap + (i - 1) * EDGE, same))
    down, across, gap = gaps(*thin.shape[1:])
    kept(thin, tap_at(gap, down // height == across // height))


def edge_terms(edge_members, smoothed):
    groups, height = edge_members.shape[1:3]
    return jnp.sum(edge_members * smoothed.reshape(1, groups, height, LANES), axis=1)


def in_slot(shape, slot):
    lane = lane_of(shape)
    return (lane >= slot * EDGE) & (lane < (slot + 1) * EDGE)


def add_columns(out, start, terms):
    levels, height, _ = terms[0].shape
    origin = start // LANES * LANES
    first = (start - origin) // EDGE
    even, odd = terms if first % 2 == 0 else terms[::-1]
    even, odd = (x.reshape(levels * height, LANES) for x in (even, odd))
    lane = lane_of(even.shape)
    total = jnp.where(
        lane // EDGE % 2 == 0,
        even + pltpu.roll(even, LANES - EDGE, 1),
        odd + pltpu.roll(odd, EDGE, 1),
    )
    total = repeated(total, 2 * EDGE)
    mask = (lane >= start - origin) & (lane < start - origin + 2 * EDGE)
    rows, span = pl.ds(0, levels * height), pl.ds(origin, LANES)
    out[rows, span] = out[rows, span] + jnp.where(mask, total, 0.0)


def beside_levels(terms):
    levels, shape = terms.shape[0], terms.shape[1:]
    slots = LANES // EDGE
    moved = []
    for k in range(slots):
        part = jnp.zeros(shape, F32)
        for slot in range(slots):
            level = (slot + k) % slots
            if level < levels:
                part = jnp.where(in_slot(shape, slot), terms[level], part)
        moved.append(pltpu.roll(part, k * EDGE, 1) if k else part)
    while len(moved) > 1:
        moved = [x + y for x, y in zip(moved[::2], moved[1::2])]
    return moved[0]


def apart_levels(packed, levels):
    slots = LANES // EDGE
    turned = [packed] + [pltpu.roll(packed, EDGE * k, 1) for k in range(1, slots)]
    lane = lane_of(packed.shape)
    out = []
    for v in range(levels):
        parts, width = [turned[(slot - v) % slots] for slot in range(slots)], EDGE
        while len(parts) > 1:
            left = lane // width % 2 == 0
            parts = [jnp.where(left, x, y) for x, y in zip(parts[::2], parts[1::2])]
            width *= 2
        out.append(parts[0])
    return out


def halo_members(block, rows, groups, levels):
    height = rows // groups
    return block[2 * rows : (2 + levels) * rows].reshape(levels, groups, height, LANES)


def edge_kernel(norm, chip, core, near, edge_members, edge, thin, out):
    levels, groups, height = edge_members.shape[1:4]
    rows = groups * height
    sides = sides_of(core[...], chip[...])
    parts = []
    for side, block in enumerate(sides):
        here = [block[rows : 2 * rows], block[:rows], near[side].reshape(rows, LANES)]
        parts += here if side == 0 else here[::-1]
    filtered = dot3(both(thin), split(jnp.concatenate(parts, axis=1)))
    filtered = split(jnp.concatenate([filtered[:, : 3 * LANES], filtered[:, 3 * LANES :]], axis=0))
    beyond = dot3(filtered, [jnp.concatenate([edge[i, k] for i in range(3)], axis=0) for k in range(2)])
    middle = tuple(x[:, LANES : 2 * LANES] for x in filtered)
    for side, block in enumerate(sides):
        own = slice(side * rows, (side + 1) * rows)
        within = dot3(tuple(x[own] for x in middle), both(edge.at[2 * side]))
        lanes = pl.ds(side * LANES, LANES)
        out[:height, lanes] = beside_levels(edge_terms(edge_members[side], within))
        out[height:, lanes] = beside_levels(edge_terms(halo_members(block, rows, groups, levels), beyond[own]))
    lane = lane_of(norm.shape)
    top = pl.ds(0, norm.shape[0])
    out[top, :LANES] = jnp.where(lane >= LANES - SPARE, norm[...], out[top, :LANES])


def weight_of(precision, covered):
    levels, height, width = precision.shape
    rows, blocks = covered.shape
    spread = lax.broadcasted_iota(jnp.int32, (blocks, width), 1) // (width // blocks)
    spread = (spread == lax.broadcasted_iota(jnp.int32, (blocks, width), 0)).astype(BF16)
    mask = jnp.dot(covered[...].astype(F32).astype(BF16), spread, preferred_element_type=F32)
    tall = height // rows
    mask = jnp.concatenate([jnp.broadcast_to(mask[i : i + 1], (tall, width)) for i in range(rows)], axis=0)
    return precision[...] * mask


def packed_adjoint(members, weighted):
    total = jnp.zeros(members.shape[1:], F32)
    for v, level in enumerate(apart_levels(weighted, members.shape[0])):
        total = total + members[v] * level
    return total


def prepare_kernel(
    after, members_ref, column_hbm, row_hbm, edge_hbm, thin_hbm, next_members, column, row, edge, thin, sems
):
    pairs = ((column_hbm, column), (row_hbm, row), (edge_hbm, edge), (thin_hbm, thin))
    copies = [pltpu.make_async_copy(x, y, sems.at[i]) for i, (x, y) in enumerate(pairs)]
    for copy in copies:
        copy.start()
    levels, width = members_ref.shape[1], members_ref.shape[-1]
    for v in range(levels):
        level = members_ref[:, v].astype(F32)
        next_members[0, v] = pack_columns(level, EDGE, EDGE)
        next_members[1, v] = pack_columns(level, width - 2 * EDGE, EDGE)
    for copy in copies:
        copy.wait()


def main_kernel(i0, i1, i2, i3, obs_weight, members_ref, column, row, first, back, second):
    first[...] = (i0[...] + i1[...]) + (i2[...] + i3[...])
    back[...] = adjoint(members_ref, obs_weight[...] * first[...].reshape(obs_weight.shape))
    second[...] = increments(members_ref, own_columns(back, column, row)).reshape(second.shape)


def correction_kernel(
    e0, e1, e2, e3, main, near_weight, chip, core, edge_members, next_members, edge, thin, outer, own, halo, out
):
    levels, groups, height = edge_members.shape[1:4]
    width = out.shape[-1]
    rows = groups * height
    outer[...] = (e0[...] + e1[...]) + (e2[...] + e3[...])
    out[...] = main[...]
    for side, block in enumerate(sides_of(core[...], chip[...])):
        lanes = pl.ds(side * LANES, LANES)
        own[side] = packed_adjoint(edge_members[side], outer[:height, lanes] * near_weight[side])
        halo[side] = packed_adjoint(
            halo_members(block, rows, groups, levels), outer[height:, lanes] * block[(2 + levels) * rows :]
        )
    parts = [x[side].reshape(rows, LANES) for side in range(2) for x in (halo, own)]
    filtered = split(dot3(both(thin), split(jnp.concatenate(parts, axis=1))))
    for side in range(2):
        span = slice(2 * side * LANES, 2 * (side + 1) * LANES)
        matrix = [jnp.concatenate([edge[2 * side, k], edge[1, k]], axis=0) for k in range(2)]
        outermost = dot3(tuple(x[:, span] for x in filtered), matrix)
        inner = dot3(tuple(x[:, span.start + LANES : span.stop] for x in filtered), both(edge.at[2 * side]))
        blocks = [edge_terms(edge_members[side], outermost), edge_terms(next_members[side], inner)]
        if side == 0:
            add_columns(out, 0, blocks)
        else:
            add_columns(out, width - 2 * EDGE, blocks[::-1])


def wide_filter_kernel(
    main, own, halo, first, outer, obs_weight, column_hbm, row_hbm, weighted, sums, out, column, row, sems
):
    copies = [pltpu.make_async_copy(x, y, sems.at[i]) for i, (x, y) in enumerate(((column_hbm, column), (row_hbm, row)))]
    for copy in copies:
        copy.start()
    levels, height, width = obs_weight.shape
    weighted[...] = first[...].reshape(obs_weight.shape)
    for side, start in enumerate((0, width - EDGE)):
        origin = start // LANES * LANES
        lane = lane_of((height, LANES))
        mask = (lane >= start - origin) & (lane < start - origin + EDGE)
        for v, level in enumerate(apart_levels(outer[:height, pl.ds(side * LANES, LANES)], levels)):
            span = pl.ds(origin, LANES)
            weighted[v, :, span] = weighted[v, :, span] + jnp.where(mask, level, 0.0)
    increment = weighted[...]
    weighted[...] = obs_weight[...] * increment
    top = outer[: sums.shape[1], :LANES]
    sums[0] = jnp.where(lane_of(top.shape) >= LANES - SPARE, top, 0.0)
    sums[1] = folded(weighted[...] * increment)
    groups = own.shape[1]
    fields = []
    for k in range(main.shape[0]):
        field = main[k]
        slot, group = k // groups, k % groups
        ends = []
        for side, at in enumerate((0, LANES - EDGE)):
            moved = pltpu.roll(own[side, group], (at - slot * EDGE) % LANES, 1)
            lane = lane_of(moved.shape)
            ends.append(jnp.where((lane >= at) & (lane < at + EDGE), moved, 0.0))
        middle = [jnp.zeros((height, width - 2 * LANES), F32)] if width > 2 * LANES else []
        fields.append(field + jnp.concatenate([ends[0]] + middle + [ends[1]], axis=1))
    for copy in copies:
        copy.wait()
    lhs = split(beside(jnp.stack(fields), halo[0], halo[1], EDGE))
    out[...] = dot3(both(row), split(dot3(lhs, both(column)))).reshape(out.shape)


def filter_kernel(back, core, chip, column, row, out):
    groups, height = back.shape[0] * EDGE // LANES, back.shape[1]
    left, right = sides_of(*(x[: groups * height].reshape(groups, height, LANES) for x in (core, chip)))
    lhs = split(beside(back[...], left, right, EDGE))
    out[...] = dot3(both(row), split(dot3(lhs, both(column)))).reshape(out.shape)


def last_kernel(i0, i1, i2, i3, obs_weight, before, sums, members_ref, back, to_core, to_chip):
    levels, height, width = obs_weight.shape
    increment = ((i0[...] + i1[...]) + (i2[...] + i3[...])).reshape(obs_weight.shape)
    weighted = obs_weight[...] * increment
    four = [sums[0], sums[1], folded(before[...] * increment), folded(weighted * increment)]
    row = lax.broadcasted_iota(jnp.int32, (8, LANES), 0)
    stacked = jnp.zeros((8, LANES), F32)
    for i, part in enumerate(four):
        stacked = jnp.where(row == i, jnp.sum(part, axis=0, keepdims=True), stacked)
    back[...] = adjoint(members_ref, weighted)
    odd = lax.axis_index("tile") % 2 == 1
    first, last = pack_edges(back, EDGE, True), pack_edges(back, EDGE, False)
    rows = first.shape[0] * height
    to_core[:rows] = jnp.where(odd, first, last).reshape(rows, LANES)
    to_core[rows:] = stacked
    to_chip[...] = jnp.where(odd, last, first).reshape(rows, LANES)


def copy_kernel(value, after, out):
    out[...] = value[...]


def pass_kernel(value, after, out):
    pass


def combine_kernel(own, other, source, first, second, weights, residual, held_weights, held_residual, sems):
    total = jnp.sum(own[...] + other[...], axis=1, keepdims=True)
    bb, bg, gg, gh = (total[i : i + 1] for i in range(4))
    bg, gg, gh = bg / bb, gg / bb, gh / bb
    q = 1.0 / (1.0 + bg)
    p = bg * q
    ratio = (gg - bg * bg) * q * q
    d = p + ratio
    square = d * d - 2.0 * d * q * bg + q * q * gg
    image = d * d * bg - 2.0 * d * q * gg + q * q * gh
    step = ratio / (square + image)
    members = source.shape[0]
    pieces = sems.shape[1]
    copies = []
    for i in range(pieces):
        part = pl.ds(i * (members // pieces), members // pieces)
        b, g, h = source[part], first[part], second[part]
        held_weights[part] = (q + step * d) * b - (step * q) * g
        held_residual[part] = (p - step * d) * b + (step * q - q - step * d) * g + (step * q) * h
        for k, (held, out) in enumerate(((held_weights, weights), (held_residual, residual))):
            copies.append(pltpu.make_async_copy(held.at[part], out.at[part], sems.at[k, i]))
            copies[-1].start()
    for copy in copies:
        copy.wait()


def call(kernel, outs, *operands, cost=None):
    shapes = [jax.ShapeDtypeStruct(shape, F32) for shape in outs]
    vmem = pl.BlockSpec(memory_space=pltpu.VMEM)
    return pl.pallas_call(
        kernel,
        out_shape=shapes,
        in_specs=[vmem] * len(operands),
        out_specs=[vmem] * len(outs),
        compiler_params=pltpu.CompilerParams(vmem_limit_bytes=24 * 1024 * 1024),
        cost_estimate=cost,
    )(*operands)


def passed(value, after):
    vmem = pl.BlockSpec(memory_space=pltpu.VMEM)
    return pl.pallas_call(
        pass_kernel,
        out_shape=pltpu.VMEM(value.shape, value.dtype),
        in_specs=[vmem] * 2,
        out_specs=vmem,
        input_output_aliases={0: 0},
        compiler_params=pltpu.CompilerParams(vmem_limit_bytes=24 * 1024 * 1024),
        cost_estimate=LONG,
    )(value, after)


def in_hbm(array):
    return pltpu.with_memory_space_constraint(array, pltpu.HBM)


def held_edges(source, members_data, precision, covered):
    members, levels, height, width = members_data.shape
    groups = members * EDGE // LANES
    payload = ((groups * (2 + levels) + 1) * height, LANES)
    vmem = pl.BlockSpec(memory_space=pltpu.VMEM)
    hbm = pl.BlockSpec(memory_space=pltpu.HBM)
    arrays = (source, members_data, precision, covered)
    return pl.pallas_call(
        edges_kernel,
        out_shape=[
            pltpu.VMEM(source.shape, F32),
            pltpu.VMEM(members_data.shape, members_data.dtype),
            pltpu.VMEM(precision.shape, F32),
            pltpu.VMEM((2, groups, height, LANES), F32),
            pltpu.VMEM((2, height, LANES), F32),
            pltpu.VMEM((2, levels, groups, height, LANES), F32),
            pltpu.VMEM(payload, F32),
            pltpu.VMEM(payload, F32),
        ],
        in_specs=[hbm] * 4,
        out_specs=[vmem] * 8,
        scratch_shapes=[
            pltpu.VMEM(precision.shape, F32),
            pltpu.VMEM(covered.shape, covered.dtype),
            pltpu.SemaphoreType.DMA((4,)),
        ],
        compiler_params=pltpu.CompilerParams(vmem_limit_bytes=24 * 1024 * 1024),
    )(*map(in_hbm, arrays))


def first_increment(source, after, members_data):
    members, levels, height, width = members_data.shape
    groups = members * EDGE // LANES
    vmem = pl.BlockSpec(memory_space=pltpu.VMEM)
    return pl.pallas_call(
        first_kernel,
        out_shape=[
            pltpu.VMEM((levels * height, width), F32),
            pltpu.VMEM((8, LANES), F32),
            pltpu.VMEM((3, 2, LANES, LANES), BF16),
            pltpu.VMEM((2, groups * height, groups * height), BF16),
        ],
        in_specs=[vmem] * 3,
        out_specs=[vmem] * 4,
        compiler_params=pltpu.CompilerParams(vmem_limit_bytes=24 * 1024 * 1024),
        cost_estimate=LONG,
    )(source, after, members_data)


def call_with_constants(kernel, outs, kept, scratch, operands, constants):
    vmem = pl.BlockSpec(memory_space=pltpu.VMEM)
    hbm = pl.BlockSpec(memory_space=pltpu.HBM)
    held = [pltpu.VMEM(x.shape, x.dtype) for x in kept]
    return pl.pallas_call(
        kernel,
        out_shape=[pltpu.VMEM(shape, F32) for shape in outs] + held,
        in_specs=[vmem] * len(operands) + [hbm] * len(constants),
        out_specs=[vmem] * (len(outs) + len(kept)),
        scratch_shapes=[pltpu.VMEM(x.shape, x.dtype) for x in scratch] + [pltpu.SemaphoreType.DMA((len(constants),))],
        compiler_params=pltpu.CompilerParams(vmem_limit_bytes=24 * 1024 * 1024),
        cost_estimate=LONG,
    )(*operands, *map(in_hbm, constants))


def combined(own, other, source, first, second):
    vmem = pl.BlockSpec(memory_space=pltpu.VMEM)
    hbm = pl.BlockSpec(memory_space=pltpu.HBM)
    return pl.pallas_call(
        combine_kernel,
        out_shape=[jax.ShapeDtypeStruct(source.shape, F32)] * 2,
        in_specs=[vmem] * 5,
        out_specs=[hbm] * 2,
        scratch_shapes=[pltpu.VMEM(source.shape, F32)] * 2 + [pltpu.SemaphoreType.DMA((2, 4))],
        compiler_params=pltpu.CompilerParams(vmem_limit_bytes=24 * 1024 * 1024),
    )(own, other, source, first, second)


def from_both_sides(to_next, to_previous, axis):
    count = lax.axis_size(axis)
    left = lax.ppermute(to_next, axis, [(i, (i + 1) % count) for i in range(count)])
    right = lax.ppermute(to_previous, axis, [((i + 1) % count, i) for i in range(count)])
    return left, right


def from_tile(value, bit):
    count = lax.axis_size("tile")
    return lax.ppermute(value, "tile", [(i, i ^ bit) for i in range(count)])


def from_core(value):
    return from_tile(value, 1)


def from_chip(value):
    count = lax.axis_size("tile")
    return lax.ppermute(value, "tile", [(i, (i + 1) % count if i % 2 else (i - 1) % count) for i in range(count)])


def from_all(value, axis, order):
    count = lax.axis_size(axis)
    return [value] + [lax.ppermute(value, axis, [(i, i ^ k) for i in range(count)]) for k in order]


def one_tile_row(right_side, perturbations, precision, covered):
    source, members_data = right_side[0], perturbations[0]
    members, levels, height, width = members_data.shape
    groups = members * EDGE // LANES
    taps = taps_np()
    twice = np.convolve(taps, taps)
    field = (members, height, width)
    plane = (levels, height, width)
    flat = (levels * height, width)
    own = np.arange(width)

    source, members_data, obs_weight, near, near_weight, edge_members, to_core, to_chip = held_edges(
        source, members_data, precision[0], covered[0]
    )
    core, chip = from_core(to_core), from_chip(to_chip)
    inside, norm, edge, thin = first_increment(source, to_chip, members_data)
    inside = from_all(inside, "mem", (1, 2, 3))
    (outer,) = call(edge_kernel, [(2 * height, 2 * LANES)], norm, chip, core, near, edge_members, edge, thin)
    column_twice, row_twice = halves(band(twice, own, own)), halves(row_matrix(taps, height, members, 2))
    edge, thin = edge_matrix(twice, EDGE), halves(row_matrix(taps, height, groups, 2))
    constants = [column_twice, row_twice, edge, thin]
    next_members, column, row, edge, thin = call_with_constants(
        prepare_kernel, [edge_members.shape], constants, [], [outer, members_data], constants
    )
    increment, main, inside = call(
        main_kernel, [flat, field, flat], *inside, obs_weight, members_data, column, row
    )
    ends = (2, groups, height, LANES)
    outer, corrected, halo, second = call(
        correction_kernel, [outer.shape, ends, ends, flat],
        *from_all(outer, "mem", (3, 2, 1)), inside, near_weight, chip, core, edge_members, next_members, edge, thin,
    )
    parts = from_all(second, "mem", (2, 1, 3))
    column, row = halves(column_matrix(taps, width, EDGE)), halves(row_matrix(taps, height, members, 1))
    weighted, sums, first, column, row = call_with_constants(
        wide_filter_kernel, [plane, (2, 8, LANES), field], [column, row], [],
        [main, corrected, halo, increment, outer, obs_weight], [column, row],
    )
    back, to_core, to_chip = call(
        last_kernel,
        [field, (groups * height + 8, LANES), (groups * height, LANES)],
        *parts, obs_weight, weighted, sums, members_data,
    )
    core = from_core(to_core)
    sums = to_core[groups * height :] + core[groups * height :]
    (to_chip,) = call(copy_kernel, [to_chip.shape], to_chip, sums)
    chip = from_chip(to_chip)
    first = passed(first, sums)
    sums = sums + from_tile(sums, 3)
    others = from_tile(sums, 5)
    (second,) = call(filter_kernel, [field], back, core, chip, column, row, cost=LONG)
    weights, residual = combined(sums, others, source, first, second)
    return weights[None], residual[None]


def passed_along(value, axis, steps):
    count = lax.axis_size(axis)
    first, last = (max(0, -steps), min(count, count - steps))
    return lax.ppermute(value, axis, [(source, source + steps) for source in range(first, last)])


def smooth(field):
    taps = taps_np().astype(np.float32)
    height, width = field.shape[1:]
    above = passed_along(field[:, height - REACH :, :], "tile", TCOLS)
    below = passed_along(field[:, :REACH, :], "tile", -TCOLS)
    padded = jnp.concatenate([above, field, below], axis=1)
    along = sum(taps[j] * padded[:, j : j + height, :] for j in range(2 * REACH + 1))
    left, right = from_both_sides(along[:, :, width - REACH :], along[:, :, :REACH], "tile")
    sided = jnp.concatenate([left, along, right], axis=2)
    return sum(taps[j] * sided[:, :, j : j + width] for j in range(2 * REACH + 1))


def several_tile_rows(right_side, perturbations, precision, covered):
    source = right_side[0]
    members_data = perturbations[0].astype(F32)
    levels, height, width = precision.shape[1:]
    rows, blocks = covered.shape[1:]
    mask = covered[0].astype(F32)
    obs_weight = (
        precision[0].reshape(levels, rows, height // rows, blocks, width // blocks) * mask[None, :, None, :, None]
    ).reshape(levels, height, width)

    def operator(direction):
        partial_terms = jnp.einsum("kvyx,kyx->vyx", members_data, smooth(direction))
        weighted = obs_weight * lax.psum(partial_terms, "mem")
        return direction + smooth(jnp.einsum("kvyx,vyx->kyx", members_data, weighted))

    weights = jnp.zeros_like(source)
    residual = direction = source
    norm_now = lax.psum(jnp.sum(source * source), ("tile", "mem"))
    for step in range(ITERS):
        image = operator(direction)
        length = norm_now / lax.psum(jnp.sum(direction * image), ("tile", "mem"))
        weights = weights + length * direction
        residual = residual - length * image
        if step + 1 < ITERS:
            norm_next = lax.psum(jnp.sum(residual * residual), ("tile", "mem"))
            direction = residual + norm_next / norm_now * direction
            norm_now = norm_next
    return weights[None], residual[None]


def solution(mesh):
    single = mesh.shape["tile"] == TCOLS and mesh.shape["mem"] == 4
    local = one_tile_row if single else several_tile_rows
    return jax.shard_map(
        local,
        mesh=mesh,
        in_specs=(
            P("tile", "mem", None, None),
            P("tile", "mem", None, None, None),
            P("tile", None, None, None),
            P("tile", None, None),
        ),
        out_specs=(P("tile", "mem", None, None), P("tile", "mem", None, None)),
        check_vma=False,
    )
```

```python
import functools

import jax
import jax.numpy as jnp
import ml_dtypes
import numpy as np
from jax import lax
from jax.experimental import pallas as pl
from jax.experimental.pallas import tpu as pltpu
from jax.sharding import PartitionSpec as P

ITERS = 2
TCOLS = 8
REACH = 8
EDGE = 2 * REACH
SPARE = 32
LANES = 128
F32 = jnp.float32
BF16 = jnp.bfloat16
LONG = pl.CostEstimate(flops=10**9, bytes_accessed=10**6, transcendentals=0)


def taps_np():
    offsets = np.arange(-REACH, REACH + 1, dtype=np.float64)
    raw = np.exp(-offsets * offsets / 32.0)
    return raw / np.sqrt(np.sum(np.exp(-offsets * offsets / 16.0)))


def band(taps, source, target):
    reach = (len(taps) - 1) // 2
    gap = source[:, None] - target[None, :]
    inside = np.abs(gap) <= reach
    return np.where(inside, taps[np.clip(gap + reach, 0, 2 * reach)], 0.0)


def halves(matrix):
    whole = matrix.astype(np.float32)
    high = whole.astype(ml_dtypes.bfloat16)
    low = (whole - high.astype(np.float32)).astype(ml_dtypes.bfloat16)
    return np.stack([high, low])


def column_matrix(taps, width, edge):
    target = np.arange(width)
    slots = LANES // edge
    left = np.tile(np.arange(edge) - edge, slots)
    right = np.tile(np.arange(edge) + width, slots)
    return np.concatenate([band(taps, s, target) for s in (np.arange(width), left, right)])


def row_matrix(taps, height, members, times):
    one = band(taps, np.arange(height), np.arange(height))
    return np.kron(np.eye(members), np.linalg.matrix_power(one, times))


def edge_matrix(taps, edge):
    inner = np.arange(edge)
    return np.stack(
        [halves(np.kron(np.eye(LANES // edge), band(taps, inner + shift * edge, inner))) for shift in (-1, 0, 1)]
    )


def split(x):
    high = x.astype(BF16)
    return high, (x - high.astype(F32)).astype(BF16)


def dot3(left, right):
    mul = functools.partial(jnp.dot, preferred_element_type=F32)
    return mul(left[0], right[0]) + (mul(left[1], right[0]) + mul(left[0], right[1]))


def both(ref):
    return ref[0], ref[1]


def lane_of(shape):
    return lax.broadcasted_iota(jnp.int32, shape, len(shape) - 1)


def pack_columns(field, start, edge):
    members, rows, _ = field.shape
    slots = LANES // edge
    groups = members // slots
    lane = lane_of((rows, LANES))
    origin = start // LANES * LANES
    out = []
    for g in range(groups):
        total = jnp.zeros((rows, LANES), F32)
        for j in range(slots):
            block = field[j * groups + g][:, origin : origin + LANES]
            shift = (j * edge - (start - origin)) % LANES
            moved = pltpu.roll(block, shift, 1) if shift else block
            total = jnp.where((lane >= j * edge) & (lane < (j + 1) * edge), moved, total)
        out.append(total)
    return jnp.stack(out)


def pack_edges(field, edge, first):
    return pack_columns(field, 0 if first else field.shape[-1] - edge, edge)


def repeated(x, period):
    while period < LANES:
        x = x + pltpu.roll(x, period, len(x.shape) - 1)
        period *= 2
    return x


def level_lanes(shape, level):
    lane = lane_of(shape)
    return (lane >= level * EDGE) & (lane < (level + 1) * EDGE)


def sides_of(core, chip):
    odd = lax.axis_index("tile") % 2 == 1
    return jnp.where(odd, core, chip), jnp.where(odd, chip, core)


def spread_edges(packed, edge):
    groups, rows, _ = packed.shape
    slots = LANES // edge
    lane = lane_of((groups, rows, LANES))
    parts = [jnp.where((lane >= j * edge) & (lane < (j + 1) * edge), packed, 0.0) for j in range(slots)]
    return jnp.concatenate(parts, axis=0).reshape(slots * groups * rows, LANES)


def beside(field, left, right, edge):
    members, rows, width = field.shape
    return jnp.concatenate(
        [field.reshape(members * rows, width), spread_edges(left, edge), spread_edges(right, edge)], axis=1
    )


def increments(members_ref, smoothed):
    members, levels = members_ref.shape[:2]
    totals = []
    for v in range(levels):
        total = members_ref[0, v].astype(F32) * smoothed[0]
        for k in range(1, members):
            total = total + members_ref[k, v].astype(F32) * smoothed[k]
        totals.append(total)
    return jnp.stack(totals)


def adjoint(members_ref, weighted):
    members, levels = members_ref.shape[:2]
    back = []
    for k in range(members):
        total = members_ref[k, 0].astype(F32) * weighted[0]
        for v in range(1, levels):
            total = total + members_ref[k, v].astype(F32) * weighted[v]
        back.append(total)
    return jnp.stack(back)


def folded(x):
    width = x.shape[-1]
    x = x.reshape(-1, 8, width).sum(axis=0)
    return sum(x[:, i : i + LANES] for i in range(0, width, LANES))


def tap_at(gap, inside):
    scale = 1.0 / np.sqrt(np.sum(np.exp(-(np.arange(-REACH, REACH + 1.0) ** 2) / 16.0)))
    square = (gap * gap).astype(F32)
    return jnp.where(inside & (jnp.abs(gap) <= REACH), jnp.exp(square * (-1.0 / 32.0)) * scale, 0.0)


def gaps(rows, columns):
    shape = (rows, columns)
    down, across = (lax.broadcasted_iota(jnp.int32, shape, i) for i in range(2))
    return down, across, down - across


def kept(ref, matrix):
    ref[0], ref[1] = split(matrix)


def edges_kernel(
    source_hbm, members_hbm, precision_hbm, covered_hbm,
    source, members_ref, obs_weight, near, near_weight, edge_members, to_core, to_chip, column, row, edge, thin,
    precision, covered, sems,
):
    members, levels, height, width = members_ref.shape
    pairs = ((source_hbm, source), (precision_hbm, precision), (covered_hbm, covered), (members_hbm, members_ref))
    copies = [pltpu.make_async_copy(x, y, sems.at[i]) for i, (x, y) in enumerate(pairs)]
    for copy in copies:
        copy.start()
    groups = members * EDGE // LANES
    odd = lax.axis_index("tile") % 2 == 1
    rows = groups * height
    _, _, gap = gaps(width, width)
    kept(column, tap_at(gap, True))
    down, across, gap = gaps(members * height, members * height)
    kept(row, tap_at(gap, down // height == across // height))
    down, across, gap = gaps(LANES, LANES)
    same = down // EDGE == across // EDGE
    for i in range(3):
        kept(edge.at[i], tap_at(gap + (i - 1) * EDGE, same))
    down, across, gap = gaps(rows, rows)
    kept(thin, tap_at(gap, down // height == across // height))

    def send(at, first, last):
        first, last = (x.reshape(-1, LANES) for x in (first, last))
        part = pl.ds(at, first.shape[0])
        to_core[part] = jnp.where(odd, first, last)
        to_chip[part] = jnp.where(odd, last, first)

    copies[0].wait()
    near[0], near[1] = pack_columns(source, 0, EDGE), pack_columns(source, width - EDGE, EDGE)
    send(0, near[0], near[1])
    send(rows, pack_columns(source, EDGE, REACH), pack_columns(source, width - EDGE - REACH, REACH))
    copies[1].wait()
    copies[2].wait()
    obs_weight[...] = weight_of(precision, covered)
    for side, start in enumerate((0, width - EDGE)):
        total = jnp.zeros((height, LANES), F32)
        for v in range(levels):
            origin = start // LANES * LANES
            shift = (v * EDGE - (start - origin)) % LANES
            block = obs_weight[v, :, origin : origin + LANES]
            total = jnp.where(level_lanes(total.shape, v), pltpu.roll(block, shift, 1) if shift else block, total)
        near_weight[side] = total
    send(rows + rows // 2 + rows * levels, near_weight[0], near_weight[1])
    copies[3].wait()
    for v in range(levels):
        level = members_ref[:, v].astype(F32)
        edge_members[0, v], edge_members[1, v] = pack_edges(level, EDGE, True), pack_edges(level, EDGE, False)
        send(rows + rows // 2 + rows * v, edge_members[0, v], edge_members[1, v])


def own_columns(field, column, row):
    members, height, width = field.shape
    lhs = split(field[...].reshape(members * height, width))
    return dot3(both(row), split(dot3(lhs, both(column)))).reshape(field.shape)


def first_kernel(source, after, members_ref, column, row, increment, norm):
    increment[...] = increments(members_ref, own_columns(source, column, row)).reshape(increment.shape)
    norm[...] = repeated(folded(source[...] * source[...]), SPARE)


def edge_terms(edge_members, smoothed):
    groups, height = edge_members.shape[1:3]
    return jnp.sum(edge_members * smoothed.reshape(1, groups, height, LANES), axis=1)


def in_slot(shape, slot):
    lane = lane_of(shape)
    return (lane >= slot * EDGE) & (lane < (slot + 1) * EDGE)


def add_columns(out, start, terms):
    levels, height, _ = terms[0].shape
    origin = start // LANES * LANES
    first = (start - origin) // EDGE
    even, odd = terms if first % 2 == 0 else terms[::-1]
    even, odd = (x.reshape(levels * height, LANES) for x in (even, odd))
    lane = lane_of(even.shape)
    total = jnp.where(
        lane // EDGE % 2 == 0,
        even + pltpu.roll(even, LANES - EDGE, 1),
        odd + pltpu.roll(odd, EDGE, 1),
    )
    total = repeated(total, 2 * EDGE)
    mask = (lane >= start - origin) & (lane < start - origin + 2 * EDGE)
    rows, span = pl.ds(0, levels * height), pl.ds(origin, LANES)
    out[rows, span] = out[rows, span] + jnp.where(mask, total, 0.0)


def beside_levels(terms):
    levels, shape = terms.shape[0], terms.shape[1:]
    slots = LANES // EDGE
    moved = []
    for k in range(slots):
        part = jnp.zeros(shape, F32)
        for slot in range(slots):
            level = (slot + k) % slots
            if level < levels:
                part = jnp.where(in_slot(shape, slot), terms[level], part)
        moved.append(pltpu.roll(part, k * EDGE, 1) if k else part)
    while len(moved) > 1:
        moved = [x + y for x, y in zip(moved[::2], moved[1::2])]
    return moved[0]


def apart_levels(packed, levels):
    slots = LANES // EDGE
    turned = [packed] + [pltpu.roll(packed, EDGE * k, 1) for k in range(1, slots)]
    lane = lane_of(packed.shape)
    out = []
    for v in range(levels):
        parts, width = [turned[(slot - v) % slots] for slot in range(slots)], EDGE
        while len(parts) > 1:
            left = lane // width % 2 == 0
            parts = [jnp.where(left, x, y) for x, y in zip(parts[::2], parts[1::2])]
            width *= 2
        out.append(parts[0])
    return out


def halo_members(block, rows, groups, levels):
    start = rows + rows // 2
    return block[start : start + levels * rows].reshape(levels, groups, rows // groups, LANES)


def halo_weight(block, rows, levels):
    return block[rows + rows // 2 + levels * rows :]


def farther_columns(block, rows, side):
    packed = block[rows : rows + rows // 2]
    lane = lane_of(packed.shape)
    if side == 0:
        halves_of = (pltpu.roll(packed, REACH, 1), packed)
        mask = lane % EDGE >= REACH
    else:
        halves_of = (packed, pltpu.roll(packed, LANES - REACH, 1))
        mask = lane % EDGE < REACH
    return jnp.concatenate([jnp.where(mask, x, 0.0) for x in halves_of], axis=0)


def edge_kernel(norm, chip, core, near, edge_members, edge, thin, out):
    levels, groups, height = edge_members.shape[1:4]
    rows = groups * height
    sides = sides_of(core[...], chip[...])
    parts = []
    for side, block in enumerate(sides):
        here = [farther_columns(block, rows, side), block[:rows], near[side].reshape(rows, LANES)]
        parts += here if side == 0 else here[::-1]
    filtered = dot3(both(thin), split(jnp.concatenate(parts, axis=1)))
    filtered = split(jnp.concatenate([filtered[:, : 3 * LANES], filtered[:, 3 * LANES :]], axis=0))
    beyond = dot3(filtered, [jnp.concatenate([edge[i, k] for i in range(3)], axis=0) for k in range(2)])
    middle = tuple(x[:, LANES : 2 * LANES] for x in filtered)
    for side, block in enumerate(sides):
        own = slice(side * rows, (side + 1) * rows)
        within = dot3(tuple(x[own] for x in middle), both(edge.at[2 * side]))
        lanes = pl.ds(side * LANES, LANES)
        out[:height, lanes] = beside_levels(edge_terms(edge_members[side], within))
        out[height:, lanes] = beside_levels(edge_terms(halo_members(block, rows, groups, levels), beyond[own]))
    lane = lane_of(norm.shape)
    top = pl.ds(0, norm.shape[0])
    out[top, :LANES] = jnp.where(lane >= LANES - SPARE, norm[...], out[top, :LANES])


def weight_of(precision, covered):
    levels, height, width = precision.shape
    rows, blocks = covered.shape
    spread = lax.broadcasted_iota(jnp.int32, (blocks, width), 1) // (width // blocks)
    spread = (spread == lax.broadcasted_iota(jnp.int32, (blocks, width), 0)).astype(BF16)
    mask = jnp.dot(covered[...].astype(F32).astype(BF16), spread, preferred_element_type=F32)
    tall = height // rows
    mask = jnp.concatenate([jnp.broadcast_to(mask[i : i + 1], (tall, width)) for i in range(rows)], axis=0)
    return precision[...] * mask


def packed_adjoint(members, weighted):
    total = jnp.zeros(members.shape[1:], F32)
    for v, level in enumerate(apart_levels(weighted, members.shape[0])):
        total = total + members[v] * level
    return total


def prepare_kernel(
    after, members_ref, column_hbm, row_hbm, edge_hbm, thin_hbm, next_members, column, row, edge, thin, sems
):
    pairs = ((column_hbm, column), (row_hbm, row), (edge_hbm, edge), (thin_hbm, thin))
    copies = [pltpu.make_async_copy(x, y, sems.at[i]) for i, (x, y) in enumerate(pairs)]
    for copy in copies:
        copy.start()
    levels, width = members_ref.shape[1], members_ref.shape[-1]
    for v in range(levels):
        level = members_ref[:, v].astype(F32)
        next_members[0, v] = pack_columns(level, EDGE, EDGE)
        next_members[1, v] = pack_columns(level, width - 2 * EDGE, EDGE)
    for copy in copies:
        copy.wait()


def main_kernel(i0, i1, i2, i3, obs_weight, members_ref, column, row, first, back, second):
    first[...] = (i0[...] + i1[...]) + (i2[...] + i3[...])
    back[...] = adjoint(members_ref, obs_weight[...] * first[...].reshape(obs_weight.shape))
    second[...] = increments(members_ref, own_columns(back, column, row)).reshape(second.shape)


def correction_kernel(
    e0, e1, e2, e3, main, near_weight, chip, core, edge_members, next_members, edge, thin, outer, own, halo, out
):
    levels, groups, height = edge_members.shape[1:4]
    width = out.shape[-1]
    rows = groups * height
    outer[...] = (e0[...] + e1[...]) + (e2[...] + e3[...])
    out[...] = main[...]
    for side, block in enumerate(sides_of(core[...], chip[...])):
        lanes = pl.ds(side * LANES, LANES)
        own[side] = packed_adjoint(edge_members[side], outer[:height, lanes] * near_weight[side])
        halo[side] = packed_adjoint(
            halo_members(block, rows, groups, levels), outer[height:, lanes] * halo_weight(block, rows, levels)
        )
    parts = [x[side].reshape(rows, LANES) for side in range(2) for x in (halo, own)]
    filtered = split(dot3(both(thin), split(jnp.concatenate(parts, axis=1))))
    for side in range(2):
        span = slice(2 * side * LANES, 2 * (side + 1) * LANES)
        matrix = [jnp.concatenate([edge[2 * side, k], edge[1, k]], axis=0) for k in range(2)]
        outermost = dot3(tuple(x[:, span] for x in filtered), matrix)
        inner = dot3(tuple(x[:, span.start + LANES : span.stop] for x in filtered), both(edge.at[2 * side]))
        blocks = [edge_terms(edge_members[side], outermost), edge_terms(next_members[side], inner)]
        if side == 0:
            add_columns(out, 0, blocks)
        else:
            add_columns(out, width - 2 * EDGE, blocks[::-1])


def wide_filter_kernel(
    main, own, halo, first, outer, obs_weight, column_hbm, row_hbm, weighted, sums, out, column, row, sems
):
    copies = [pltpu.make_async_copy(x, y, sems.at[i]) for i, (x, y) in enumerate(((column_hbm, column), (row_hbm, row)))]
    for copy in copies:
        copy.start()
    levels, height, width = obs_weight.shape
    weighted[...] = first[...].reshape(obs_weight.shape)
    for side, start in enumerate((0, width - EDGE)):
        origin = start // LANES * LANES
        lane = lane_of((height, LANES))
        mask = (lane >= start - origin) & (lane < start - origin + EDGE)
        for v, level in enumerate(apart_levels(outer[:height, pl.ds(side * LANES, LANES)], levels)):
            span = pl.ds(origin, LANES)
            weighted[v, :, span] = weighted[v, :, span] + jnp.where(mask, level, 0.0)
    increment = weighted[...]
    weighted[...] = obs_weight[...] * increment
    top = outer[: sums.shape[1], :LANES]
    sums[0] = jnp.where(lane_of(top.shape) >= LANES - SPARE, top, 0.0)
    sums[1] = folded(weighted[...] * increment)
    groups = own.shape[1]
    fields = []
    for k in range(main.shape[0]):
        field = main[k]
        slot, group = k // groups, k % groups
        ends = []
        for side, at in enumerate((0, LANES - EDGE)):
            moved = pltpu.roll(own[side, group], (at - slot * EDGE) % LANES, 1)
            lane = lane_of(moved.shape)
            ends.append(jnp.where((lane >= at) & (lane < at + EDGE), moved, 0.0))
        middle = [jnp.zeros((height, width - 2 * LANES), F32)] if width > 2 * LANES else []
        fields.append(field + jnp.concatenate([ends[0]] + middle + [ends[1]], axis=1))
    for copy in copies:
        copy.wait()
    lhs = split(beside(jnp.stack(fields), halo[0], halo[1], EDGE))
    out[...] = dot3(both(row), split(dot3(lhs, both(column)))).reshape(out.shape)


def filter_kernel(back, core, chip, column, row, out):
    groups, height = back.shape[0] * EDGE // LANES, back.shape[1]
    left, right = sides_of(*(x[: groups * height].reshape(groups, height, LANES) for x in (core, chip)))
    lhs = split(beside(back[...], left, right, EDGE))
    out[...] = dot3(both(row), split(dot3(lhs, both(column)))).reshape(out.shape)


def norms_kernel(i0, i1, i2, i3, obs_weight, before, sums, weighted, norms):
    increment = ((i0[...] + i1[...]) + (i2[...] + i3[...])).reshape(obs_weight.shape)
    weighted[...] = obs_weight[...] * increment
    four = [sums[0], sums[1], folded(before[...] * increment), folded(weighted[...] * increment)]
    row = lax.broadcasted_iota(jnp.int32, (8, LANES), 0)
    stacked = jnp.zeros((8, LANES), F32)
    for i, part in enumerate(four):
        stacked = jnp.where(row == i, jnp.sum(part, axis=0, keepdims=True), stacked)
    norms[...] = stacked


def last_kernel(weighted, members_ref, back, to_core, to_chip):
    height = back.shape[1]
    back[...] = adjoint(members_ref, weighted)
    odd = lax.axis_index("tile") % 2 == 1
    first, last = pack_edges(back, EDGE, True), pack_edges(back, EDGE, False)
    rows = first.shape[0] * height
    to_core[...] = jnp.where(odd, first, last).reshape(rows, LANES)
    to_chip[...] = jnp.where(odd, last, first).reshape(rows, LANES)


def copy_kernel(value, after, out):
    out[...] = value[...]


def pass_kernel(value, after, out):
    pass


def combine_kernel(own, other, source, first, second, weights, residual, held_weights, held_residual, sems):
    total = jnp.sum(own[...] + other[...], axis=1, keepdims=True)
    bb, bg, gg, gh = (total[i : i + 1] for i in range(4))
    bg, gg, gh = bg / bb, gg / bb, gh / bb
    q = 1.0 / (1.0 + bg)
    p = bg * q
    ratio = (gg - bg * bg) * q * q
    d = p + ratio
    square = d * d - 2.0 * d * q * bg + q * q * gg
    image = d * d * bg - 2.0 * d * q * gg + q * q * gh
    step = ratio / (square + image)
    members = source.shape[0]
    pieces = sems.shape[1]
    copies = []
    for i in range(pieces):
        part = pl.ds(i * (members // pieces), members // pieces)
        b, g, h = source[part], first[part], second[part]
        held_weights[part] = (q + step * d) * b - (step * q) * g
        held_residual[part] = (p - step * d) * b + (step * q - q - step * d) * g + (step * q) * h
        for k, (held, out) in enumerate(((held_weights, weights), (held_residual, residual))):
            copies.append(pltpu.make_async_copy(held.at[part], out.at[part], sems.at[k, i]))
            copies[-1].start()
    for copy in copies:
        copy.wait()


def call(kernel, outs, *operands, cost=None):
    shapes = [jax.ShapeDtypeStruct(shape, F32) for shape in outs]
    vmem = pl.BlockSpec(memory_space=pltpu.VMEM)
    return pl.pallas_call(
        kernel,
        out_shape=shapes,
        in_specs=[vmem] * len(operands),
        out_specs=[vmem] * len(outs),
        compiler_params=pltpu.CompilerParams(vmem_limit_bytes=24 * 1024 * 1024),
        cost_estimate=cost,
    )(*operands)


def passed(value, after):
    vmem = pl.BlockSpec(memory_space=pltpu.VMEM)
    return pl.pallas_call(
        pass_kernel,
        out_shape=pltpu.VMEM(value.shape, value.dtype),
        in_specs=[vmem] * 2,
        out_specs=vmem,
        input_output_aliases={0: 0},
        compiler_params=pltpu.CompilerParams(vmem_limit_bytes=24 * 1024 * 1024),
        cost_estimate=LONG,
    )(value, after)


def in_hbm(array):
    return pltpu.with_memory_space_constraint(array, pltpu.HBM)


def held_edges(source, members_data, precision, covered):
    members, levels, height, width = members_data.shape
    groups = members * EDGE // LANES
    rows = groups * height
    payload = (rows + rows // 2 + rows * levels + height, LANES)
    vmem = pl.BlockSpec(memory_space=pltpu.VMEM)
    hbm = pl.BlockSpec(memory_space=pltpu.HBM)
    arrays = (source, members_data, precision, covered)
    return pl.pallas_call(
        edges_kernel,
        out_shape=[
            pltpu.VMEM(source.shape, F32),
            pltpu.VMEM(members_data.shape, members_data.dtype),
            pltpu.VMEM(precision.shape, F32),
            pltpu.VMEM((2, groups, height, LANES), F32),
            pltpu.VMEM((2, height, LANES), F32),
            pltpu.VMEM((2, levels, groups, height, LANES), F32),
            pltpu.VMEM(payload, F32),
            pltpu.VMEM(payload, F32),
            pltpu.VMEM((2, width, width), BF16),
            pltpu.VMEM((2, members * height, members * height), BF16),
            pltpu.VMEM((3, 2, LANES, LANES), BF16),
            pltpu.VMEM((2, groups * height, groups * height), BF16),
        ],
        in_specs=[hbm] * 4,
        out_specs=[vmem] * 12,
        scratch_shapes=[
            pltpu.VMEM(precision.shape, F32),
            pltpu.VMEM(covered.shape, covered.dtype),
            pltpu.SemaphoreType.DMA((4,)),
        ],
        compiler_params=pltpu.CompilerParams(vmem_limit_bytes=24 * 1024 * 1024),
    )(*map(in_hbm, arrays))


def first_increment(source, after, members_data, column, row):
    _, levels, height, width = members_data.shape
    vmem = pl.BlockSpec(memory_space=pltpu.VMEM)
    return pl.pallas_call(
        first_kernel,
        out_shape=[pltpu.VMEM((levels * height, width), F32), pltpu.VMEM((8, LANES), F32)],
        in_specs=[vmem] * 5,
        out_specs=[vmem] * 2,
        compiler_params=pltpu.CompilerParams(vmem_limit_bytes=24 * 1024 * 1024),
        cost_estimate=LONG,
    )(source, after, members_data, column, row)


def call_with_constants(kernel, outs, kept, scratch, operands, constants):
    vmem = pl.BlockSpec(memory_space=pltpu.VMEM)
    hbm = pl.BlockSpec(memory_space=pltpu.HBM)
    held = [pltpu.VMEM(x.shape, x.dtype) for x in kept]
    return pl.pallas_call(
        kernel,
        out_shape=[pltpu.VMEM(shape, F32) for shape in outs] + held,
        in_specs=[vmem] * len(operands) + [hbm] * len(constants),
        out_specs=[vmem] * (len(outs) + len(kept)),
        scratch_shapes=[pltpu.VMEM(x.shape, x.dtype) for x in scratch] + [pltpu.SemaphoreType.DMA((len(constants),))],
        compiler_params=pltpu.CompilerParams(vmem_limit_bytes=24 * 1024 * 1024),
        cost_estimate=LONG,
    )(*operands, *map(in_hbm, constants))


def combined(own, other, source, first, second):
    vmem = pl.BlockSpec(memory_space=pltpu.VMEM)
    hbm = pl.BlockSpec(memory_space=pltpu.HBM)
    return pl.pallas_call(
        combine_kernel,
        out_shape=[jax.ShapeDtypeStruct(source.shape, F32)] * 2,
        in_specs=[vmem] * 5,
        out_specs=[hbm] * 2,
        scratch_shapes=[pltpu.VMEM(source.shape, F32)] * 2 + [pltpu.SemaphoreType.DMA((2, 4))],
        compiler_params=pltpu.CompilerParams(vmem_limit_bytes=24 * 1024 * 1024),
    )(own, other, source, first, second)


def from_both_sides(to_next, to_previous, axis):
    count = lax.axis_size(axis)
    left = lax.ppermute(to_next, axis, [(i, (i + 1) % count) for i in range(count)])
    right = lax.ppermute(to_previous, axis, [((i + 1) % count, i) for i in range(count)])
    return left, right


def from_tile(value, bit):
    count = lax.axis_size("tile")
    return lax.ppermute(value, "tile", [(i, i ^ bit) for i in range(count)])


def from_core(value):
    return from_tile(value, 1)


def from_chip(value):
    count = lax.axis_size("tile")
    return lax.ppermute(value, "tile", [(i, (i + 1) % count if i % 2 else (i - 1) % count) for i in range(count)])


def from_all(value, axis, order):
    count = lax.axis_size(axis)
    return [value] + [lax.ppermute(value, axis, [(i, i ^ k) for i in range(count)]) for k in order]


def one_tile_row(right_side, perturbations, precision, covered):
    source, members_data = right_side[0], perturbations[0]
    members, levels, height, width = members_data.shape
    groups = members * EDGE // LANES
    taps = taps_np()
    twice = np.convolve(taps, taps)
    field = (members, height, width)
    plane = (levels, height, width)
    flat = (levels * height, width)
    own = np.arange(width)

    held = held_edges(source, members_data, precision[0], covered[0])
    source, members_data, obs_weight, near, near_weight, edge_members, to_core, to_chip, column, row, edge, thin = held
    core, chip = from_core(to_core), from_chip(to_chip)
    inside, norm = first_increment(source, to_chip, members_data, column, row)
    inside = from_all(inside, "mem", (1, 2, 3))
    (outer,) = call(edge_kernel, [(2 * height, 2 * LANES)], norm, chip, core, near, edge_members, edge, thin)
    column_twice, row_twice = halves(band(twice, own, own)), halves(row_matrix(taps, height, members, 2))
    edge, thin = edge_matrix(twice, EDGE), halves(row_matrix(taps, height, groups, 2))
    constants = [column_twice, row_twice, edge, thin]
    next_members, column, row, edge, thin = call_with_constants(
        prepare_kernel, [edge_members.shape], constants, [], [outer, members_data], constants
    )
    increment, main, inside = call(
        main_kernel, [flat, field, flat], *inside, obs_weight, members_data, column, row
    )
    ends = (2, groups, height, LANES)
    outer, corrected, halo, second = call(
        correction_kernel, [outer.shape, ends, ends, flat],
        *from_all(outer, "mem", (3, 2, 1)), inside, near_weight, chip, core, edge_members, next_members, edge, thin,
    )
    parts = from_all(second, "mem", (2, 1, 3))
    column, row = halves(column_matrix(taps, width, EDGE)), halves(row_matrix(taps, height, members, 1))
    weighted, sums, first, column, row = call_with_constants(
        wide_filter_kernel, [plane, (2, 8, LANES), field], [column, row], [],
        [main, corrected, halo, increment, outer, obs_weight], [column, row],
    )
    weighted, sums = call(norms_kernel, [plane, (8, LANES)], *parts, obs_weight, weighted, sums)
    ends = (groups * height, LANES)
    back, to_core, to_chip = call(last_kernel, [field, ends, ends], weighted, members_data)
    sums = sums + from_core(sums)
    core = from_core(to_core)
    (to_chip,) = call(copy_kernel, [to_chip.shape], to_chip, sums)
    chip = from_chip(to_chip)
    first = passed(first, sums)
    sums = sums + from_tile(sums, 5)
    others = from_tile(sums, 3)
    (second,) = call(filter_kernel, [field], back, core, chip, column, row, cost=LONG)
    weights, residual = combined(sums, others, source, first, second)
    return weights[None], residual[None]


def passed_along(value, axis, steps):
    count = lax.axis_size(axis)
    first, last = (max(0, -steps), min(count, count - steps))
    return lax.ppermute(value, axis, [(source, source + steps) for source in range(first, last)])


def smooth(field):
    taps = taps_np().astype(np.float32)
    height, width = field.shape[1:]
    above = passed_along(field[:, height - REACH :, :], "tile", TCOLS)
    below = passed_along(field[:, :REACH, :], "tile", -TCOLS)
    padded = jnp.concatenate([above, field, below], axis=1)
    along = sum(taps[j] * padded[:, j : j + height, :] for j in range(2 * REACH + 1))
    left, right = from_both_sides(along[:, :, width - REACH :], along[:, :, :REACH], "tile")
    sided = jnp.concatenate([left, along, right], axis=2)
    return sum(taps[j] * sided[:, :, j : j + width] for j in range(2 * REACH + 1))


def several_tile_rows(right_side, perturbations, precision, covered):
    source = right_side[0]
    members_data = perturbations[0].astype(F32)
    levels, height, width = precision.shape[1:]
    rows, blocks = covered.shape[1:]
    mask = covered[0].astype(F32)
    obs_weight = (
        precision[0].reshape(levels, rows, height // rows, blocks, width // blocks) * mask[None, :, None, :, None]
    ).reshape(levels, height, width)

    def operator(direction):
        partial_terms = jnp.einsum("kvyx,kyx->vyx", members_data, smooth(direction))
        weighted = obs_weight * lax.psum(partial_terms, "mem")
        return direction + smooth(jnp.einsum("kvyx,vyx->kyx", members_data, weighted))

    weights = jnp.zeros_like(source)
    residual = direction = source
    norm_now = lax.psum(jnp.sum(source * source), ("tile", "mem"))
    for step in range(ITERS):
        image = operator(direction)
        length = norm_now / lax.psum(jnp.sum(direction * image), ("tile", "mem"))
        weights = weights + length * direction
        residual = residual - length * image
        if step + 1 < ITERS:
            norm_next = lax.psum(jnp.sum(residual * residual), ("tile", "mem"))
            direction = residual + norm_next / norm_now * direction
            norm_now = norm_next
    return weights[None], residual[None]


def solution(mesh):
    single = mesh.shape["tile"] == TCOLS and mesh.shape["mem"] == 4
    local = one_tile_row if single else several_tile_rows
    return jax.shard_map(
        local,
        mesh=mesh,
        in_specs=(
            P("tile", "mem", None, None),
            P("tile", "mem", None, None, None),
            P("tile", None, None, None),
            P("tile", None, None),
        ),
        out_specs=(P("tile", "mem", None, None), P("tile", "mem", None, None)),
        check_vma=False,
    )
```

```python
import functools

import jax
import jax.numpy as jnp
import ml_dtypes
import numpy as np
from jax import lax
from jax.experimental import pallas as pl
from jax.experimental.pallas import tpu as pltpu
from jax.sharding import PartitionSpec as P

ITERS = 2
TCOLS = 8
REACH = 8
EDGE = 2 * REACH
SPARE = 32
LANES = 128
F32 = jnp.float32
BF16 = jnp.bfloat16
LONG = pl.CostEstimate(flops=10**9, bytes_accessed=10**6, transcendentals=0)


def taps_np():
    offsets = np.arange(-REACH, REACH + 1, dtype=np.float64)
    raw = np.exp(-offsets * offsets / 32.0)
    return raw / np.sqrt(np.sum(np.exp(-offsets * offsets / 16.0)))


def band(taps, source, target):
    reach = (len(taps) - 1) // 2
    gap = source[:, None] - target[None, :]
    inside = np.abs(gap) <= reach
    return np.where(inside, taps[np.clip(gap + reach, 0, 2 * reach)], 0.0)


def halves(matrix):
    whole = matrix.astype(np.float32)
    high = whole.astype(ml_dtypes.bfloat16)
    low = (whole - high.astype(np.float32)).astype(ml_dtypes.bfloat16)
    return np.stack([high, low])


def column_matrix(taps, width, edge):
    target = np.arange(width)
    slots = LANES // edge
    left = np.tile(np.arange(edge) - edge, slots)
    right = np.tile(np.arange(edge) + width, slots)
    return np.concatenate([band(taps, s, target) for s in (np.arange(width), left, right)])


def row_matrix(taps, height, members, times):
    one = band(taps, np.arange(height), np.arange(height))
    return np.kron(np.eye(members), np.linalg.matrix_power(one, times))


def edge_matrix(taps, edge):
    inner = np.arange(edge)
    return np.stack(
        [halves(np.kron(np.eye(LANES // edge), band(taps, inner + shift * edge, inner))) for shift in (-1, 0, 1)]
    )


def split(x):
    high = x.astype(BF16)
    return high, (x - high.astype(F32)).astype(BF16)


def dot3(left, right):
    mul = functools.partial(jnp.dot, preferred_element_type=F32)
    return mul(left[0], right[0]) + (mul(left[1], right[0]) + mul(left[0], right[1]))


def thin3(thin, x):
    high, low = split(x)
    left = jnp.concatenate([thin[0], thin[1], thin[0]], axis=1)
    return jnp.dot(left, jnp.concatenate([high, high, low], axis=0), preferred_element_type=F32)


def both(ref):
    return ref[0], ref[1]


def lane_of(shape):
    return lax.broadcasted_iota(jnp.int32, shape, len(shape) - 1)


def pack_columns(field, start, edge):
    members, rows, _ = field.shape
    slots = LANES // edge
    groups = members // slots
    lane = lane_of((rows, LANES))
    origin = start // LANES * LANES
    out = []
    for g in range(groups):
        total = jnp.zeros((rows, LANES), F32)
        for j in range(slots):
            block = field[j * groups + g][:, origin : origin + LANES]
            shift = (j * edge - (start - origin)) % LANES
            moved = pltpu.roll(block, shift, 1) if shift else block
            total = jnp.where((lane >= j * edge) & (lane < (j + 1) * edge), moved, total)
        out.append(total)
    return jnp.stack(out)


def pack_edges(field, edge, first):
    return pack_columns(field, 0 if first else field.shape[-1] - edge, edge)


def repeated(x, period):
    while period < LANES:
        x = x + pltpu.roll(x, period, len(x.shape) - 1)
        period *= 2
    return x


def level_lanes(shape, level):
    lane = lane_of(shape)
    return (lane >= level * EDGE) & (lane < (level + 1) * EDGE)


def sides_of(core, chip):
    odd = lax.axis_index("tile") % 2 == 1
    return jnp.where(odd, core, chip), jnp.where(odd, chip, core)


def spread_edges(packed, edge):
    groups, rows, _ = packed.shape
    slots = LANES // edge
    lane = lane_of((groups, rows, LANES))
    parts = [jnp.where((lane >= j * edge) & (lane < (j + 1) * edge), packed, 0.0) for j in range(slots)]
    return jnp.concatenate(parts, axis=0).reshape(slots * groups * rows, LANES)


def beside(field, left, right, edge):
    members, rows, width = field.shape
    return jnp.concatenate(
        [field.reshape(members * rows, width), spread_edges(left, edge), spread_edges(right, edge)], axis=1
    )


def increments(members_ref, smoothed):
    members, levels = members_ref.shape[:2]
    totals = []
    for v in range(levels):
        total = members_ref[0, v].astype(F32) * smoothed[0]
        for k in range(1, members):
            total = total + members_ref[k, v].astype(F32) * smoothed[k]
        totals.append(total)
    return jnp.stack(totals)


def adjoint(members_ref, weighted):
    members, levels = members_ref.shape[:2]
    back = []
    for k in range(members):
        total = members_ref[k, 0].astype(F32) * weighted[0]
        for v in range(1, levels):
            total = total + members_ref[k, v].astype(F32) * weighted[v]
        back.append(total)
    return jnp.stack(back)


def folded(x):
    width = x.shape[-1]
    x = x.reshape(-1, 8, width).sum(axis=0)
    return sum(x[:, i : i + LANES] for i in range(0, width, LANES))


def tap_at(gap, inside):
    scale = 1.0 / np.sqrt(np.sum(np.exp(-(np.arange(-REACH, REACH + 1.0) ** 2) / 16.0)))
    square = (gap * gap).astype(F32)
    return jnp.where(inside & (jnp.abs(gap) <= REACH), jnp.exp(square * (-1.0 / 32.0)) * scale, 0.0)


def gaps(rows, columns):
    shape = (rows, columns)
    down, across = (lax.broadcasted_iota(jnp.int32, shape, i) for i in range(2))
    return down, across, down - across


def kept(ref, matrix):
    ref[0], ref[1] = split(matrix)


def edges_kernel(
    source_hbm, members_hbm, precision_hbm, covered_hbm,
    source, members_ref, obs_weight, near, near_weight, edge_members, to_core, to_chip, column, row, edge, thin,
    precision, covered, sems,
):
    members, levels, height, width = members_ref.shape
    pairs = ((source_hbm, source), (precision_hbm, precision), (covered_hbm, covered), (members_hbm, members_ref))
    copies = [pltpu.make_async_copy(x, y, sems.at[i]) for i, (x, y) in enumerate(pairs)]
    for copy in copies:
        copy.start()
    groups = members * EDGE // LANES
    odd = lax.axis_index("tile") % 2 == 1
    rows = groups * height
    _, _, gap = gaps(width, width)
    kept(column, tap_at(gap, True))
    down, across, gap = gaps(members * height, members * height)
    kept(row, tap_at(gap, down // height == across // height))
    down, across, gap = gaps(LANES, LANES)
    same = down // EDGE == across // EDGE
    for i in range(3):
        kept(edge.at[i], tap_at(gap + (i - 1) * EDGE, same))
    down, across, gap = gaps(rows, rows)
    kept(thin, tap_at(gap, down // height == across // height))

    def send(at, first, last):
        first, last = (x.reshape(-1, LANES) for x in (first, last))
        part = pl.ds(at, first.shape[0])
        to_core[part] = jnp.where(odd, first, last)
        to_chip[part] = jnp.where(odd, last, first)

    copies[0].wait()
    near[0], near[1] = pack_columns(source, 0, EDGE), pack_columns(source, width - EDGE, EDGE)
    send(0, near[0], near[1])
    send(rows, pack_columns(source, EDGE, REACH), pack_columns(source, width - EDGE - REACH, REACH))
    copies[1].wait()
    copies[2].wait()
    obs_weight[...] = weight_of(precision, covered)
    for side, start in enumerate((0, width - EDGE)):
        total = jnp.zeros((height, LANES), F32)
        for v in range(levels):
            origin = start // LANES * LANES
            shift = (v * EDGE - (start - origin)) % LANES
            block = obs_weight[v, :, origin : origin + LANES]
            total = jnp.where(level_lanes(total.shape, v), pltpu.roll(block, shift, 1) if shift else block, total)
        near_weight[side] = total
    send(rows + rows // 2 + rows * levels, near_weight[0], near_weight[1])
    copies[3].wait()
    for v in range(levels):
        level = members_ref[:, v].astype(F32)
        edge_members[0, v], edge_members[1, v] = pack_edges(level, EDGE, True), pack_edges(level, EDGE, False)
        send(rows + rows // 2 + rows * v, edge_members[0, v], edge_members[1, v])


def own_columns(field, column, row):
    members, height, width = field.shape
    lhs = split(field[...].reshape(members * height, width))
    return dot3(both(row), split(dot3(lhs, both(column)))).reshape(field.shape)


def first_kernel(source, after, members_ref, column, row, increment, norm):
    increment[...] = increments(members_ref, own_columns(source, column, row)).reshape(increment.shape)
    norm[...] = repeated(folded(source[...] * source[...]), SPARE)


def edge_terms(edge_members, smoothed):
    groups, height = edge_members.shape[1:3]
    return jnp.sum(edge_members * smoothed.reshape(1, groups, height, LANES), axis=1)


def in_slot(shape, slot):
    lane = lane_of(shape)
    return (lane >= slot * EDGE) & (lane < (slot + 1) * EDGE)


def add_columns(out, start, terms):
    levels, height, _ = terms[0].shape
    origin = start // LANES * LANES
    first = (start - origin) // EDGE
    even, odd = terms if first % 2 == 0 else terms[::-1]
    even, odd = (x.reshape(levels * height, LANES) for x in (even, odd))
    lane = lane_of(even.shape)
    total = jnp.where(
        lane // EDGE % 2 == 0,
        even + pltpu.roll(even, LANES - EDGE, 1),
        odd + pltpu.roll(odd, EDGE, 1),
    )
    total = repeated(total, 2 * EDGE)
    mask = (lane >= start - origin) & (lane < start - origin + 2 * EDGE)
    rows, span = pl.ds(0, levels * height), pl.ds(origin, LANES)
    out[rows, span] = out[rows, span] + jnp.where(mask, total, 0.0)


def beside_levels(terms):
    levels, shape = terms.shape[0], terms.shape[1:]
    slots = LANES // EDGE
    moved = []
    for k in range(slots):
        part = jnp.zeros(shape, F32)
        for slot in range(slots):
            level = (slot + k) % slots
            if level < levels:
                part = jnp.where(in_slot(shape, slot), terms[level], part)
        moved.append(pltpu.roll(part, k * EDGE, 1) if k else part)
    while len(moved) > 1:
        moved = [x + y for x, y in zip(moved[::2], moved[1::2])]
    return moved[0]


def apart_levels(packed, levels):
    slots = LANES // EDGE
    turned = [packed] + [pltpu.roll(packed, EDGE * k, 1) for k in range(1, slots)]
    lane = lane_of(packed.shape)
    out = []
    for v in range(levels):
        parts, width = [turned[(slot - v) % slots] for slot in range(slots)], EDGE
        while len(parts) > 1:
            left = lane // width % 2 == 0
            parts = [jnp.where(left, x, y) for x, y in zip(parts[::2], parts[1::2])]
            width *= 2
        out.append(parts[0])
    return out


def halo_members(block, rows, groups, levels):
    start = rows + rows // 2
    return block[start : start + levels * rows].reshape(levels, groups, rows // groups, LANES)


def halo_weight(block, rows, levels):
    return block[rows + rows // 2 + levels * rows :]


def farther_columns(block, rows, side):
    packed = block[rows : rows + rows // 2]
    lane = lane_of(packed.shape)
    if side == 0:
        halves_of = (pltpu.roll(packed, REACH, 1), packed)
        mask = lane % EDGE >= REACH
    else:
        halves_of = (packed, pltpu.roll(packed, LANES - REACH, 1))
        mask = lane % EDGE < REACH
    return jnp.concatenate([jnp.where(mask, x, 0.0) for x in halves_of], axis=0)


def edge_kernel(norm, chip, core, near, edge_members, edge, thin, out):
    levels, groups, height = edge_members.shape[1:4]
    rows = groups * height
    sides = sides_of(core[...], chip[...])
    parts = []
    for side, block in enumerate(sides):
        here = [farther_columns(block, rows, side), block[:rows], near[side].reshape(rows, LANES)]
        parts += here if side == 0 else here[::-1]
    filtered = thin3(thin, jnp.concatenate(parts, axis=1))
    filtered = split(jnp.concatenate([filtered[:, : 3 * LANES], filtered[:, 3 * LANES :]], axis=0))
    beyond = dot3(filtered, [jnp.concatenate([edge[i, k] for i in range(3)], axis=0) for k in range(2)])
    middle = tuple(x[:, LANES : 2 * LANES] for x in filtered)
    for side, block in enumerate(sides):
        own = slice(side * rows, (side + 1) * rows)
        within = dot3(tuple(x[own] for x in middle), both(edge.at[2 * side]))
        lanes = pl.ds(side * LANES, LANES)
        out[:height, lanes] = beside_levels(edge_terms(edge_members[side], within))
        out[height:, lanes] = beside_levels(edge_terms(halo_members(block, rows, groups, levels), beyond[own]))
    lane = lane_of(norm.shape)
    top = pl.ds(0, norm.shape[0])
    out[top, :LANES] = jnp.where(lane >= LANES - SPARE, norm[...], out[top, :LANES])


def weight_of(precision, covered):
    levels, height, width = precision.shape
    rows, blocks = covered.shape
    spread = lax.broadcasted_iota(jnp.int32, (blocks, width), 1) // (width // blocks)
    spread = (spread == lax.broadcasted_iota(jnp.int32, (blocks, width), 0)).astype(BF16)
    mask = jnp.dot(covered[...].astype(F32).astype(BF16), spread, preferred_element_type=F32)
    tall = height // rows
    mask = jnp.concatenate([jnp.broadcast_to(mask[i : i + 1], (tall, width)) for i in range(rows)], axis=0)
    return precision[...] * mask


def packed_adjoint(members, weighted):
    total = jnp.zeros(members.shape[1:], F32)
    for v, level in enumerate(apart_levels(weighted, members.shape[0])):
        total = total + members[v] * level
    return total


def prepare_kernel(
    after, members_ref, column_hbm, row_hbm, edge_hbm, thin_hbm, next_members, column, row, edge, thin, sems
):
    pairs = ((column_hbm, column), (row_hbm, row), (edge_hbm, edge), (thin_hbm, thin))
    copies = [pltpu.make_async_copy(x, y, sems.at[i]) for i, (x, y) in enumerate(pairs)]
    for copy in copies:
        copy.start()
    levels, width = members_ref.shape[1], members_ref.shape[-1]
    for v in range(levels):
        level = members_ref[:, v].astype(F32)
        next_members[0, v] = pack_columns(level, EDGE, EDGE)
        next_members[1, v] = pack_columns(level, width - 2 * EDGE, EDGE)
    for copy in copies:
        copy.wait()


def main_kernel(i0, i1, i2, i3, obs_weight, members_ref, column, row, first, back, second):
    first[...] = (i0[...] + i1[...]) + (i2[...] + i3[...])
    back[...] = adjoint(members_ref, obs_weight[...] * first[...].reshape(obs_weight.shape))
    second[...] = increments(members_ref, own_columns(back, column, row)).reshape(second.shape)


def correction_kernel(
    e0, e1, e2, e3, main, near_weight, chip, core, edge_members, next_members, edge, thin, outer, own, halo, out
):
    levels, groups, height = edge_members.shape[1:4]
    width = out.shape[-1]
    rows = groups * height
    outer[...] = (e0[...] + e1[...]) + (e2[...] + e3[...])
    out[...] = main[...]
    for side, block in enumerate(sides_of(core[...], chip[...])):
        lanes = pl.ds(side * LANES, LANES)
        own[side] = packed_adjoint(edge_members[side], outer[:height, lanes] * near_weight[side])
        halo[side] = packed_adjoint(
            halo_members(block, rows, groups, levels), outer[height:, lanes] * halo_weight(block, rows, levels)
        )
    parts = [x[side].reshape(rows, LANES) for side in range(2) for x in (halo, own)]
    filtered = split(thin3(thin, jnp.concatenate(parts, axis=1)))
    for side in range(2):
        span = slice(2 * side * LANES, 2 * (side + 1) * LANES)
        matrix = [jnp.concatenate([edge[2 * side, k], edge[1, k]], axis=0) for k in range(2)]
        outermost = dot3(tuple(x[:, span] for x in filtered), matrix)
        inner = dot3(tuple(x[:, span.start + LANES : span.stop] for x in filtered), both(edge.at[2 * side]))
        blocks = [edge_terms(edge_members[side], outermost), edge_terms(next_members[side], inner)]
        if side == 0:
            add_columns(out, 0, blocks)
        else:
            add_columns(out, width - 2 * EDGE, blocks[::-1])


def wide_filter_kernel(
    main, own, halo, first, outer, obs_weight, column_hbm, row_hbm, weighted, sums, out, column, row, sems
):
    copies = [pltpu.make_async_copy(x, y, sems.at[i]) for i, (x, y) in enumerate(((column_hbm, column), (row_hbm, row)))]
    for copy in copies:
        copy.start()
    levels, height, width = obs_weight.shape
    weighted[...] = first[...].reshape(obs_weight.shape)
    for side, start in enumerate((0, width - EDGE)):
        origin = start // LANES * LANES
        lane = lane_of((height, LANES))
        mask = (lane >= start - origin) & (lane < start - origin + EDGE)
        for v, level in enumerate(apart_levels(outer[:height, pl.ds(side * LANES, LANES)], levels)):
            span = pl.ds(origin, LANES)
            weighted[v, :, span] = weighted[v, :, span] + jnp.where(mask, level, 0.0)
    increment = weighted[...]
    weighted[...] = obs_weight[...] * increment
    top = outer[: sums.shape[1], :LANES]
    sums[0] = jnp.where(lane_of(top.shape) >= LANES - SPARE, top, 0.0)
    sums[1] = folded(weighted[...] * increment)
    groups = own.shape[1]
    fields = []
    for k in range(main.shape[0]):
        field = main[k]
        slot, group = k // groups, k % groups
        ends = []
        for side, at in enumerate((0, LANES - EDGE)):
            moved = pltpu.roll(own[side, group], (at - slot * EDGE) % LANES, 1)
            lane = lane_of(moved.shape)
            ends.append(jnp.where((lane >= at) & (lane < at + EDGE), moved, 0.0))
        middle = [jnp.zeros((height, width - 2 * LANES), F32)] if width > 2 * LANES else []
        fields.append(field + jnp.concatenate([ends[0]] + middle + [ends[1]], axis=1))
    for copy in copies:
        copy.wait()
    lhs = split(beside(jnp.stack(fields), halo[0], halo[1], EDGE))
    out[...] = dot3(both(row), split(dot3(lhs, both(column)))).reshape(out.shape)


def filter_kernel(back, core, chip, column, row, out):
    groups, height = back.shape[0] * EDGE // LANES, back.shape[1]
    left, right = sides_of(*(x[: groups * height].reshape(groups, height, LANES) for x in (core, chip)))
    lhs = split(beside(back[...], left, right, EDGE))
    out[...] = dot3(both(row), split(dot3(lhs, both(column)))).reshape(out.shape)


def norms_kernel(i0, i1, i2, i3, obs_weight, before, sums, weighted, norms):
    increment = ((i0[...] + i1[...]) + (i2[...] + i3[...])).reshape(obs_weight.shape)
    weighted[...] = obs_weight[...] * increment
    four = [sums[0], sums[1], folded(before[...] * increment), folded(weighted[...] * increment)]
    row = lax.broadcasted_iota(jnp.int32, (8, LANES), 0)
    stacked = jnp.zeros((8, LANES), F32)
    for i, part in enumerate(four):
        stacked = jnp.where(row == i, jnp.sum(part, axis=0, keepdims=True), stacked)
    norms[...] = stacked


def last_kernel(weighted, members_ref, back, to_core, to_chip):
    height = back.shape[1]
    back[...] = adjoint(members_ref, weighted)
    odd = lax.axis_index("tile") % 2 == 1
    first, last = pack_edges(back, EDGE, True), pack_edges(back, EDGE, False)
    rows = first.shape[0] * height
    to_core[...] = jnp.where(odd, first, last).reshape(rows, LANES)
    to_chip[...] = jnp.where(odd, last, first).reshape(rows, LANES)


def copy_kernel(value, after, out):
    out[...] = value[...]


def pass_kernel(value, after, out):
    pass


def combine_kernel(own, other, source, first, second, weights, residual, held_weights, held_residual, sems):
    total = jnp.sum(own[...] + other[...], axis=1, keepdims=True)
    bb, bg, gg, gh = (total[i : i + 1] for i in range(4))
    bg, gg, gh = bg / bb, gg / bb, gh / bb
    q = 1.0 / (1.0 + bg)
    p = bg * q
    ratio = (gg - bg * bg) * q * q
    d = p + ratio
    square = d * d - 2.0 * d * q * bg + q * q * gg
    image = d * d * bg - 2.0 * d * q * gg + q * q * gh
    step = ratio / (square + image)
    members = source.shape[0]
    pieces = sems.shape[1]
    copies = []
    for i in range(pieces):
        part = pl.ds(i * (members // pieces), members // pieces)
        b, g, h = source[part], first[part], second[part]
        held_weights[part] = (q + step * d) * b - (step * q) * g
        held_residual[part] = (p - step * d) * b + (step * q - q - step * d) * g + (step * q) * h
        for k, (held, out) in enumerate(((held_weights, weights), (held_residual, residual))):
            copies.append(pltpu.make_async_copy(held.at[part], out.at[part], sems.at[k, i]))
            copies[-1].start()
    for copy in copies:
        copy.wait()


def call(kernel, outs, *operands, cost=None):
    shapes = [jax.ShapeDtypeStruct(shape, F32) for shape in outs]
    vmem = pl.BlockSpec(memory_space=pltpu.VMEM)
    return pl.pallas_call(
        kernel,
        out_shape=shapes,
        in_specs=[vmem] * len(operands),
        out_specs=[vmem] * len(outs),
        compiler_params=pltpu.CompilerParams(vmem_limit_bytes=24 * 1024 * 1024),
        cost_estimate=cost,
    )(*operands)


def passed(value, after):
    vmem = pl.BlockSpec(memory_space=pltpu.VMEM)
    return pl.pallas_call(
        pass_kernel,
        out_shape=pltpu.VMEM(value.shape, value.dtype),
        in_specs=[vmem] * 2,
        out_specs=vmem,
        input_output_aliases={0: 0},
        compiler_params=pltpu.CompilerParams(vmem_limit_bytes=24 * 1024 * 1024),
        cost_estimate=LONG,
    )(value, after)


def in_hbm(array):
    return pltpu.with_memory_space_constraint(array, pltpu.HBM)


def held_edges(source, members_data, precision, covered):
    members, levels, height, width = members_data.shape
    groups = members * EDGE // LANES
    rows = groups * height
    payload = (rows + rows // 2 + rows * levels + height, LANES)
    vmem = pl.BlockSpec(memory_space=pltpu.VMEM)
    hbm = pl.BlockSpec(memory_space=pltpu.HBM)
    arrays = (source, members_data, precision, covered)
    return pl.pallas_call(
        edges_kernel,
        out_shape=[
            pltpu.VMEM(source.shape, F32),
            pltpu.VMEM(members_data.shape, members_data.dtype),
            pltpu.VMEM(precision.shape, F32),
            pltpu.VMEM((2, groups, height, LANES), F32),
            pltpu.VMEM((2, height, LANES), F32),
            pltpu.VMEM((2, levels, groups, height, LANES), F32),
            pltpu.VMEM(payload, F32),
            pltpu.VMEM(payload, F32),
            pltpu.VMEM((2, width, width), BF16),
            pltpu.VMEM((2, members * height, members * height), BF16),
            pltpu.VMEM((3, 2, LANES, LANES), BF16),
            pltpu.VMEM((2, groups * height, groups * height), BF16),
        ],
        in_specs=[hbm] * 4,
        out_specs=[vmem] * 12,
        scratch_shapes=[
            pltpu.VMEM(precision.shape, F32),
            pltpu.VMEM(covered.shape, covered.dtype),
            pltpu.SemaphoreType.DMA((4,)),
        ],
        compiler_params=pltpu.CompilerParams(vmem_limit_bytes=24 * 1024 * 1024),
    )(*map(in_hbm, arrays))


def first_increment(source, after, members_data, column, row):
    _, levels, height, width = members_data.shape
    vmem = pl.BlockSpec(memory_space=pltpu.VMEM)
    return pl.pallas_call(
        first_kernel,
        out_shape=[pltpu.VMEM((levels * height, width), F32), pltpu.VMEM((8, LANES), F32)],
        in_specs=[vmem] * 5,
        out_specs=[vmem] * 2,
        compiler_params=pltpu.CompilerParams(vmem_limit_bytes=24 * 1024 * 1024),
        cost_estimate=LONG,
    )(source, after, members_data, column, row)


def call_with_constants(kernel, outs, kept, scratch, operands, constants):
    vmem = pl.BlockSpec(memory_space=pltpu.VMEM)
    hbm = pl.BlockSpec(memory_space=pltpu.HBM)
    held = [pltpu.VMEM(x.shape, x.dtype) for x in kept]
    return pl.pallas_call(
        kernel,
        out_shape=[pltpu.VMEM(shape, F32) for shape in outs] + held,
        in_specs=[vmem] * len(operands) + [hbm] * len(constants),
        out_specs=[vmem] * (len(outs) + len(kept)),
        scratch_shapes=[pltpu.VMEM(x.shape, x.dtype) for x in scratch] + [pltpu.SemaphoreType.DMA((len(constants),))],
        compiler_params=pltpu.CompilerParams(vmem_limit_bytes=24 * 1024 * 1024),
        cost_estimate=LONG,
    )(*operands, *map(in_hbm, constants))


def combined(own, other, source, first, second):
    vmem = pl.BlockSpec(memory_space=pltpu.VMEM)
    hbm = pl.BlockSpec(memory_space=pltpu.HBM)
    return pl.pallas_call(
        combine_kernel,
        out_shape=[jax.ShapeDtypeStruct(source.shape, F32)] * 2,
        in_specs=[vmem] * 5,
        out_specs=[hbm] * 2,
        scratch_shapes=[pltpu.VMEM(source.shape, F32)] * 2 + [pltpu.SemaphoreType.DMA((2, 4))],
        compiler_params=pltpu.CompilerParams(vmem_limit_bytes=24 * 1024 * 1024),
    )(own, other, source, first, second)


def from_both_sides(to_next, to_previous, axis):
    count = lax.axis_size(axis)
    left = lax.ppermute(to_next, axis, [(i, (i + 1) % count) for i in range(count)])
    right = lax.ppermute(to_previous, axis, [((i + 1) % count, i) for i in range(count)])
    return left, right


def from_tile(value, bit):
    count = lax.axis_size("tile")
    return lax.ppermute(value, "tile", [(i, i ^ bit) for i in range(count)])


def from_core(value):
    return from_tile(value, 1)


def from_chip(value):
    count = lax.axis_size("tile")
    return lax.ppermute(value, "tile", [(i, (i + 1) % count if i % 2 else (i - 1) % count) for i in range(count)])


def from_all(value, axis, order):
    count = lax.axis_size(axis)
    return [value] + [lax.ppermute(value, axis, [(i, i ^ k) for i in range(count)]) for k in order]


def one_tile_row(right_side, perturbations, precision, covered):
    source, members_data = right_side[0], perturbations[0]
    members, levels, height, width = members_data.shape
    groups = members * EDGE // LANES
    taps = taps_np()
    twice = np.convolve(taps, taps)
    field = (members, height, width)
    plane = (levels, height, width)
    flat = (levels * height, width)
    own = np.arange(width)

    held = held_edges(source, members_data, precision[0], covered[0])
    source, members_data, obs_weight, near, near_weight, edge_members, to_core, to_chip, column, row, edge, thin = held
    core, chip = from_core(to_core), from_chip(to_chip)
    inside, norm = first_increment(source, to_chip, members_data, column, row)
    inside = from_all(inside, "mem", (1, 2, 3))
    (outer,) = call(edge_kernel, [(2 * height, 2 * LANES)], norm, chip, core, near, edge_members, edge, thin)
    column_twice, row_twice = halves(band(twice, own, own)), halves(row_matrix(taps, height, members, 2))
    edge, thin = edge_matrix(twice, EDGE), halves(row_matrix(taps, height, groups, 2))
    constants = [column_twice, row_twice, edge, thin]
    next_members, column, row, edge, thin = call_with_constants(
        prepare_kernel, [edge_members.shape], constants, [], [outer, members_data], constants
    )
    increment, main, inside = call(
        main_kernel, [flat, field, flat], *inside, obs_weight, members_data, column, row
    )
    ends = (2, groups, height, LANES)
    outer, corrected, halo, second = call(
        correction_kernel, [outer.shape, ends, ends, flat],
        *from_all(outer, "mem", (3, 2, 1)), inside, near_weight, chip, core, edge_members, next_members, edge, thin,
    )
    parts = from_all(second, "mem", (2, 1, 3))
    column, row = halves(column_matrix(taps, width, EDGE)), halves(row_matrix(taps, height, members, 1))
    weighted, sums, first, column, row = call_with_constants(
        wide_filter_kernel, [plane, (2, 8, LANES), field], [column, row], [],
        [main, corrected, halo, increment, outer, obs_weight], [column, row],
    )
    weighted, sums = call(norms_kernel, [plane, (8, LANES)], *parts, obs_weight, weighted, sums)
    ends = (groups * height, LANES)
    back, to_core, to_chip = call(last_kernel, [field, ends, ends], weighted, members_data)
    sums = sums + from_core(sums)
    core = from_core(to_core)
    (to_chip,) = call(copy_kernel, [to_chip.shape], to_chip, sums)
    chip = from_chip(to_chip)
    first = passed(first, sums)
    sums = sums + from_tile(sums, 5)
    others = from_tile(sums, 3)
    (second,) = call(filter_kernel, [field], back, core, chip, column, row, cost=LONG)
    weights, residual = combined(sums, others, source, first, second)
    return weights[None], residual[None]


def passed_along(value, axis, steps):
    count = lax.axis_size(axis)
    first, last = (max(0, -steps), min(count, count - steps))
    return lax.ppermute(value, axis, [(source, source + steps) for source in range(first, last)])


def smooth(field):
    taps = taps_np().astype(np.float32)
    height, width = field.shape[1:]
    above = passed_along(field[:, height - REACH :, :], "tile", TCOLS)
    below = passed_along(field[:, :REACH, :], "tile", -TCOLS)
    padded = jnp.concatenate([above, field, below], axis=1)
    along = sum(taps[j] * padded[:, j : j + height, :] for j in range(2 * REACH + 1))
    left, right = from_both_sides(along[:, :, width - REACH :], along[:, :, :REACH], "tile")
    sided = jnp.concatenate([left, along, right], axis=2)
    return sum(taps[j] * sided[:, :, j : j + width] for j in range(2 * REACH + 1))


def several_tile_rows(right_side, perturbations, precision, covered):
    source = right_side[0]
    members_data = perturbations[0].astype(F32)
    levels, height, width = precision.shape[1:]
    rows, blocks = covered.shape[1:]
    mask = covered[0].astype(F32)
    obs_weight = (
        precision[0].reshape(levels, rows, height // rows, blocks, width // blocks) * mask[None, :, None, :, None]
    ).reshape(levels, height, width)

    def operator(direction):
        partial_terms = jnp.einsum("kvyx,kyx->vyx", members_data, smooth(direction))
        weighted = obs_weight * lax.psum(partial_terms, "mem")
        return direction + smooth(jnp.einsum("kvyx,vyx->kyx", members_data, weighted))

    weights = jnp.zeros_like(source)
    residual = direction = source
    norm_now = lax.psum(jnp.sum(source * source), ("tile", "mem"))
    for step in range(ITERS):
        image = operator(direction)
        length = norm_now / lax.psum(jnp.sum(direction * image), ("tile", "mem"))
        weights = weights + length * direction
        residual = residual - length * image
        if step + 1 < ITERS:
            norm_next = lax.psum(jnp.sum(residual * residual), ("tile", "mem"))
            direction = residual + norm_next / norm_now * direction
            norm_now = norm_next
    return weights[None], residual[None]


def solution(mesh):
    single = mesh.shape["tile"] == TCOLS and mesh.shape["mem"] == 4
    local = one_tile_row if single else several_tile_rows
    return jax.shard_map(
        local,
        mesh=mesh,
        in_specs=(
            P("tile", "mem", None, None),
            P("tile", "mem", None, None, None),
            P("tile", None, None, None),
            P("tile", None, None),
        ),
        out_specs=(P("tile", "mem", None, None), P("tile", "mem", None, None)),
        check_vma=False,
    )
```

```python
import functools

import jax
import jax.numpy as jnp
import ml_dtypes
import numpy as np
from jax import lax
from jax.experimental import pallas as pl
from jax.experimental.pallas import tpu as pltpu
from jax.sharding import PartitionSpec as P

ITERS = 2
TCOLS = 8
REACH = 8
EDGE = 2 * REACH
SPARE = 32
LANES = 128
F32 = jnp.float32
BF16 = jnp.bfloat16
LONG = pl.CostEstimate(flops=10**9, bytes_accessed=10**6, transcendentals=0)


def taps_np():
    offsets = np.arange(-REACH, REACH + 1, dtype=np.float64)
    raw = np.exp(-offsets * offsets / 32.0)
    return raw / np.sqrt(np.sum(np.exp(-offsets * offsets / 16.0)))


def band(taps, source, target):
    reach = (len(taps) - 1) // 2
    gap = source[:, None] - target[None, :]
    inside = np.abs(gap) <= reach
    return np.where(inside, taps[np.clip(gap + reach, 0, 2 * reach)], 0.0)


def halves(matrix):
    whole = matrix.astype(np.float32)
    high = whole.astype(ml_dtypes.bfloat16)
    low = (whole - high.astype(np.float32)).astype(ml_dtypes.bfloat16)
    return np.stack([high, low])


def column_matrix(taps, width, edge):
    target = np.arange(width)
    slots = LANES // edge
    left = np.tile(np.arange(edge) - edge, slots)
    right = np.tile(np.arange(edge) + width, slots)
    return np.concatenate([band(taps, s, target) for s in (np.arange(width), left, right)])


def row_matrix(taps, height, members, times):
    one = band(taps, np.arange(height), np.arange(height))
    return np.kron(np.eye(members), np.linalg.matrix_power(one, times))


def edge_matrix(taps, edge):
    inner = np.arange(edge)
    return np.stack(
        [halves(np.kron(np.eye(LANES // edge), band(taps, inner + shift * edge, inner))) for shift in (-1, 0, 1)]
    )


def split(x):
    high = x.astype(BF16)
    return high, (x - high.astype(F32)).astype(BF16)


def dot3(left, right):
    mul = functools.partial(jnp.dot, preferred_element_type=F32)
    if left[0].shape[1] == LANES:
        return mul(
            jnp.concatenate([left[0], left[1], left[0]], axis=1), jnp.concatenate([right[0], right[0], right[1]], axis=0)
        )
    return mul(left[0], right[0]) + (mul(left[1], right[0]) + mul(left[0], right[1]))


def thin3(thin, x):
    high, low = split(x)
    left = jnp.concatenate([thin[0], thin[1], thin[0]], axis=1)
    return jnp.dot(left, jnp.concatenate([high, high, low], axis=0), preferred_element_type=F32)


def both(ref):
    return ref[0], ref[1]


def lane_of(shape):
    return lax.broadcasted_iota(jnp.int32, shape, len(shape) - 1)


def pack_columns(field, start, edge):
    members, rows, _ = field.shape
    slots = LANES // edge
    groups = members // slots
    lane = lane_of((rows, LANES))
    origin = start // LANES * LANES
    out = []
    for g in range(groups):
        total = jnp.zeros((rows, LANES), F32)
        for j in range(slots):
            block = field[j * groups + g][:, origin : origin + LANES]
            shift = (j * edge - (start - origin)) % LANES
            moved = pltpu.roll(block, shift, 1) if shift else block
            total = jnp.where((lane >= j * edge) & (lane < (j + 1) * edge), moved, total)
        out.append(total)
    return jnp.stack(out)


def pack_edges(field, edge, first):
    return pack_columns(field, 0 if first else field.shape[-1] - edge, edge)


def repeated(x, period):
    while period < LANES:
        x = x + pltpu.roll(x, period, len(x.shape) - 1)
        period *= 2
    return x


def level_lanes(shape, level):
    lane = lane_of(shape)
    return (lane >= level * EDGE) & (lane < (level + 1) * EDGE)


def sides_of(core, chip):
    odd = lax.axis_index("tile") % 2 == 1
    return jnp.where(odd, core, chip), jnp.where(odd, chip, core)


def spread_edges(packed, edge):
    groups, rows, _ = packed.shape
    slots = LANES // edge
    lane = lane_of((groups, rows, LANES))
    parts = [jnp.where((lane >= j * edge) & (lane < (j + 1) * edge), packed, 0.0) for j in range(slots)]
    return jnp.concatenate(parts, axis=0).reshape(slots * groups * rows, LANES)


def beside(field, left, right, edge):
    members, rows, width = field.shape
    return jnp.concatenate(
        [field.reshape(members * rows, width), spread_edges(left, edge), spread_edges(right, edge)], axis=1
    )


def increments(members_ref, smoothed):
    members, levels = members_ref.shape[:2]
    totals = []
    for v in range(levels):
        total = members_ref[0, v].astype(F32) * smoothed[0]
        for k in range(1, members):
            total = total + members_ref[k, v].astype(F32) * smoothed[k]
        totals.append(total)
    return jnp.stack(totals)


def adjoint(members_ref, weighted):
    members, levels = members_ref.shape[:2]
    back = []
    for k in range(members):
        total = members_ref[k, 0].astype(F32) * weighted[0]
        for v in range(1, levels):
            total = total + members_ref[k, v].astype(F32) * weighted[v]
        back.append(total)
    return jnp.stack(back)


def folded(x):
    width = x.shape[-1]
    x = x.reshape(-1, 8, width).sum(axis=0)
    return sum(x[:, i : i + LANES] for i in range(0, width, LANES))


def tap_at(gap, inside):
    scale = 1.0 / np.sqrt(np.sum(np.exp(-(np.arange(-REACH, REACH + 1.0) ** 2) / 16.0)))
    square = (gap * gap).astype(F32)
    return jnp.where(inside & (jnp.abs(gap) <= REACH), jnp.exp(square * (-1.0 / 32.0)) * scale, 0.0)


def gaps(rows, columns):
    shape = (rows, columns)
    down, across = (lax.broadcasted_iota(jnp.int32, shape, i) for i in range(2))
    return down, across, down - across


def kept(ref, matrix):
    ref[0], ref[1] = split(matrix)


def edges_kernel(
    source_hbm, members_hbm, precision_hbm, covered_hbm,
    source, members_ref, obs_weight, near, near_weight, edge_members, to_core, to_chip, column, row, edge, thin,
    precision, covered, sems,
):
    members, levels, height, width = members_ref.shape
    pairs = ((source_hbm, source), (precision_hbm, precision), (covered_hbm, covered), (members_hbm, members_ref))
    copies = [pltpu.make_async_copy(x, y, sems.at[i]) for i, (x, y) in enumerate(pairs)]
    for copy in copies:
        copy.start()
    groups = members * EDGE // LANES
    odd = lax.axis_index("tile") % 2 == 1
    rows = groups * height
    _, _, gap = gaps(width, width)
    kept(column, tap_at(gap, True))
    down, across, gap = gaps(members * height, members * height)
    kept(row, tap_at(gap, down // height == across // height))
    down, across, gap = gaps(LANES, LANES)
    same = down // EDGE == across // EDGE
    for i in range(3):
        kept(edge.at[i], tap_at(gap + (i - 1) * EDGE, same))
    down, across, gap = gaps(rows, rows)
    kept(thin, tap_at(gap, down // height == across // height))

    def send(at, first, last):
        first, last = (x.reshape(-1, LANES) for x in (first, last))
        part = pl.ds(at, first.shape[0])
        to_core[part] = jnp.where(odd, first, last)
        to_chip[part] = jnp.where(odd, last, first)

    copies[0].wait()
    near[0], near[1] = pack_columns(source, 0, EDGE), pack_columns(source, width - EDGE, EDGE)
    send(0, near[0], near[1])
    send(rows, pack_columns(source, EDGE, REACH), pack_columns(source, width - EDGE - REACH, REACH))
    copies[1].wait()
    copies[2].wait()
    obs_weight[...] = weight_of(precision, covered)
    for side, start in enumerate((0, width - EDGE)):
        total = jnp.zeros((height, LANES), F32)
        for v in range(levels):
            origin = start // LANES * LANES
            shift = (v * EDGE - (start - origin)) % LANES
            block = obs_weight[v, :, origin : origin + LANES]
            total = jnp.where(level_lanes(total.shape, v), pltpu.roll(block, shift, 1) if shift else block, total)
        near_weight[side] = total
    send(rows + rows // 2 + rows * levels, near_weight[0], near_weight[1])
    copies[3].wait()
    for v in range(levels):
        level = members_ref[:, v].astype(F32)
        edge_members[0, v], edge_members[1, v] = pack_edges(level, EDGE, True), pack_edges(level, EDGE, False)
        send(rows + rows // 2 + rows * v, edge_members[0, v], edge_members[1, v])


def own_columns(field, column, row):
    members, height, width = field.shape
    lhs = split(field[...].reshape(members * height, width))
    return dot3(both(row), split(dot3(lhs, both(column)))).reshape(field.shape)


def first_kernel(source, after, members_ref, column, row, increment, norm):
    increment[...] = increments(members_ref, own_columns(source, column, row)).reshape(increment.shape)
    norm[...] = repeated(folded(source[...] * source[...]), SPARE)


def edge_terms(edge_members, smoothed):
    groups, height = edge_members.shape[1:3]
    return jnp.sum(edge_members * smoothed.reshape(1, groups, height, LANES), axis=1)


def in_slot(shape, slot):
    lane = lane_of(shape)
    return (lane >= slot * EDGE) & (lane < (slot + 1) * EDGE)


def add_columns(out, start, terms):
    levels, height, _ = terms[0].shape
    origin = start // LANES * LANES
    first = (start - origin) // EDGE
    even, odd = terms if first % 2 == 0 else terms[::-1]
    even, odd = (x.reshape(levels * height, LANES) for x in (even, odd))
    lane = lane_of(even.shape)
    total = jnp.where(
        lane // EDGE % 2 == 0,
        even + pltpu.roll(even, LANES - EDGE, 1),
        odd + pltpu.roll(odd, EDGE, 1),
    )
    total = repeated(total, 2 * EDGE)
    mask = (lane >= start - origin) & (lane < start - origin + 2 * EDGE)
    rows, span = pl.ds(0, levels * height), pl.ds(origin, LANES)
    out[rows, span] = out[rows, span] + jnp.where(mask, total, 0.0)


def beside_levels(terms):
    levels, shape = terms.shape[0], terms.shape[1:]
    slots = LANES // EDGE
    moved = []
    for k in range(slots):
        part = jnp.zeros(shape, F32)
        for slot in range(slots):
            level = (slot + k) % slots
            if level < levels:
                part = jnp.where(in_slot(shape, slot), terms[level], part)
        moved.append(pltpu.roll(part, k * EDGE, 1) if k else part)
    while len(moved) > 1:
        moved = [x + y for x, y in zip(moved[::2], moved[1::2])]
    return moved[0]


def apart_levels(packed, levels):
    slots = LANES // EDGE
    turned = [packed] + [pltpu.roll(packed, EDGE * k, 1) for k in range(1, slots)]
    lane = lane_of(packed.shape)
    out = []
    for v in range(levels):
        parts, width = [turned[(slot - v) % slots] for slot in range(slots)], EDGE
        while len(parts) > 1:
            left = lane // width % 2 == 0
            parts = [jnp.where(left, x, y) for x, y in zip(parts[::2], parts[1::2])]
            width *= 2
        out.append(parts[0])
    return out


def halo_members(block, rows, groups, levels):
    start = rows + rows // 2
    return block[start : start + levels * rows].reshape(levels, groups, rows // groups, LANES)


def halo_weight(block, rows, levels):
    return block[rows + rows // 2 + levels * rows :]


def farther_columns(block, rows, side):
    packed = block[rows : rows + rows // 2]
    lane = lane_of(packed.shape)
    if side == 0:
        halves_of = (pltpu.roll(packed, REACH, 1), packed)
        mask = lane % EDGE >= REACH
    else:
        halves_of = (packed, pltpu.roll(packed, LANES - REACH, 1))
        mask = lane % EDGE < REACH
    return jnp.concatenate([jnp.where(mask, x, 0.0) for x in halves_of], axis=0)


def edge_kernel(norm, chip, core, near, edge_members, edge, thin, out):
    levels, groups, height = edge_members.shape[1:4]
    rows = groups * height
    sides = sides_of(core[...], chip[...])
    parts = []
    for side, block in enumerate(sides):
        here = [farther_columns(block, rows, side), block[:rows], near[side].reshape(rows, LANES)]
        parts += here if side == 0 else here[::-1]
    filtered = thin3(thin, jnp.concatenate(parts, axis=1))
    filtered = split(jnp.concatenate([filtered[:, : 3 * LANES], filtered[:, 3 * LANES :]], axis=0))
    beyond = dot3(filtered, [jnp.concatenate([edge[i, k] for i in range(3)], axis=0) for k in range(2)])
    middle = tuple(x[:, LANES : 2 * LANES] for x in filtered)
    for side, block in enumerate(sides):
        own = slice(side * rows, (side + 1) * rows)
        within = dot3(tuple(x[own] for x in middle), both(edge.at[2 * side]))
        lanes = pl.ds(side * LANES, LANES)
        out[:height, lanes] = beside_levels(edge_terms(edge_members[side], within))
        out[height:, lanes] = beside_levels(edge_terms(halo_members(block, rows, groups, levels), beyond[own]))
    lane = lane_of(norm.shape)
    top = pl.ds(0, norm.shape[0])
    out[top, :LANES] = jnp.where(lane >= LANES - SPARE, norm[...], out[top, :LANES])


def weight_of(precision, covered):
    levels, height, width = precision.shape
    rows, blocks = covered.shape
    spread = lax.broadcasted_iota(jnp.int32, (blocks, width), 1) // (width // blocks)
    spread = (spread == lax.broadcasted_iota(jnp.int32, (blocks, width), 0)).astype(BF16)
    mask = jnp.dot(covered[...].astype(F32).astype(BF16), spread, preferred_element_type=F32)
    tall = height // rows
    mask = jnp.concatenate([jnp.broadcast_to(mask[i : i + 1], (tall, width)) for i in range(rows)], axis=0)
    return precision[...] * mask


def packed_adjoint(members, weighted):
    total = jnp.zeros(members.shape[1:], F32)
    for v, level in enumerate(apart_levels(weighted, members.shape[0])):
        total = total + members[v] * level
    return total


def prepare_kernel(
    after, members_ref, column_hbm, row_hbm, edge_hbm, thin_hbm, next_members, column, row, edge, thin, sems
):
    pairs = ((column_hbm, column), (row_hbm, row), (edge_hbm, edge), (thin_hbm, thin))
    copies = [pltpu.make_async_copy(x, y, sems.at[i]) for i, (x, y) in enumerate(pairs)]
    for copy in copies:
        copy.start()
    levels, width = members_ref.shape[1], members_ref.shape[-1]
    for v in range(levels):
        level = members_ref[:, v].astype(F32)
        next_members[0, v] = pack_columns(level, EDGE, EDGE)
        next_members[1, v] = pack_columns(level, width - 2 * EDGE, EDGE)
    for copy in copies:
        copy.wait()


def main_kernel(i0, i1, i2, i3, obs_weight, members_ref, column, row, first, back, second):
    first[...] = (i0[...] + i1[...]) + (i2[...] + i3[...])
    back[...] = adjoint(members_ref, obs_weight[...] * first[...].reshape(obs_weight.shape))
    second[...] = increments(members_ref, own_columns(back, column, row)).reshape(second.shape)


def correction_kernel(
    e0, e1, e2, e3, main, near_weight, chip, core, edge_members, next_members, edge, thin, outer, own, halo, out
):
    levels, groups, height = edge_members.shape[1:4]
    width = out.shape[-1]
    rows = groups * height
    outer[...] = (e0[...] + e1[...]) + (e2[...] + e3[...])
    out[...] = main[...]
    for side, block in enumerate(sides_of(core[...], chip[...])):
        lanes = pl.ds(side * LANES, LANES)
        own[side] = packed_adjoint(edge_members[side], outer[:height, lanes] * near_weight[side])
        halo[side] = packed_adjoint(
            halo_members(block, rows, groups, levels), outer[height:, lanes] * halo_weight(block, rows, levels)
        )
    parts = [x[side].reshape(rows, LANES) for side in range(2) for x in (halo, own)]
    filtered = split(thin3(thin, jnp.concatenate(parts, axis=1)))
    for side in range(2):
        span = slice(2 * side * LANES, 2 * (side + 1) * LANES)
        matrix = [jnp.concatenate([edge[2 * side, k], edge[1, k]], axis=0) for k in range(2)]
        outermost = dot3(tuple(x[:, span] for x in filtered), matrix)
        inner = dot3(tuple(x[:, span.start + LANES : span.stop] for x in filtered), both(edge.at[2 * side]))
        blocks = [edge_terms(edge_members[side], outermost), edge_terms(next_members[side], inner)]
        if side == 0:
            add_columns(out, 0, blocks)
        else:
            add_columns(out, width - 2 * EDGE, blocks[::-1])


def wide_filter_kernel(
    main, own, halo, first, outer, obs_weight, column_hbm, row_hbm, weighted, sums, out, column, row, sems
):
    copies = [pltpu.make_async_copy(x, y, sems.at[i]) for i, (x, y) in enumerate(((column_hbm, column), (row_hbm, row)))]
    for copy in copies:
        copy.start()
    levels, height, width = obs_weight.shape
    weighted[...] = first[...].reshape(obs_weight.shape)
    for side, start in enumerate((0, width - EDGE)):
        origin = start // LANES * LANES
        lane = lane_of((height, LANES))
        mask = (lane >= start - origin) & (lane < start - origin + EDGE)
        for v, level in enumerate(apart_levels(outer[:height, pl.ds(side * LANES, LANES)], levels)):
            span = pl.ds(origin, LANES)
            weighted[v, :, span] = weighted[v, :, span] + jnp.where(mask, level, 0.0)
    increment = weighted[...]
    weighted[...] = obs_weight[...] * increment
    top = outer[: sums.shape[1], :LANES]
    sums[0] = jnp.where(lane_of(top.shape) >= LANES - SPARE, top, 0.0)
    sums[1] = folded(weighted[...] * increment)
    groups = own.shape[1]
    fields = []
    for k in range(main.shape[0]):
        field = main[k]
        slot, group = k // groups, k % groups
        ends = []
        for side, at in enumerate((0, LANES - EDGE)):
            moved = pltpu.roll(own[side, group], (at - slot * EDGE) % LANES, 1)
            lane = lane_of(moved.shape)
            ends.append(jnp.where((lane >= at) & (lane < at + EDGE), moved, 0.0))
        middle = [jnp.zeros((height, width - 2 * LANES), F32)] if width > 2 * LANES else []
        fields.append(field + jnp.concatenate([ends[0]] + middle + [ends[1]], axis=1))
    for copy in copies:
        copy.wait()
    lhs = split(beside(jnp.stack(fields), halo[0], halo[1], EDGE))
    out[...] = dot3(both(row), split(dot3(lhs, both(column)))).reshape(out.shape)


def filter_kernel(back, core, chip, column, row, out):
    groups, height = back.shape[0] * EDGE // LANES, back.shape[1]
    left, right = sides_of(*(x[: groups * height].reshape(groups, height, LANES) for x in (core, chip)))
    lhs = split(beside(back[...], left, right, EDGE))
    out[...] = dot3(both(row), split(dot3(lhs, both(column)))).reshape(out.shape)


def norms_kernel(i0, i1, i2, i3, obs_weight, before, sums, weighted, norms):
    increment = ((i0[...] + i1[...]) + (i2[...] + i3[...])).reshape(obs_weight.shape)
    weighted[...] = obs_weight[...] * increment
    four = [sums[0], sums[1], folded(before[...] * increment), folded(weighted[...] * increment)]
    row = lax.broadcasted_iota(jnp.int32, (8, LANES), 0)
    stacked = jnp.zeros((8, LANES), F32)
    for i, part in enumerate(four):
        stacked = jnp.where(row == i, jnp.sum(part, axis=0, keepdims=True), stacked)
    norms[...] = stacked


def last_kernel(weighted, members_ref, back, to_core, to_chip):
    height = back.shape[1]
    back[...] = adjoint(members_ref, weighted)
    odd = lax.axis_index("tile") % 2 == 1
    first, last = pack_edges(back, EDGE, True), pack_edges(back, EDGE, False)
    rows = first.shape[0] * height
    to_core[...] = jnp.where(odd, first, last).reshape(rows, LANES)
    to_chip[...] = jnp.where(odd, last, first).reshape(rows, LANES)


def copy_kernel(value, after, out):
    out[...] = value[...]


def pass_kernel(value, after, out):
    pass


def combine_kernel(own, other, source, first, second, weights, residual, held_weights, held_residual, sems):
    total = jnp.sum(own[...] + other[...], axis=1, keepdims=True)
    bb, bg, gg, gh = (total[i : i + 1] for i in range(4))
    bg, gg, gh = bg / bb, gg / bb, gh / bb
    q = 1.0 / (1.0 + bg)
    p = bg * q
    ratio = (gg - bg * bg) * q * q
    d = p + ratio
    square = d * d - 2.0 * d * q * bg + q * q * gg
    image = d * d * bg - 2.0 * d * q * gg + q * q * gh
    step = ratio / (square + image)
    members = source.shape[0]
    pieces = sems.shape[1]
    copies = []
    for i in range(pieces):
        part = pl.ds(i * (members // pieces), members // pieces)
        b, g, h = source[part], first[part], second[part]
        held_weights[part] = (q + step * d) * b - (step * q) * g
        held_residual[part] = (p - step * d) * b + (step * q - q - step * d) * g + (step * q) * h
        for k, (held, out) in enumerate(((held_weights, weights), (held_residual, residual))):
            copies.append(pltpu.make_async_copy(held.at[part], out.at[part], sems.at[k, i]))
            copies[-1].start()
    for copy in copies:
        copy.wait()


def call(kernel, outs, *operands, cost=None):
    shapes = [jax.ShapeDtypeStruct(shape, F32) for shape in outs]
    vmem = pl.BlockSpec(memory_space=pltpu.VMEM)
    return pl.pallas_call(
        kernel,
        out_shape=shapes,
        in_specs=[vmem] * len(operands),
        out_specs=[vmem] * len(outs),
        compiler_params=pltpu.CompilerParams(vmem_limit_bytes=24 * 1024 * 1024),
        cost_estimate=cost,
    )(*operands)


def passed(value, after):
    vmem = pl.BlockSpec(memory_space=pltpu.VMEM)
    return pl.pallas_call(
        pass_kernel,
        out_shape=pltpu.VMEM(value.shape, value.dtype),
        in_specs=[vmem] * 2,
        out_specs=vmem,
        input_output_aliases={0: 0},
        compiler_params=pltpu.CompilerParams(vmem_limit_bytes=24 * 1024 * 1024),
        cost_estimate=LONG,
    )(value, after)


def in_hbm(array):
    return pltpu.with_memory_space_constraint(array, pltpu.HBM)


def held_edges(source, members_data, precision, covered):
    members, levels, height, width = members_data.shape
    groups = members * EDGE // LANES
    rows = groups * height
    payload = (rows + rows // 2 + rows * levels + height, LANES)
    vmem = pl.BlockSpec(memory_space=pltpu.VMEM)
    hbm = pl.BlockSpec(memory_space=pltpu.HBM)
    arrays = (source, members_data, precision, covered)
    return pl.pallas_call(
        edges_kernel,
        out_shape=[
            pltpu.VMEM(source.shape, F32),
            pltpu.VMEM(members_data.shape, members_data.dtype),
            pltpu.VMEM(precision.shape, F32),
            pltpu.VMEM((2, groups, height, LANES), F32),
            pltpu.VMEM((2, height, LANES), F32),
            pltpu.VMEM((2, levels, groups, height, LANES), F32),
            pltpu.VMEM(payload, F32),
            pltpu.VMEM(payload, F32),
            pltpu.VMEM((2, width, width), BF16),
            pltpu.VMEM((2, members * height, members * height), BF16),
            pltpu.VMEM((3, 2, LANES, LANES), BF16),
            pltpu.VMEM((2, groups * height, groups * height), BF16),
        ],
        in_specs=[hbm] * 4,
        out_specs=[vmem] * 12,
        scratch_shapes=[
            pltpu.VMEM(precision.shape, F32),
            pltpu.VMEM(covered.shape, covered.dtype),
            pltpu.SemaphoreType.DMA((4,)),
        ],
        compiler_params=pltpu.CompilerParams(vmem_limit_bytes=24 * 1024 * 1024),
    )(*map(in_hbm, arrays))


def first_increment(source, after, members_data, column, row):
    _, levels, height, width = members_data.shape
    vmem = pl.BlockSpec(memory_space=pltpu.VMEM)
    return pl.pallas_call(
        first_kernel,
        out_shape=[pltpu.VMEM((levels * height, width), F32), pltpu.VMEM((8, LANES), F32)],
        in_specs=[vmem] * 5,
        out_specs=[vmem] * 2,
        compiler_params=pltpu.CompilerParams(vmem_limit_bytes=24 * 1024 * 1024),
        cost_estimate=LONG,
    )(source, after, members_data, column, row)


def call_with_constants(kernel, outs, kept, scratch, operands, constants):
    vmem = pl.BlockSpec(memory_space=pltpu.VMEM)
    hbm = pl.BlockSpec(memory_space=pltpu.HBM)
    held = [pltpu.VMEM(x.shape, x.dtype) for x in kept]
    return pl.pallas_call(
        kernel,
        out_shape=[pltpu.VMEM(shape, F32) for shape in outs] + held,
        in_specs=[vmem] * len(operands) + [hbm] * len(constants),
        out_specs=[vmem] * (len(outs) + len(kept)),
        scratch_shapes=[pltpu.VMEM(x.shape, x.dtype) for x in scratch] + [pltpu.SemaphoreType.DMA((len(constants),))],
        compiler_params=pltpu.CompilerParams(vmem_limit_bytes=24 * 1024 * 1024),
        cost_estimate=LONG,
    )(*operands, *map(in_hbm, constants))


def combined(own, other, source, first, second):
    vmem = pl.BlockSpec(memory_space=pltpu.VMEM)
    hbm = pl.BlockSpec(memory_space=pltpu.HBM)
    return pl.pallas_call(
        combine_kernel,
        out_shape=[jax.ShapeDtypeStruct(source.shape, F32)] * 2,
        in_specs=[vmem] * 5,
        out_specs=[hbm] * 2,
        scratch_shapes=[pltpu.VMEM(source.shape, F32)] * 2 + [pltpu.SemaphoreType.DMA((2, 4))],
        compiler_params=pltpu.CompilerParams(vmem_limit_bytes=24 * 1024 * 1024),
    )(own, other, source, first, second)


def from_both_sides(to_next, to_previous, axis):
    count = lax.axis_size(axis)
    left = lax.ppermute(to_next, axis, [(i, (i + 1) % count) for i in range(count)])
    right = lax.ppermute(to_previous, axis, [((i + 1) % count, i) for i in range(count)])
    return left, right


def from_tile(value, bit):
    count = lax.axis_size("tile")
    return lax.ppermute(value, "tile", [(i, i ^ bit) for i in range(count)])


def from_core(value):
    return from_tile(value, 1)


def from_chip(value):
    count = lax.axis_size("tile")
    return lax.ppermute(value, "tile", [(i, (i + 1) % count if i % 2 else (i - 1) % count) for i in range(count)])


def from_all(value, axis, order):
    count = lax.axis_size(axis)
    return [value] + [lax.ppermute(value, axis, [(i, i ^ k) for i in range(count)]) for k in order]


def one_tile_row(right_side, perturbations, precision, covered):
    source, members_data = right_side[0], perturbations[0]
    members, levels, height, width = members_data.shape
    groups = members * EDGE // LANES
    taps = taps_np()
    twice = np.convolve(taps, taps)
    field = (members, height, width)
    plane = (levels, height, width)
    flat = (levels * height, width)
    own = np.arange(width)

    held = held_edges(source, members_data, precision[0], covered[0])
    source, members_data, obs_weight, near, near_weight, edge_members, to_core, to_chip, column, row, edge, thin = held
    core, chip = from_core(to_core), from_chip(to_chip)
    inside, norm = first_increment(source, to_chip, members_data, column, row)
    inside = from_all(inside, "mem", (1, 2, 3))
    (outer,) = call(edge_kernel, [(2 * height, 2 * LANES)], norm, chip, core, near, edge_members, edge, thin)
    column_twice, row_twice = halves(band(twice, own, own)), halves(row_matrix(taps, height, members, 2))
    edge, thin = edge_matrix(twice, EDGE), halves(row_matrix(taps, height, groups, 2))
    constants = [column_twice, row_twice, edge, thin]
    next_members, column, row, edge, thin = call_with_constants(
        prepare_kernel, [edge_members.shape], constants, [], [outer, members_data], constants
    )
    increment, main, inside = call(
        main_kernel, [flat, field, flat], *inside, obs_weight, members_data, column, row
    )
    ends = (2, groups, height, LANES)
    outer, corrected, halo, second = call(
        correction_kernel, [outer.shape, ends, ends, flat],
        *from_all(outer, "mem", (3, 2, 1)), inside, near_weight, chip, core, edge_members, next_members, edge, thin,
    )
    parts = from_all(second, "mem", (2, 1, 3))
    column, row = halves(column_matrix(taps, width, EDGE)), halves(row_matrix(taps, height, members, 1))
    weighted, sums, first, column, row = call_with_constants(
        wide_filter_kernel, [plane, (2, 8, LANES), field], [column, row], [],
        [main, corrected, halo, increment, outer, obs_weight], [column, row],
    )
    weighted, sums = call(norms_kernel, [plane, (8, LANES)], *parts, obs_weight, weighted, sums)
    ends = (groups * height, LANES)
    back, to_core, to_chip = call(last_kernel, [field, ends, ends], weighted, members_data)
    sums = sums + from_core(sums)
    core = from_core(to_core)
    (to_chip,) = call(copy_kernel, [to_chip.shape], to_chip, sums)
    chip = from_chip(to_chip)
    first = passed(first, sums)
    sums = sums + from_tile(sums, 5)
    others = from_tile(sums, 3)
    (second,) = call(filter_kernel, [field], back, core, chip, column, row, cost=LONG)
    weights, residual = combined(sums, others, source, first, second)
    return weights[None], residual[None]


def passed_along(value, axis, steps):
    count = lax.axis_size(axis)
    first, last = (max(0, -steps), min(count, count - steps))
    return lax.ppermute(value, axis, [(source, source + steps) for source in range(first, last)])


def smooth(field):
    taps = taps_np().astype(np.float32)
    height, width = field.shape[1:]
    above = passed_along(field[:, height - REACH :, :], "tile", TCOLS)
    below = passed_along(field[:, :REACH, :], "tile", -TCOLS)
    padded = jnp.concatenate([above, field, below], axis=1)
    along = sum(taps[j] * padded[:, j : j + height, :] for j in range(2 * REACH + 1))
    left, right = from_both_sides(along[:, :, width - REACH :], along[:, :, :REACH], "tile")
    sided = jnp.concatenate([left, along, right], axis=2)
    return sum(taps[j] * sided[:, :, j : j + width] for j in range(2 * REACH + 1))


def several_tile_rows(right_side, perturbations, precision, covered):
    source = right_side[0]
    members_data = perturbations[0].astype(F32)
    levels, height, width = precision.shape[1:]
    rows, blocks = covered.shape[1:]
    mask = covered[0].astype(F32)
    obs_weight = (
        precision[0].reshape(levels, rows, height // rows, blocks, width // blocks) * mask[None, :, None, :, None]
    ).reshape(levels, height, width)

    def operator(direction):
        partial_terms = jnp.einsum("kvyx,kyx->vyx", members_data, smooth(direction))
        weighted = obs_weight * lax.psum(partial_terms, "mem")
        return direction + smooth(jnp.einsum("kvyx,vyx->kyx", members_data, weighted))

    weights = jnp.zeros_like(source)
    residual = direction = source
    norm_now = lax.psum(jnp.sum(source * source), ("tile", "mem"))
    for step in range(ITERS):
        image = operator(direction)
        length = norm_now / lax.psum(jnp.sum(direction * image), ("tile", "mem"))
        weights = weights + length * direction
        residual = residual - length * image
        if step + 1 < ITERS:
            norm_next = lax.psum(jnp.sum(residual * residual), ("tile", "mem"))
            direction = residual + norm_next / norm_now * direction
            norm_now = norm_next
    return weights[None], residual[None]


def solution(mesh):
    single = mesh.shape["tile"] == TCOLS and mesh.shape["mem"] == 4
    local = one_tile_row if single else several_tile_rows
    return jax.shard_map(
        local,
        mesh=mesh,
        in_specs=(
            P("tile", "mem", None, None),
            P("tile", "mem", None, None, None),
            P("tile", None, None, None),
            P("tile", None, None),
        ),
        out_specs=(P("tile", "mem", None, None), P("tile", "mem", None, None)),
        check_vma=False,
    )
```
